128 devices in a mesh: frame: 32 (over y, x, core), tensor: 4 (over z).
Axes of the slice: x: 4, y: 4, z: 4, core: 2. Of those that a mesh axis runs over, the one named last changes fastest.
Arguments:
- llm_input: bfloat16 [256, 8192], P('frame'), may hold values from -50 to 50
- out_grad: bfloat16 [256, 8192], P('frame'), may hold values from -6 to 6
- llm_gain: float32 [8192], replicated, may hold values from 0.3 to 2.1
- w_gate: bfloat16 [8192, 29568], P(None, ('frame', 'tensor')), may hold values from -0.0625 to 0.0625
- w_up: bfloat16 [8192, 29568], P(None, ('frame', 'tensor')), may hold values from -0.0625 to 0.0625
- w_down: bfloat16 [29568, 8192], P(('frame', 'tensor')), may hold values from -0.03125 to 0.03125
- keep_index: int32 [32, 12], P('frame'), may hold values from 0 to 195, as said below
- keep_count: int32 [32], P('frame'), may hold values from 1 to 12, 192 in all
- seq_order: int32 [256], replicated, may hold values from 0 to 255, each once
- vision_in: bfloat16 [23328, 1152], P('frame'), may hold values from -50 to 50
- vision_out: bfloat16 [23328, 1152], P('frame'), may hold values from -6 to 6
- vis_gain: float32 [1152], replicated, may hold values from 0.3 to 2.1
- w_proj: bfloat16 [1152, 8192], P(None, 'tensor'), may hold values from -0.1875 to 0.1875
- w_fc1: bfloat16 [1152, 4304], P(None, 'tensor'), may hold values from -0.1875 to 0.1875
- w_fc2: bfloat16 [4304, 1152], P('tensor'), may hold values from -0.09375 to 0.09375
Outputs:
- embed_grad: bfloat16 [256, 8192], P('frame', 'tensor')
- proj_grad: float32 [1152, 8192], P('frame', 'tensor')
- fc1_grad: float32 [1152, 4304], P('frame', 'tensor')
- fc2_grad: float32 [4304, 1152], P('tensor', 'frame')
- feature_grad: bfloat16 [23328, 1152], P('frame', 'tensor')
The draws below stay inside these ranges and needn't reach their ends.
Inputs may be any that keep to these rules, and one draw needn't show every extreme that they name: `keep_index`: in each frame the 12 entries are distinct pooled token indices; only the first keep_count of them are kept. `keep_count`: the counts of all frames sum to 192; some frame keeps exactly 12. `seq_order`: each position once; positions not named by a kept token hold text.
All inputs are finite; a program needn't handle non-finite values. No bound on the sum of `keep_count` on one device may be relied on, other than what follows from the above.
Results may differ from the reference program's by a relative error of at most 0.01.
Values may be sent and summed in bfloat16 or wider, within the bound.
A program may use at most 128 MiB of HBM per device.

```python
import math
import jax
import jax.numpy as jnp
import numpy as np
from jax import lax

D = 8192
FF = 29568
V_W = 1152
V_FF = 4304
P_H = 8192
GRID = 27
KMAX = 12
POOLED = 196
TOKF = 729
TOUCH = 48
FRAMES = 32
SEQ = 256
KEPT = 192


def scaled_field(key, noise, rows, cols):
    key_row, key_col = jax.random.split(key, 2)
    row_scale = jnp.exp(jax.random.uniform(key_row, (rows, 1), jnp.float32, 0.0, math.log(10.0)))
    col_scale = jnp.exp(jax.random.uniform(key_col, (1, cols), jnp.float32, 0.0, math.log(10.0)))
    return noise * row_scale * col_scale / 10.0


def rising_gain(key, width, lower, upper):
    ramp = 0.5 + jnp.arange(width, dtype=jnp.float32) / (width - 1)
    return ramp * jax.random.uniform(key, (width,), jnp.float32, lower, upper)


def draw_llm_input(key, part):
    key = jax.random.fold_in(key, 11)
    key_noise, key_field = jax.random.split(key)
    noise = jnp.clip(jax.random.normal(key_noise, (SEQ, D), jnp.float32), -4.0, 4.0)
    return scaled_field(key_field, noise, SEQ, D).astype(jnp.bfloat16)


def draw_vision_in(key, part):
    key = jax.random.fold_in(key, 12)
    key_noise, key_field = jax.random.split(key)
    noise = jnp.clip(jax.random.normal(key_noise, (FRAMES * TOKF, V_W), jnp.float32), -4.0, 4.0)
    return scaled_field(key_field, noise, FRAMES * TOKF, V_W).astype(jnp.bfloat16)


def draw_llm_gain(key, part):
    key = jax.random.fold_in(key, 13)
    return rising_gain(key, D, 0.6, 1.4)


def draw_vis_gain(key, part):
    key = jax.random.fold_in(key, 14)
    return rising_gain(key, V_W, 0.6, 1.4)


def draw_keep_index(key, part):
    key = jax.random.fold_in(key, 15)
    scores = jax.random.randint(key, (FRAMES, POOLED), 0, 65536) * POOLED + jnp.arange(POOLED, dtype=jnp.int32)[None, :]
    ordering = jnp.argsort(scores, axis=1, stable=True)
    return ordering[:, :KMAX].astype(jnp.int32)


def block_scale(stream_key, shape, pieces, low, high):
    factor_of, own = 1.0, jax.random.fold_in(stream_key, 6)
    for dim, parts in pieces:
        draws = jnp.exp(jax.random.uniform(jax.random.fold_in(own, dim), (parts,), jnp.float32, low / len(pieces), high / len(pieces)))
        factor_of = factor_of * jnp.repeat(draws, shape[dim] // parts).reshape([-1 if axis == dim else 1 for axis in range(len(shape))])
    return factor_of


def length_profile(amount, total, reach, slope):
    weights = [(1 << 20) // math.isqrt(grade ** slope) + 1 for grade in range(2, amount + 1)]
    rest, counts = total - reach - (amount - 1), [1] * (amount - 1)
    while rest > 0:
        free = [i for i in range(amount - 1) if counts[i] < reach]
        mass, budget = sum([weights[i] for i in free]), rest
        for i in free:
            addition = min(reach - counts[i], max(1, budget * weights[i] // mass), rest)
            counts[i] = counts[i] + addition
            rest = rest - addition
    return np.array([reach] + counts)


def ragged(key, number_of, total, most, slope):
    if number_of == 2:
        one = jax.random.randint(key, (), max(1, total - most), min(most, total - 1) + 1)
        return jnp.stack([one, total - one])
    sizes = jnp.asarray(length_profile(number_of, total, most, slope), jnp.int32)
    twos = (number_of - 1) // 2
    giver, receiver = sizes[1:1 + 2 * twos:2], sizes[2:2 + 2 * twos:2]
    margin = jnp.minimum(giver - 1, most - receiver)
    moved = jax.random.randint(jax.random.fold_in(key, 1), (twos,), 0, 1 << 20) % (margin + 1)
    sizes = sizes.at[1:1 + 2 * twos:2].set(giver - moved).at[2:2 + 2 * twos:2].set(receiver + moved)
    return sizes[jax.random.permutation(jax.random.fold_in(key, 2), number_of)]


def bell_draw(key, dims, scale, most, cuts=(), kind=jnp.bfloat16):
    level = block_scale(key, dims, cuts, -0.22, 0.18) if cuts else 1.0
    result = jax.random.normal(key, dims, jnp.float32) * scale * level
    return jnp.minimum(jnp.maximum(result, -most), most).astype(kind)


def setup_inputs(seed: int = 0) -> dict:
    key_list = jax.random.split(jax.random.key(seed), 16)
    return {
        "llm_input": draw_llm_input(jax.random.fold_in(key_list[15], 71), 0),
        "out_grad": bell_draw(key_list[1], (SEQ, D), 1.0, 6.0, ((0, 32),)),
        "llm_gain": draw_llm_gain(jax.random.fold_in(key_list[15], 71), 0),
        "w_gate": bell_draw(key_list[3], (D, FF), D ** -0.5, 0.0625, ((1, 128),)),
        "w_up": bell_draw(key_list[4], (D, FF), D ** -0.5, 0.0625, ((1, 128),)),
        "w_down": bell_draw(key_list[5], (FF, D), FF ** -0.5, 0.03125, ((0, 128),)),
        "keep_index": draw_keep_index(jax.random.fold_in(key_list[15], 71), 0),
        "keep_count": ragged(key_list[7], FRAMES, KEPT, KMAX, 2).astype(jnp.int32),
        "seq_order": jax.random.permutation(key_list[8], SEQ).astype(jnp.int32),
        "vision_in": draw_vision_in(jax.random.fold_in(key_list[15], 71), 0),
        "vision_out": bell_draw(key_list[10], (FRAMES * TOKF, V_W), 1.0, 6.0, ((0, 32),)),
        "vis_gain": draw_vis_gain(jax.random.fold_in(key_list[15], 71), 0),
        "w_proj": bell_draw(key_list[12], (V_W, P_H), V_W ** -0.5, 0.1875, ((1, 4),)),
        "w_fc1": bell_draw(key_list[13], (V_W, V_FF), V_W ** -0.5, 0.1875, ((1, 4),)),
        "w_fc2": bell_draw(key_list[14], (V_FF, V_W), V_FF ** -0.5, 0.09375, ((0, 4),)),
    }


def contract_rows(left, right):
    return lax.dot_general(left, right, (((0,), (0,)), ((), ())), preferred_element_type=jnp.float32)

def contract_cols(left, right):
    return lax.dot_general(left, right, (((1,), (1,)), ((), ())), preferred_element_type=jnp.float32)

def root_mean(inputs):
    values = inputs.astype(jnp.float32)
    return jnp.sqrt(lax.optimization_barrier(jnp.mean(values * values, axis=1, keepdims=True)) + 1e-06)

def hidden_grads(inputs, grads, llm_gain, w_gate, w_up, w_down):
    scale = root_mean(inputs)
    normed = (inputs.astype(jnp.float32) / scale * llm_gain).astype(jnp.bfloat16)
    gate_value = jnp.dot(normed, w_gate, preferred_element_type=jnp.float32)
    up_value = jnp.dot(normed, w_up, preferred_element_type=jnp.float32)
    hidden_grad = contract_cols(grads, w_down)
    sigmoid_value = jax.nn.sigmoid(gate_value)
    up_grad = (hidden_grad * gate_value * sigmoid_value).astype(jnp.bfloat16)
    gate_grad = (hidden_grad * up_value * sigmoid_value * (1.0 + gate_value * (1.0 - sigmoid_value))).astype(jnp.bfloat16)
    return (gate_grad, up_grad)

def rms_backward(inputs, grads, llm_gain, normed_grad):
    scale = root_mean(inputs)
    unit = inputs.astype(jnp.float32) / scale
    scaled = normed_grad * llm_gain
    inner = lax.optimization_barrier(jnp.mean(scaled * unit, axis=1, keepdims=True))
    return (grads.astype(jnp.float32) + (scaled - unit * inner) / scale).astype(jnp.bfloat16)

def erf_gelu_slope(values):
    return 0.5 * (1.0 + lax.erf(values * 0.7071067811865476)) + values * jnp.exp(-0.5 * values * values) * 0.3989422804014327

def tanh_gelu(values):
    inner = 0.7978845608028654 * (values + 0.044715 * values * values * values)
    return 0.5 * values * (1.0 + jnp.tanh(inner))

def tanh_gelu_slope(values):
    inner = 0.7978845608028654 * (values + 0.044715 * values * values * values)
    tangent = jnp.tanh(inner)
    return 0.5 * (1.0 + tangent) + 0.5 * values * (1.0 - tangent * tangent) * 0.7978845608028654 * (1.0 + 3.0 * 0.044715 * values * values)

def touched_rows(keep_row, live_count, grid):
    width = (grid + 1) // 2
    slots = jnp.arange(keep_row.shape[0], dtype=jnp.int32)
    quarter = jnp.arange(4, dtype=jnp.int32)
    pool_row = keep_row // width
    pool_col = keep_row % width
    grid_row = 2 * pool_row[:, None] + quarter[None, :] // 2
    grid_col = 2 * pool_col[:, None] + quarter[None, :] % 2
    inside = (grid_row < grid) & (grid_col < grid) & (slots < live_count)[:, None]
    row_cells = jnp.where(2 * pool_row + 1 < grid, 2.0, 1.0)
    col_cells = jnp.where(2 * pool_col + 1 < grid, 2.0, 1.0)
    weight = jnp.where(inside, (1.0 / (row_cells * col_cells))[:, None], 0.0).astype(jnp.float32)
    feature = jnp.where(inside, grid_row * grid + grid_col, 0).astype(jnp.int32)
    return (feature, weight)

def reference(llm_input, out_grad, llm_gain, w_gate, w_up, w_down, keep_index, keep_count, seq_order, vision_in, vision_out, vis_gain, w_proj, w_fc1, w_fc2):
    gate_grad, up_grad = hidden_grads(llm_input, out_grad, llm_gain, w_gate, w_up, w_down)
    normed_grad = contract_cols(gate_grad, w_gate) + contract_cols(up_grad, w_up)
    embed_grad = rms_backward(llm_input, out_grad, llm_gain, normed_grad)
    offset = (jnp.cumsum(keep_count) - keep_count).astype(jnp.int32)
    slots = jnp.arange(KMAX, dtype=jnp.int32)
    position = jnp.minimum(offset[:, None] + slots[None, :], SEQ - 1).astype(jnp.int32)
    destination = jnp.take(seq_order, position.reshape(-1)).astype(jnp.int32)
    alive_slots = (slots[None, :] < keep_count[:, None]).reshape(-1)
    kept = jnp.where(alive_slots[:, None], jnp.take(embed_grad, destination, axis=0), jnp.zeros((), jnp.bfloat16))
    kept = kept.reshape(FRAMES, KMAX, D)
    feature, weight = jax.vmap(touched_rows, in_axes=(0, 0, None))(keep_index, keep_count, GRID)
    frame_base = (jnp.arange(FRAMES, dtype=jnp.int32) * TOKF)[:, None, None]
    global_rows = (feature + frame_base).reshape(-1).astype(jnp.int32)
    feature_up = (kept.astype(jnp.float32)[:, :, None, :] * weight[:, :, :, None]).reshape(FRAMES * TOUCH, P_H)
    rows_out = jnp.take(vision_out, global_rows, axis=0)
    pre_act = jnp.dot(rows_out, w_proj, preferred_element_type=jnp.float32)
    act_grad = (feature_up * erf_gelu_slope(pre_act)).astype(jnp.bfloat16)
    proj_grad = contract_rows(rows_out, act_grad)
    vis_grad = contract_cols(act_grad, w_proj)
    vis_grad_b = vis_grad.astype(jnp.bfloat16)
    rows_in = jnp.take(vision_in, global_rows, axis=0).astype(jnp.float32)
    center = lax.optimization_barrier(jnp.mean(rows_in, axis=1, keepdims=True))
    variance = lax.optimization_barrier(jnp.mean((rows_in - center) * (rows_in - center), axis=1, keepdims=True))
    deviation = jnp.sqrt(variance + 1e-06)
    unit_in = (rows_in - center) / deviation
    ln_out = (unit_in * vis_gain).astype(jnp.bfloat16)
    fc_pre = jnp.dot(ln_out, w_fc1, preferred_element_type=jnp.float32)
    fc_act = tanh_gelu(fc_pre).astype(jnp.bfloat16)
    fc_act_grad = contract_cols(vis_grad_b, w_fc2)
    fc_pre_grad = (fc_act_grad * tanh_gelu_slope(fc_pre)).astype(jnp.bfloat16)
    fc2_grad = contract_rows(fc_act, vis_grad_b)
    fc1_grad = contract_rows(ln_out, fc_pre_grad)
    ln_grad = contract_cols(fc_pre_grad, w_fc1)
    scaled = ln_grad * vis_gain
    back = vis_grad + (scaled - lax.optimization_barrier(jnp.mean(scaled, axis=1, keepdims=True)) - unit_in * lax.optimization_barrier(jnp.mean(scaled * unit_in, axis=1, keepdims=True))) / deviation
    feature_grad = jax.ops.segment_sum(back, global_rows, num_segments=FRAMES * TOKF).astype(jnp.bfloat16)
    return (embed_grad, proj_grad, fc1_grad, fc2_grad, feature_grad)
```

```python
import functools

import jax
import jax.numpy as jnp
from jax import lax
from jax.experimental import pallas as pl
from jax.experimental.pallas import tpu as pltpu
from jax.sharding import PartitionSpec as P

GRID = 27
BF = jnp.bfloat16
F32 = jnp.float32
MESH = pl.DeviceIdType.MESH
ANY = pl.BlockSpec(memory_space=pl.ANY)
VM = pl.BlockSpec(memory_space=pltpu.VMEM)


def nt(left, right):
    return lax.dot_general(left, right, (((1,), (1,)), ((), ())), preferred_element_type=F32)


def tn(left, right):
    return lax.dot_general(left, right, (((0,), (0,)), ((), ())), preferred_element_type=F32)


def nn(left, right):
    return jnp.dot(left, right, preferred_element_type=F32)


class Place:
    def __init__(self):
        frame = lax.axis_index("frame")
        self.frame = frame
        self.t = lax.axis_index("tensor")
        self.c = lax.rem(frame, 2)
        self.k = frame // 2
        self.x = lax.rem(self.k, 4)
        self.y = self.k // 4

    def at(self, y=None, x=None, z=None, core=None):
        y = self.y if y is None else y
        x = self.x if x is None else x
        z = self.t if z is None else z
        core = self.c if core is None else core
        return ((y * 4 + x) * 2 + core, z)

    def other(self):
        return self.at(core=1 - self.c)


def greet(targets):
    barrier = pltpu.get_barrier_semaphore()
    for target in targets:
        pl.semaphore_signal(barrier, inc=1, device_id=target, device_id_type=MESH)
    pl.semaphore_wait(barrier, len(targets))


def wrap(pos, d):
    return lax.rem(pos + d, 4)


class Copies:
    def __init__(self, send, recv):
        self.send, self.recv, self.used, self.open = send, recv, 0, []

    def start(self, src, dst, target):
        i = self.used
        self.used += 1
        copy = pltpu.make_async_remote_copy(
            src_ref=src,
            dst_ref=dst,
            send_sem=self.send.at[i],
            recv_sem=self.recv.at[i],
            device_id=target,
            device_id_type=MESH,
        )
        copy.start()
        self.open.append(copy)
        return copy

    def finish(self):
        for copy in self.open:
            copy.wait_send()


def ring_begin(copies, pos, view, dev):
    right = copies.start(view(pos, None), view(pos, None), dev(wrap(pos, 1)))
    left = copies.start(view(pos, None), view(pos, None), dev(wrap(pos, 3)))
    return (right, left)


def ring_middle(copies, pos, view, dev, begun):
    right, left = begun
    right.wait_recv()
    on_right = copies.start(view(wrap(pos, 3), 0), view(wrap(pos, 3), 0), dev(wrap(pos, 1)))
    left.wait_recv()
    on_left = copies.start(view(wrap(pos, 1), 1), view(wrap(pos, 1), 1), dev(wrap(pos, 3)))
    return (on_right, on_left)


def ring_end(middle):
    for copy in middle:
        copy.wait_recv()


def direct_begin(copies, pos, view, dev):
    return [copies.start(view(pos), view(pos), dev(wrap(pos, d))) for d in (1, 3, 2)]


def pick(start, width, half):
    if half is None:
        return pl.ds(start, width)
    return pl.ds(start + half * (width // 2), width // 2)


def llm_kernel(
    x_ref, g_ref, gain_ref, wg_hbm, wu_hbm, wd_hbm,
    embed_ref, eall_ref,
    xg, buf, wg, wu, wd, acc_g, acc_u, acc_h, gg, ug, sb, rb, q,
    ra1, ra2, ra3, sa1, sa2,
    wsem, send, recv,
):
    me = Place()
    c, t, x, y = me.c, me.t, me.x, me.y
    loads = [
        pltpu.make_async_copy(wg_hbm, wg, wsem.at[0]),
        pltpu.make_async_copy(wu_hbm, wu, wsem.at[1]),
        pltpu.make_async_copy(wd_hbm, wd, wsem.at[2]),
    ]
    for load in loads:
        load.start()
    xg[c, 0] = x_ref[...].astype(F32)
    xg[c, 1] = g_ref[...].astype(F32)
    targets = [me.other()]
    targets += [me.at(z=wrap(t, d)) for d in (1, 2, 3)]
    targets += [
        me.at(y=wrap(y, dy), x=wrap(x, dx)) for dy in range(4) for dx in range(4) if dy or dx
    ]
    greet(targets)
    copies = Copies(send, recv)
    swap = copies.start(xg.at[c], xg.at[c], me.other())
    swap.wait_recv()

    rows = xg[:, 0]
    total = jnp.sum(rows * rows, axis=2, keepdims=True)
    root = jnp.sqrt(total / 8192.0 + 1e-06)

    def make_block(i, _):
        cols = pl.ds(pl.multiple_of(i * 1024, 1024), 1024)
        normed = xg[:, 0, :, cols] / root * gain_ref[:, cols][None]
        block = jnp.where(c == 0, normed, xg[:, 1, :, cols])
        buf[c, y, x, :, cols] = block.reshape(16, 1024).astype(BF)
        return 0

    lax.fori_loop(0, 8, make_block, 0)

    def view0x(pos, half):
        return buf.at[c, y, pos, :, pick(0, 4096, half)]

    def view1y(pos, half):
        return buf.at[c, pos, x, :, pick(4096, 4096, half)]

    def view0y(pos, half):
        return buf.at[c, pos, :, :, pick(0, 4096, half)]

    def view1x(pos, half):
        return buf.at[c, :, pos, :, pick(4096, 4096, half)]

    def dev_x(pos):
        return me.at(x=pos)

    def dev_y(pos):
        return me.at(y=pos)

    crossed = []

    def cross(view):
        crossed.append(copies.start(view, view, me.other()))

    for step in (0, 1):
        rings = (
            [(x, view0x, dev_x), (y, view1y, dev_y)]
            if step == 0
            else [(y, view0y, dev_y), (x, view1x, dev_x)]
        )
        begun = [ring_begin(copies, *ring) for ring in rings]
        if step == 1:
            for pos, view, _ in rings:
                cross(view(pos, None))
        middle = [ring_middle(copies, *ring, b) for ring, b in zip(rings, begun)]
        if step == 1:
            for pos, view, _ in rings:
                cross(view(wrap(pos, 1), None))
                cross(view(wrap(pos, 3), None))
        for m in middle:
            ring_end(m)
        if step == 1:
            for pos, view, _ in rings:
                cross(view(wrap(pos, 2), None))
    for load in loads:
        load.wait()
    for copy in crossed:
        copy.wait_recv()

    acc_g[...] = jnp.zeros_like(acc_g)
    acc_u[...] = jnp.zeros_like(acc_u)
    acc_h[...] = jnp.zeros_like(acc_h)

    def first(i, _):
        cols = pl.ds(pl.multiple_of(i * 1024, 1024), 1024)
        normed = buf[0, :, :, :, cols].reshape(256, 1024)
        acc_g[...] += nn(normed, wg[cols, :])
        acc_u[...] += nn(normed, wu[cols, :])
        grads = buf[1, :, :, :, cols].reshape(256, 1024)
        acc_h[...] += nt(grads, wd[:, cols])
        return 0

    lax.fori_loop(0, 8, first, 0)
    gate, up, hidden = acc_g[...], acc_u[...], acc_h[...]
    sig = jax.nn.sigmoid(gate)
    up_grad = (hidden * gate * sig).astype(BF)
    gate_grad = (hidden * up * sig * (1.0 + gate * (1.0 - sig))).astype(BF)
    gg[...] = gate_grad
    ug[...] = up_grad
    inner = jnp.sum(
        gate_grad.astype(F32) * gate + up_grad.astype(F32) * up, axis=1, keepdims=True
    )
    inner = jnp.broadcast_to(inner, (256, 128)).reshape(4, 4, 16, 128)

    def part(base, i):
        cols = pl.ds(pl.multiple_of(base + i * 256, 256), 256)
        value = nt(gg[...], wg[cols, :]) + nt(ug[...], wu[cols, :])
        return value.reshape(4, 4, 16, 256)

    halves = []
    for step in range(4):
        to = wrap(t, step + 1)

        def give(i, _):
            cols = pl.ds(pl.multiple_of(i * 256, 256), 256)
            sb[to, :, :, :, cols] = part(to * 2048 + (1 - c) * 1024, i).astype(BF)
            return 0

        lax.fori_loop(0, 4, give, 0)
        sb[to, :, :, :, 1024:1152] = inner.astype(BF)
        halves.append(copies.start(sb.at[to], rb.at[to], me.other()))

    cuts = (pl.ds(0, 384), pl.ds(384, 384), pl.ds(768, 384))
    stage1 = []
    for step in range(4):
        to = wrap(t, step + 1)
        halves[step].wait_recv()

        def keep(i, _):
            cols = pl.ds(pl.multiple_of(i * 256, 256), 256)
            mine = part(to * 2048 + c * 1024, i)
            q[to, :, :, :, cols] = (mine + rb[to, :, :, :, cols].astype(F32)).astype(BF)
            return 0

        lax.fori_loop(0, 4, keep, 0)
        q[to, :, :, :, 1024:1152] = (inner + rb[to, :, :, :, 1024:1152].astype(F32)).astype(BF)
        if step < 3:
            stage1.append(
                copies.start(q.at[to, :, :, :, cuts[0]], ra1.at[0, step], me.at(z=to))
            )
    for d in (1, 2, 3):
        to = wrap(y, d)
        stage1.append(copies.start(q.at[:, to, :, :, cuts[1]], ra1.at[1, d - 1], me.at(y=to)))
        to = wrap(x, d)
        stage1.append(copies.start(q.at[:, :, to, :, cuts[2]], ra1.at[2, d - 1], me.at(x=to)))
    own1 = (
        lambda: q[t, :, :, :, cuts[0]],
        lambda: q[:, y, :, :, cuts[1]],
        lambda: q[:, :, x, :, cuts[2]],
    )
    stage2 = []
    for p in range(3):
        arrived = stage1[:3] if p == 0 else stage1[2 + p :: 2]
        for copy in arrived:
            copy.wait_recv()
        value = own1[p]().astype(F32)
        for d in range(3):
            value = value + ra1[p, d].astype(F32)
        sa1[p] = value.astype(BF)
        for d in (1, 2, 3):
            if p == 0:
                to = wrap(y, d)
                stage2.append(copies.start(sa1.at[0, to], ra2.at[0, d - 1], me.at(y=to)))
            elif p == 1:
                to = wrap(x, d)
                stage2.append(copies.start(sa1.at[1, :, to], ra2.at[1, d - 1], me.at(x=to)))
            else:
                to = wrap(t, d)
                stage2.append(copies.start(sa1.at[2, to], ra2.at[2, d - 1], me.at(z=to)))
    own2 = (lambda: sa1[0, y], lambda: sa1[1, :, x], lambda: sa1[2, t])
    stage3 = []
    for p in range(3):
        for copy in stage2[3 * p : 3 * p + 3]:
            copy.wait_recv()
        value = own2[p]().astype(F32)
        for d in range(3):
            value = value + ra2[p, d].astype(F32)
        sa2[p] = value.astype(BF)
        for d in (1, 2, 3):
            if p == 0:
                to = wrap(x, d)
                stage3.append(copies.start(sa2.at[0, to], ra3.at[0, d - 1], me.at(x=to)))
            elif p == 1:
                to = wrap(t, d)
                stage3.append(copies.start(sa2.at[1, to], ra3.at[1, d - 1], me.at(z=to)))
            else:
                to = wrap(y, d)
                stage3.append(copies.start(sa2.at[2, to], ra3.at[2, d - 1], me.at(y=to)))
    own3 = (lambda: sa2[0, x], lambda: sa2[1, t], lambda: sa2[2, y])
    pieces = []
    for p in range(3):
        for copy in stage3[3 * p : 3 * p + 3]:
            copy.wait_recv()
        value = own3[p]().astype(F32)
        for d in range(3):
            value = value + ra3[p, d].astype(F32)
        pieces.append(value)
    root16 = root.reshape(16, 1)
    mean = pieces[2][:, 256:257] / 8192.0
    for p in range(3):
        width = 384 if p < 2 else 256
        cols = pl.ds(pl.multiple_of(t * 2048 + c * 1024 + p * 384, 128), width)
        unit = xg[:, 0, :, cols].reshape(16, width) / root16
        scaled = pieces[p][:, :width] * gain_ref[:, cols]
        out = xg[:, 1, :, cols].reshape(16, width) + (scaled - unit * mean) / root16
        eall_ref[y, x, :, pl.ds(pl.multiple_of(c * 1024 + p * 384, 128), width)] = out.astype(BF)

    base = c * 1024

    def e0x(pos):
        return eall_ref.at[y, pos, :, pl.ds(base, 512)]

    def e1y(pos):
        return eall_ref.at[pos, x, :, pl.ds(base + 512, 512)]

    def e0y(pos):
        return eall_ref.at[pos, :, :, pl.ds(base, 512)]

    def e1x(pos):
        return eall_ref.at[:, pos, :, pl.ds(base + 512, 512)]

    for rings in ([(x, e0x, dev_x), (y, e1y, dev_y)], [(y, e0y, dev_y), (x, e1x, dev_x)]):
        begun = [direct_begin(copies, *ring) for ring in rings]
        for b in begun:
            for copy in b:
                copy.wait_recv()
    whole = eall_ref.at[:, :, :, pl.ds(base, 1024)]
    copies.start(whole, whole, me.other()).wait_recv()
    both = eall_ref[y, x].astype(F32)
    embed_ref[...] = jnp.where(c == 0, both[:8], both[8:]).astype(BF)
    copies.finish()


def llm_part(llm_input, out_grad, llm_gain, w_gate, w_up, w_down):
    sems = 64
    part = (3, 3)
    return pl.pallas_call(
        llm_kernel,
        name="llm_part",
        out_shape=(
            jax.ShapeDtypeStruct((8, 2048), BF),
            jax.ShapeDtypeStruct((4, 4, 16, 2048), BF),
        ),
        in_specs=[VM, VM, VM, ANY, ANY, ANY],
        out_specs=(VM, VM),
        scratch_shapes=[
            pltpu.VMEM((2, 2, 8, 8192), F32),
            pltpu.VMEM((2, 4, 4, 16, 8192), BF),
            pltpu.VMEM(w_gate.shape, BF),
            pltpu.VMEM(w_up.shape, BF),
            pltpu.VMEM(w_down.shape, BF),
            pltpu.VMEM((256, w_gate.shape[1]), F32),
            pltpu.VMEM((256, w_gate.shape[1]), F32),
            pltpu.VMEM((256, w_gate.shape[1]), F32),
            pltpu.VMEM((256, w_gate.shape[1]), BF),
            pltpu.VMEM((256, w_gate.shape[1]), BF),
            pltpu.VMEM((4, 4, 4, 16, 1152), BF),
            pltpu.VMEM((4, 4, 4, 16, 1152), BF),
            pltpu.VMEM((4, 4, 4, 16, 1152), BF),
            pltpu.VMEM(part + (4, 4, 16, 384), BF),
            pltpu.VMEM(part + (4, 16, 384), BF),
            pltpu.VMEM(part + (16, 384), BF),
            pltpu.VMEM((3, 4, 4, 16, 384), BF),
            pltpu.VMEM((3, 4, 16, 384), BF),
            pltpu.SemaphoreType.DMA((3,)),
            pltpu.SemaphoreType.DMA((sems + 20,)),
            pltpu.SemaphoreType.DMA((sems + 20,)),
        ],
        compiler_params=pltpu.CompilerParams(
            collective_id=0, has_side_effects=True, vmem_limit_bytes=60 * 1024 * 1024
        ),
    )(llm_input, out_grad, llm_gain.reshape(1, -1), w_gate, w_up, w_down)


def vis_kernel(part_ref, all_ref, mine, got, send, recv):
    me = Place()
    c, t, x, y = me.c, me.t, me.x, me.y
    targets = [me.other()]
    targets += [me.at(z=wrap(t, d)) for d in (1, 2, 3)]
    targets += [me.at(x=wrap(x, d)) for d in (1, 2, 3)]
    targets += [me.at(y=wrap(y, d)) for d in (1, 2, 3)]
    mine[...] = part_ref[...].astype(BF)
    greet(targets)
    copies = Copies(send, recv)
    begun = [copies.start(mine, got.at[d - 1], me.at(z=wrap(t, d))) for d in (1, 3, 2)]
    value = part_ref[...]
    for copy in begun:
        copy.wait_recv()
    for d in range(3):
        value = value + got[d].astype(F32)
    all_ref[c, y, x] = value.astype(BF)

    def dev_x(pos):
        return me.at(x=pos)

    def dev_y(pos):
        return me.at(y=pos)

    def e0x(pos):
        return all_ref.at[c, y, pos, :, pl.ds(0, 384)]

    def e1y(pos):
        return all_ref.at[c, pos, x, :, pl.ds(384, 256)]

    def e0y(pos):
        return all_ref.at[c, pos, :, :, pl.ds(0, 384)]

    def e1x(pos):
        return all_ref.at[c, :, pos, :, pl.ds(384, 256)]

    for rings in ([(x, e0x, dev_x), (y, e1y, dev_y)], [(y, e0y, dev_y), (x, e1x, dev_x)]):
        begun = [direct_begin(copies, *ring) for ring in rings]
        for b in begun:
            for copy in b:
                copy.wait_recv()
    copies.start(all_ref.at[c], all_ref.at[c], me.other()).wait_recv()
    copies.finish()


def vis_exchange(part):
    return pl.pallas_call(
        vis_kernel,
        name="vis_exchange",
        out_shape=jax.ShapeDtypeStruct((2, 4, 4, 48, 640), BF),
        in_specs=[VM],
        out_specs=VM,
        scratch_shapes=[
            pltpu.VMEM((48, 640), BF),
            pltpu.VMEM((3, 48, 640), BF),
            pltpu.SemaphoreType.DMA((20,)),
            pltpu.SemaphoreType.DMA((20,)),
        ],
        compiler_params=pltpu.CompilerParams(collective_id=1, has_side_effects=True),
    )(part)


def ln_kernel(part_ref, sum_ref, mine, got, send, recv):
    me = Place()
    t = me.t
    mine[...] = part_ref[...].astype(BF)
    greet([me.at(z=wrap(t, d)) for d in (1, 2, 3)])
    copies = Copies(send, recv)
    begun = [
        copies.start(mine.at[wrap(t, d)], got.at[d - 1], me.at(z=wrap(t, d))) for d in (1, 3, 2)
    ]
    value = part_ref[t]
    for copy in begun:
        copy.wait_recv()
    for d in range(3):
        value = value + got[d].astype(F32)
    sum_ref[...] = value
    copies.finish()


def ln_exchange(part):
    return pl.pallas_call(
        ln_kernel,
        name="ln_exchange",
        out_shape=jax.ShapeDtypeStruct((48, 384), F32),
        in_specs=[VM],
        out_specs=VM,
        scratch_shapes=[
            pltpu.VMEM((4, 48, 384), BF),
            pltpu.VMEM((3, 48, 384), BF),
            pltpu.SemaphoreType.DMA((3,)),
            pltpu.SemaphoreType.DMA((3,)),
        ],
        compiler_params=pltpu.CompilerParams(collective_id=2, has_side_effects=True),
    )(part)


def erf_gelu_slope(values):
    return (
        0.5 * (1.0 + lax.erf(values * 0.7071067811865476))
        + values * jnp.exp(-0.5 * values * values) * 0.3989422804014327
    )


def tanh_gelu_and_slope(values):
    inner = 0.7978845608028654 * (values + 0.044715 * values * values * values)
    tangent = jnp.tanh(inner)
    act = 0.5 * values * (1.0 + tangent)
    slope = 0.5 * (1.0 + tangent) + 0.5 * values * (
        1.0 - tangent * tangent
    ) * 0.7978845608028654 * (1.0 + 3.0 * 0.044715 * values * values)
    return act, slope


def touched_rows(keep_row, live_count, grid):
    width = (grid + 1) // 2
    slots = jnp.arange(keep_row.shape[0], dtype=jnp.int32)[None, :]
    quarter = jnp.arange(4, dtype=jnp.int32)[:, None]
    pool_row = (keep_row // width)[None, :]
    pool_col = (keep_row % width)[None, :]
    grid_row = 2 * pool_row + quarter // 2
    grid_col = 2 * pool_col + quarter % 2
    inside = (grid_row < grid) & (grid_col < grid) & (slots < live_count)
    row_cells = jnp.where(2 * pool_row + 1 < grid, 2.0, 1.0)
    col_cells = jnp.where(2 * pool_col + 1 < grid, 2.0, 1.0)
    weight = jnp.where(inside, 1.0 / (row_cells * col_cells), 0.0).astype(F32)
    feature = jnp.where(inside, grid_row * grid + grid_col, 0)
    return feature.reshape(-1), weight.reshape(-1)


def shards(
    llm_input,
    out_grad,
    llm_gain,
    w_gate,
    w_up,
    w_down,
    keep_index,
    keep_count,
    seq_order,
    vision_in,
    vision_out,
    vis_gain,
    w_proj,
    w_fc1,
    w_fc2,
):
    frame = lax.axis_index("frame")
    tensor = lax.axis_index("tensor")
    core = frame % 2
    chip = frame // 2
    cells, width = vision_in.shape

    feature, weight = touched_rows(keep_index[0], keep_count[0], GRID)
    spot = (feature[:, None] == jnp.arange(cells, dtype=jnp.int32)[None, :]).astype(BF)
    rows_out = nn(spot, vision_out).astype(BF)
    rows_in = nn(spot, vision_in)
    center = jnp.mean(rows_in, axis=1, keepdims=True)
    variance = jnp.mean((rows_in - center) * (rows_in - center), axis=1, keepdims=True)
    deviation = jnp.sqrt(variance + 1e-06)
    unit_in = (rows_in - center) / deviation
    ln_out = (unit_in * vis_gain).astype(BF)
    meta = jnp.zeros((16, width), F32).at[0, :48].set(weight)
    meta = meta.at[1, 0].set(keep_count[0].astype(F32)).astype(BF)
    packed = jnp.concatenate([rows_out, ln_out, meta], axis=0)
    spread = lax.all_gather(packed, "frame", axis=0, tiled=False)

    embed, embed_all = llm_part(llm_input, out_grad, llm_gain, w_gate, w_up, w_down)

    counts = spread[:, 97, 0].astype(jnp.int32)
    ends = jnp.cumsum(counts)
    token = jnp.arange(192, dtype=jnp.int32)
    owner = jnp.sum((ends[None, :] <= token[:, None]).astype(jnp.int32), axis=1)
    starts = ends - counts
    slot = token - starts[owner]
    source = owner[:, None] * 48 + jnp.arange(4, dtype=jnp.int32)[None, :] * 12 + slot[:, None]
    source = source.reshape(16, 12, 4).transpose(0, 2, 1).reshape(768)
    pick_rows = (source[:, None] == jnp.arange(1536, dtype=jnp.int32)[None, :]).astype(BF)
    out_rows = nn(pick_rows, spread[:, :48].reshape(1536, width)).astype(BF)
    ln_rows = nn(pick_rows, spread[:, 48:96].reshape(1536, width)).astype(BF)
    weights = spread[:, 96, :48].reshape(1536).astype(F32)[source]
    token_of = jnp.broadcast_to(token.reshape(16, 1, 12), (16, 4, 12)).reshape(768)
    position = seq_order[:192][token_of]

    pre_act = nn(out_rows, w_proj)
    slope = erf_gelu_slope(pre_act) * weights[:, None]
    fc_pre = nn(ln_rows, w_fc1)
    fc_act, fc_slope = tanh_gelu_and_slope(fc_pre)
    fc_act = fc_act.astype(BF)

    choose = (position[:, None] == jnp.arange(256, dtype=jnp.int32)[None, :]).astype(BF)
    kept = nn(choose, embed_all.reshape(256, 2048))
    act_grad = (kept * slope).astype(BF)
    mine = lax.dynamic_slice_in_dim(act_grad, chip * 48, 48, 0)
    w_mine = lax.dynamic_slice_in_dim(w_proj, core * 512, 640, 0)
    gathered = vis_exchange(nt(mine, w_mine)).reshape(2, 768, 640)
    vis_b = jnp.concatenate([gathered[0], gathered[1][:, 128:]], axis=1)
    block = width // 32
    out_cols = lax.dynamic_slice_in_dim(out_rows, frame * block, block, 1)
    proj_grad = tn(out_cols, act_grad)
    fc_pre_grad = (nt(vis_b, w_fc2) * fc_slope).astype(BF)
    local = jnp.arange(48, dtype=jnp.int32)
    here = (source[None, :] == frame * 48 + local[:, None]).astype(BF)
    here_grad = nn(here, fc_pre_grad).astype(BF)
    quarter_w = width // 4
    gain4 = vis_gain.reshape(4, 1, quarter_w)
    unit4 = unit_in.reshape(48, 4, quarter_w).transpose(1, 0, 2)
    ln_part = jnp.stack(
        [nt(here_grad, w_fc1[i * quarter_w : (i + 1) * quarter_w]) for i in range(4)]
    )
    ln_part = ln_part * gain4
    sums = jnp.sum(ln_part, axis=(0, 2))
    dots = jnp.sum(ln_part * unit4, axis=(0, 2))
    extra = jnp.stack([sums, dots], axis=1)
    extra = jnp.broadcast_to(extra[None], (4, 48, 2))
    packed_ln = jnp.concatenate([ln_part, extra, jnp.zeros((4, 48, 94), F32)], axis=2)
    ln_sum = ln_exchange(packed_ln)
    vis_mine = lax.dynamic_slice_in_dim(vis_b, tensor * quarter_w, quarter_w, 1)
    vis_mine = nn(here, vis_mine)
    unit_mine = lax.dynamic_index_in_dim(unit4, tensor, 0, keepdims=False)
    back = (
        vis_mine
        + (
            ln_sum[:, :quarter_w]
            - ln_sum[:, quarter_w : quarter_w + 1] / width
            - unit_mine * (ln_sum[:, quarter_w + 1 : quarter_w + 2] / width)
        )
        / deviation
    )
    feature_grad = tn(spot, back.astype(BF)).astype(BF)
    ln_cols = lax.dynamic_slice_in_dim(ln_rows, frame * block, block, 1)
    fc1_grad = tn(ln_cols, fc_pre_grad)
    vis_cols = lax.dynamic_slice_in_dim(vis_b, frame * block, block, 1)
    fc2_grad = tn(fc_act, vis_cols)
    return (embed, proj_grad, fc1_grad, fc2_grad, feature_grad)


def solution(mesh):
    in_specs = (
        P("frame", None),
        P("frame", None),
        P(),
        P(None, ("frame", "tensor")),
        P(None, ("frame", "tensor")),
        P(("frame", "tensor"), None),
        P("frame", None),
        P("frame"),
        P(),
        P("frame", None),
        P("frame", None),
        P(),
        P(None, "tensor"),
        P(None, "tensor"),
        P("tensor", None),
    )
    out_specs = (
        P("frame", "tensor"),
        P("frame", "tensor"),
        P("frame", "tensor"),
        P("tensor", "frame"),
        P("frame", "tensor"),
    )
    return jax.shard_map(shards, mesh=mesh, in_specs=in_specs, out_specs=out_specs, check_vma=False)
```

```python
import functools

import jax
import jax.numpy as jnp
import numpy as np
from jax import lax
from jax.experimental import pallas as pl
from jax.experimental.pallas import tpu as pltpu
from jax.sharding import PartitionSpec as P

GRID = 27
BF = jnp.bfloat16
F32 = jnp.float32
MESH = pl.DeviceIdType.MESH
ANY = pl.BlockSpec(memory_space=pl.ANY)
VM = pl.BlockSpec(memory_space=pltpu.VMEM)


def nt(left, right):
    return lax.dot_general(left, right, (((1,), (1,)), ((), ())), preferred_element_type=F32)


def tn(left, right):
    return lax.dot_general(left, right, (((0,), (0,)), ((), ())), preferred_element_type=F32)


def nn(left, right):
    return jnp.dot(left, right, preferred_element_type=F32)


class Place:
    def __init__(self):
        frame = lax.axis_index("frame")
        self.frame = frame
        self.t = lax.axis_index("tensor")
        self.c = lax.rem(frame, 2)
        self.k = frame // 2
        self.x = lax.rem(self.k, 4)
        self.y = self.k // 4

    def at(self, y=None, x=None, z=None, core=None):
        y = self.y if y is None else y
        x = self.x if x is None else x
        z = self.t if z is None else z
        core = self.c if core is None else core
        return ((y * 4 + x) * 2 + core, z)

    def other(self):
        return self.at(core=1 - self.c)


def greet(targets):
    barrier = pltpu.get_barrier_semaphore()
    for target in targets:
        pl.semaphore_signal(barrier, inc=1, device_id=target, device_id_type=MESH)
    pl.semaphore_wait(barrier, len(targets))


def wrap(pos, d):
    return lax.rem(pos + d, 4)


class Copies:
    def __init__(self, send, recv):
        self.send, self.recv, self.used, self.open = send, recv, 0, []

    def start(self, src, dst, target):
        i = self.used
        self.used += 1
        copy = pltpu.make_async_remote_copy(
            src_ref=src,
            dst_ref=dst,
            send_sem=self.send.at[i],
            recv_sem=self.recv.at[i],
            device_id=target,
            device_id_type=MESH,
        )
        copy.start()
        self.open.append(copy)
        return copy

    def finish(self):
        for copy in self.open:
            copy.wait_send()


def ring_begin(copies, pos, view, dev):
    right = copies.start(view(pos, None), view(pos, None), dev(wrap(pos, 1)))
    left = copies.start(view(pos, None), view(pos, None), dev(wrap(pos, 3)))
    return (right, left)


def ring_middle(copies, pos, view, dev, begun):
    right, left = begun
    right.wait_recv()
    on_right = copies.start(view(wrap(pos, 3), 0), view(wrap(pos, 3), 0), dev(wrap(pos, 1)))
    left.wait_recv()
    on_left = copies.start(view(wrap(pos, 1), 1), view(wrap(pos, 1), 1), dev(wrap(pos, 3)))
    return (on_right, on_left)


def ring_end(middle):
    for copy in middle:
        copy.wait_recv()


def direct_begin(copies, pos, view, dev):
    return [copies.start(view(pos), view(pos), dev(wrap(pos, d))) for d in (1, 3, 2)]


def pick(start, width, half):
    if half is None:
        return pl.ds(start, width)
    return pl.ds(start + half * (width // 2), width // 2)


def llm_kernel(
    x_ref, g_ref, gain_ref, wg_hbm, wu_hbm, wd_hbm,
    embed_ref, eall_ref,
    xg, buf, wg, wu, wd, acc_g, acc_u, acc_h, gg, ug, sb, rb, q,
    ra1, ra2, ra3, sa1, sa2,
    wsem, send, recv,
):
    me = Place()
    c, t, x, y = me.c, me.t, me.x, me.y
    loads = [
        pltpu.make_async_copy(wg_hbm, wg, wsem.at[0]),
        pltpu.make_async_copy(wu_hbm, wu, wsem.at[1]),
        pltpu.make_async_copy(wd_hbm, wd, wsem.at[2]),
    ]
    for load in loads:
        load.start()
    xg[c, 0] = x_ref[...].astype(F32)
    xg[c, 1] = g_ref[...].astype(F32)
    targets = [me.other()]
    targets += [me.at(z=wrap(t, d)) for d in (1, 2, 3)]
    targets += [
        me.at(y=wrap(y, dy), x=wrap(x, dx)) for dy in range(4) for dx in range(4) if dy or dx
    ]
    greet(targets)
    copies = Copies(send, recv)
    swap = copies.start(xg.at[c], xg.at[c], me.other())
    swap.wait_recv()

    rows = xg[:, 0]
    total = jnp.sum(rows * rows, axis=2, keepdims=True)
    root = jnp.sqrt(total / 8192.0 + 1e-06)

    def make_block(i, _):
        cols = pl.ds(pl.multiple_of(i * 1024, 1024), 1024)
        normed = xg[:, 0, :, cols] / root * gain_ref[:, cols][None]
        block = jnp.where(c == 0, normed, xg[:, 1, :, cols])
        buf[c, y, x, :, cols] = block.reshape(16, 1024).astype(BF)
        return 0

    lax.fori_loop(0, 8, make_block, 0)

    def view0x(pos, half):
        return buf.at[c, y, pos, :, pick(0, 4096, half)]

    def view1y(pos, half):
        return buf.at[c, pos, x, :, pick(4096, 4096, half)]

    def view0y(pos, half):
        return buf.at[c, pos, :, :, pick(0, 4096, half)]

    def view1x(pos, half):
        return buf.at[c, :, pos, :, pick(4096, 4096, half)]

    def dev_x(pos):
        return me.at(x=pos)

    def dev_y(pos):
        return me.at(y=pos)

    crossed = []

    def cross(view):
        crossed.append(copies.start(view, view, me.other()))

    for step in (0, 1):
        rings = (
            [(x, view0x, dev_x), (y, view1y, dev_y)]
            if step == 0
            else [(y, view0y, dev_y), (x, view1x, dev_x)]
        )
        begun = [ring_begin(copies, *ring) for ring in rings]
        if step == 1:
            for pos, view, _ in rings:
                cross(view(pos, None))
        middle = [ring_middle(copies, *ring, b) for ring, b in zip(rings, begun)]
        if step == 1:
            for pos, view, _ in rings:
                cross(view(wrap(pos, 1), None))
                cross(view(wrap(pos, 3), None))
        for m in middle:
            ring_end(m)
        if step == 1:
            for pos, view, _ in rings:
                cross(view(wrap(pos, 2), None))
    for load in loads:
        load.wait()
    for copy in crossed:
        copy.wait_recv()

    acc_g[...] = jnp.zeros_like(acc_g)
    acc_u[...] = jnp.zeros_like(acc_u)
    acc_h[...] = jnp.zeros_like(acc_h)

    def first(i, _):
        cols = pl.ds(pl.multiple_of(i * 1024, 1024), 1024)
        normed = buf[0, :, :, :, cols].reshape(256, 1024)
        acc_g[...] += nt(normed, wg[:, cols])
        acc_u[...] += nt(normed, wu[:, cols])
        grads = buf[1, :, :, :, cols].reshape(256, 1024)
        acc_h[...] += nt(grads, wd[:, cols])
        return 0

    lax.fori_loop(0, 8, first, 0)
    gate, up, hidden = acc_g[...], acc_u[...], acc_h[...]
    sig = jax.nn.sigmoid(gate)
    up_grad = (hidden * gate * sig).astype(BF)
    gate_grad = (hidden * up * sig * (1.0 + gate * (1.0 - sig))).astype(BF)
    gg[...] = gate_grad
    ug[...] = up_grad
    inner = jnp.sum(
        gate_grad.astype(F32) * gate + up_grad.astype(F32) * up, axis=1, keepdims=True
    )
    inner = jnp.broadcast_to(inner, (256, 128)).reshape(4, 4, 16, 128)

    def part(base, i):
        cols = pl.ds(pl.multiple_of(base + i * 256, 256), 256)
        value = nn(gg[...], wg[:, cols]) + nn(ug[...], wu[:, cols])
        return value.reshape(4, 4, 16, 256)

    halves = []
    for step in range(4):
        to = wrap(t, step + 1)

        def give(i, _):
            cols = pl.ds(pl.multiple_of(i * 256, 256), 256)
            sb[to, :, :, :, cols] = part(to * 2048 + (1 - c) * 1024, i).astype(BF)
            return 0

        lax.fori_loop(0, 4, give, 0)
        sb[to, :, :, :, 1024:1152] = inner.astype(BF)
        halves.append(copies.start(sb.at[to], rb.at[to], me.other()))

    cuts = (pl.ds(0, 384), pl.ds(384, 384), pl.ds(768, 384))
    stage1 = []
    for step in range(4):
        to = wrap(t, step + 1)
        halves[step].wait_recv()

        def keep(i, _):
            cols = pl.ds(pl.multiple_of(i * 256, 256), 256)
            mine = part(to * 2048 + c * 1024, i)
            q[to, :, :, :, cols] = (mine + rb[to, :, :, :, cols].astype(F32)).astype(BF)
            return 0

        lax.fori_loop(0, 4, keep, 0)
        q[to, :, :, :, 1024:1152] = (inner + rb[to, :, :, :, 1024:1152].astype(F32)).astype(BF)
        if step < 3:
            stage1.append(
                copies.start(q.at[to, :, :, :, cuts[0]], ra1.at[0, step], me.at(z=to))
            )
    for d in (1, 2, 3):
        to = wrap(y, d)
        stage1.append(copies.start(q.at[:, to, :, :, cuts[1]], ra1.at[1, d - 1], me.at(y=to)))
        to = wrap(x, d)
        stage1.append(copies.start(q.at[:, :, to, :, cuts[2]], ra1.at[2, d - 1], me.at(x=to)))
    own1 = (
        lambda: q[t, :, :, :, cuts[0]],
        lambda: q[:, y, :, :, cuts[1]],
        lambda: q[:, :, x, :, cuts[2]],
    )
    stage2 = []
    for p in range(3):
        arrived = stage1[:3] if p == 0 else stage1[2 + p :: 2]
        for copy in arrived:
            copy.wait_recv()
        value = own1[p]().astype(F32)
        for d in range(3):
            value = value + ra1[p, d].astype(F32)
        sa1[p] = value.astype(BF)
        for d in (1, 2, 3):
            if p == 0:
                to = wrap(y, d)
                stage2.append(copies.start(sa1.at[0, to], ra2.at[0, d - 1], me.at(y=to)))
            elif p == 1:
                to = wrap(x, d)
                stage2.append(copies.start(sa1.at[1, :, to], ra2.at[1, d - 1], me.at(x=to)))
            else:
                to = wrap(t, d)
                stage2.append(copies.start(sa1.at[2, to], ra2.at[2, d - 1], me.at(z=to)))
    own2 = (lambda: sa1[0, y], lambda: sa1[1, :, x], lambda: sa1[2, t])
    stage3 = []
    for p in range(3):
        for copy in stage2[3 * p : 3 * p + 3]:
            copy.wait_recv()
        value = own2[p]().astype(F32)
        for d in range(3):
            value = value + ra2[p, d].astype(F32)
        sa2[p] = value.astype(BF)
        for d in (1, 2, 3):
            if p == 0:
                to = wrap(x, d)
                stage3.append(copies.start(sa2.at[0, to], ra3.at[0, d - 1], me.at(x=to)))
            elif p == 1:
                to = wrap(t, d)
                stage3.append(copies.start(sa2.at[1, to], ra3.at[1, d - 1], me.at(z=to)))
            else:
                to = wrap(y, d)
                stage3.append(copies.start(sa2.at[2, to], ra3.at[2, d - 1], me.at(y=to)))
    own3 = (lambda: sa2[0, x], lambda: sa2[1, t], lambda: sa2[2, y])
    pieces = []
    for p in range(3):
        for copy in stage3[3 * p : 3 * p + 3]:
            copy.wait_recv()
        value = own3[p]().astype(F32)
        for d in range(3):
            value = value + ra3[p, d].astype(F32)
        pieces.append(value)
    root16 = root.reshape(16, 1)
    mean = pieces[2][:, 256:257] / 8192.0
    for p in range(3):
        width = 384 if p < 2 else 256
        cols = pl.ds(pl.multiple_of(t * 2048 + c * 1024 + p * 384, 128), width)
        unit = xg[:, 0, :, cols].reshape(16, width) / root16
        scaled = pieces[p][:, :width] * gain_ref[:, cols]
        out = xg[:, 1, :, cols].reshape(16, width) + (scaled - unit * mean) / root16
        eall_ref[y, x, :, pl.ds(pl.multiple_of(c * 1024 + p * 384, 128), width)] = out.astype(BF)

    base = c * 1024

    def e0x(pos):
        return eall_ref.at[y, pos, :, pl.ds(base, 512)]

    def e1y(pos):
        return eall_ref.at[pos, x, :, pl.ds(base + 512, 512)]

    def e0y(pos):
        return eall_ref.at[pos, :, :, pl.ds(base, 512)]

    def e1x(pos):
        return eall_ref.at[:, pos, :, pl.ds(base + 512, 512)]

    for rings in ([(x, e0x, dev_x), (y, e1y, dev_y)], [(y, e0y, dev_y), (x, e1x, dev_x)]):
        begun = [direct_begin(copies, *ring) for ring in rings]
        for b in begun:
            for copy in b:
                copy.wait_recv()
    whole = eall_ref.at[:, :, :, pl.ds(base, 1024)]
    copies.start(whole, whole, me.other()).wait_recv()
    both = eall_ref[y, x].astype(F32)
    embed_ref[...] = jnp.where(c == 0, both[:8], both[8:]).astype(BF)
    copies.finish()


def llm_part(llm_input, out_grad, llm_gain, w_gate, w_up, w_down):
    sems = 64
    w_gate, w_up = w_gate.T, w_up.T
    hidden = w_gate.shape[0]
    part = (3, 3)
    return pl.pallas_call(
        llm_kernel,
        name="llm_part",
        out_shape=(
            jax.ShapeDtypeStruct((8, 2048), BF),
            jax.ShapeDtypeStruct((4, 4, 16, 2048), BF),
        ),
        in_specs=[VM, VM, VM, ANY, ANY, ANY],
        out_specs=(VM, VM),
        scratch_shapes=[
            pltpu.VMEM((2, 2, 8, 8192), F32),
            pltpu.VMEM((2, 4, 4, 16, 8192), BF),
            pltpu.VMEM(w_gate.shape, BF),
            pltpu.VMEM(w_up.shape, BF),
            pltpu.VMEM(w_down.shape, BF),
            pltpu.VMEM((256, hidden), F32),
            pltpu.VMEM((256, hidden), F32),
            pltpu.VMEM((256, hidden), F32),
            pltpu.VMEM((256, hidden), BF),
            pltpu.VMEM((256, hidden), BF),
            pltpu.VMEM((4, 4, 4, 16, 1152), BF),
            pltpu.VMEM((4, 4, 4, 16, 1152), BF),
            pltpu.VMEM((4, 4, 4, 16, 1152), BF),
            pltpu.VMEM(part + (4, 4, 16, 384), BF),
            pltpu.VMEM(part + (4, 16, 384), BF),
            pltpu.VMEM(part + (16, 384), BF),
            pltpu.VMEM((3, 4, 4, 16, 384), BF),
            pltpu.VMEM((3, 4, 16, 384), BF),
            pltpu.SemaphoreType.DMA((3,)),
            pltpu.SemaphoreType.DMA((sems + 20,)),
            pltpu.SemaphoreType.DMA((sems + 20,)),
        ],
        compiler_params=pltpu.CompilerParams(
            collective_id=0, has_side_effects=True, vmem_limit_bytes=60 * 1024 * 1024
        ),
    )(llm_input, out_grad, llm_gain.reshape(1, -1), w_gate, w_up, w_down)


def erf_gelu_slope(values):
    return (
        0.5 * (1.0 + lax.erf(values * 0.7071067811865476))
        + values * jnp.exp(-0.5 * values * values) * 0.3989422804014327
    )


def tanh_gelu_and_slope(values):
    square = values * values
    inner = 0.7978845608028654 * values * (1.0 + 0.044715 * square)
    tangent = jnp.tanh(inner)
    half = 0.5 * (1.0 + tangent)
    act = values * half
    slope = half + 0.5 * values * (1.0 - tangent * tangent) * 0.7978845608028654 * (
        1.0 + 3.0 * 0.044715 * square
    )
    return act, slope


def one_hot(left, right):
    return jnp.where(left == right, 1.0, 0.0).astype(BF)


def vision_kernel(
    spread_hbm, eall_hbm, pos_ref, feature_ref, unit_ref, dev_ref, gain_ref, column_ref, rowcode_ref,
    rowline_ref, local_ref, wp_hbm, w1_hbm, w2_hbm,
    proj_ref, fc1_ref, fc2_ref, fg_ref,
    spread, eall, wp, w1, w2, comp, hot, slope, act_b, fslope, fgrad, grads,
    vmine, vgot, vis, away, px, lnp, lnmine, lngot, unit4, vis4,
    wsem, send, recv,
):
    me = Place()
    c, t, x, y, k = me.c, me.t, me.x, me.y, me.k
    loads = [
        pltpu.make_async_copy(spread_hbm, spread, wsem.at[0]),
        pltpu.make_async_copy(wp_hbm, wp, wsem.at[1]),
        pltpu.make_async_copy(w1_hbm, w1, wsem.at[2]),
        pltpu.make_async_copy(eall_hbm, eall, wsem.at[3]),
        pltpu.make_async_copy(w2_hbm, w2, wsem.at[4]),
    ]
    for load in loads:
        load.start()
    targets = [me.other()]
    targets += [me.at(z=wrap(t, d)) for d in (1, 2, 3)]
    targets += [me.at(x=wrap(x, d)) for d in (1, 2, 3)]
    targets += [me.at(y=wrap(y, d)) for d in (1, 2, 3)]
    greet(targets)
    copies = Copies(send, recv)

    loads[0].wait()
    counts = spread[:, 0:16, 2432:2560].astype(F32)[:, 0, :]
    frame_of, quarter_of, slot_of = column_ref[0:1, :], column_ref[1:2, :], column_ref[2:3, :]
    frames = lax.broadcasted_iota(jnp.int32, (32, 1536), 0)
    wide = jnp.broadcast_to(counts[:, :1], (32, 1536))
    offset = jnp.sum(jnp.where(frames < frame_of, wide, 0.0), axis=0, keepdims=True)
    count = jnp.sum(jnp.where(frames == frame_of, wide, 0.0), axis=0, keepdims=True)
    code = (offset.astype(jnp.int32) + slot_of) * 4 + quarter_of
    code = jnp.where(slot_of < count.astype(jnp.int32), code, -1)
    hot[...] = one_hot(rowcode_ref[...], code)
    lanes = lax.broadcasted_iota(jnp.int32, (32, 128), 0)
    own_offset = jnp.sum(jnp.where(lanes < me.frame, counts, 0.0), axis=0, keepdims=True)
    own_count = jnp.sum(jnp.where(lanes == me.frame, counts, 0.0), axis=0, keepdims=True)
    own_offset = own_offset.astype(jnp.int32)[:, :1]
    own_count = own_count.astype(jnp.int32)[:, :1]
    local_slot, local_quarter = local_ref[:, 0:1], local_ref[:, 1:2]
    own_code = (own_offset + local_slot) * 4 + local_quarter
    own_code = jnp.where(local_slot < own_count, own_code, -1)
    here = one_hot(own_code, rowline_ref[...])

    def compact(i, _):
        cols = pl.ds(pl.multiple_of(i * 256, 256), 256)
        comp[:, cols] = nn(hot[...], spread[:, :, cols].reshape(1536, 256)).astype(BF)
        return 0

    lax.fori_loop(0, 10, compact, 0)

    loads[1].wait()
    base = c * 1024

    def first(i, _):
        rows = pl.ds(pl.multiple_of((i // 4) * 256, 256), 256)
        cols = pl.multiple_of(lax.rem(i, 4) * 256, 256)
        pre = nn(comp[rows, 0:1152], wp[:, pl.ds(base + cols, 256)])
        weight = comp[rows, 2304:2305].astype(F32)
        slope[rows, pl.ds(cols, 256)] = erf_gelu_slope(pre) * weight
        return 0

    lax.fori_loop(0, 12, first, 0)
    loads[2].wait()

    def second(i, _):
        rows = pl.ds(pl.multiple_of(i * 128, 128), 128)
        act, tilt = tanh_gelu_and_slope(nt(comp[rows, 1152:2304], w1[...]))
        act_b[rows, :] = act.astype(BF)
        fslope[rows, :] = tilt
        return 0

    lax.fori_loop(0, 6, second, 0)

    mine = pl.ds(pl.multiple_of(k * 48, 48), 48)
    pre = nn(comp[mine, 0:1152], wp[...])
    tilt = erf_gelu_slope(pre) * comp[mine, 2304:2305].astype(F32)
    loads[3].wait()
    places = lax.broadcasted_iota(jnp.int32, (48, 256), 1)
    kept = nn(one_hot(pos_ref[mine, :], places), eall[...].reshape(256, 2048))
    act48 = (kept * tilt).astype(BF)
    part = nt(act48, wp[pl.ds(pl.multiple_of(c * 512, 512), 640), :])
    vmine[...] = part.astype(BF)
    begun = [copies.start(vmine, vgot.at[d - 1], me.at(z=wrap(t, d))) for d in (1, 3, 2)]

    places = lax.broadcasted_iota(jnp.int32, (768, 256), 1)
    choose = one_hot(pos_ref[...], places)

    def third(i, _):
        cols = pl.multiple_of(i * 256, 256)
        kept = nn(choose, eall[:, :, :, pl.ds(base + cols, 256)].reshape(256, 256))
        grads[:, pl.ds(cols, 256)] = (kept * slope[:, pl.ds(cols, 256)]).astype(BF)
        return 0

    value = part
    for copy in begun:
        copy.wait_recv()
    for d in range(3):
        value = value + vgot[d].astype(F32)
    vis[c, y, x] = value.astype(BF)

    def dev_x(pos):
        return me.at(x=pos)

    def dev_y(pos):
        return me.at(y=pos)

    def e0x(pos):
        return vis.at[c, y, pos, :, pl.ds(0, 384)]

    def e1y(pos):
        return vis.at[c, pos, x, :, pl.ds(384, 256)]

    def e0y(pos):
        return vis.at[c, pos, :, :, pl.ds(0, 384)]

    def e1x(pos):
        return vis.at[c, :, pos, :, pl.ds(384, 256)]

    begun = [direct_begin(copies, x, e0x, dev_x), direct_begin(copies, y, e1y, dev_y)]
    lax.fori_loop(0, 4, third, 0)
    for b in begun:
        for copy in b:
            copy.wait_recv()
    begun = [direct_begin(copies, y, e0y, dev_y), direct_begin(copies, x, e1x, dev_x)]
    crossed = [
        copies.start(e0y(y), e0y(y), me.other()),
        copies.start(e1x(x), e1x(x), me.other()),
    ]

    source = lax.broadcasted_iota(jnp.int32, (1152, 128), 0)
    lane = lax.broadcasted_iota(jnp.int32, (1152, 128), 1)
    block = me.frame * 36
    other = (me.frame + 1 - 2 * c) * 36
    want = jnp.where(lane < 64, jnp.where(lane < 36, block + lane, -1),
                     jnp.where(lane < 100, other + lane - 64, -1))
    chosen = one_hot(source, want)
    out_cols = nn(comp[:, 0:1152], chosen).astype(BF)
    proj = tn(out_cols, grads[...])
    away[...] = proj[64:128]
    px_copy = copies.start(away, px, me.other())
    proj_ref[:, pl.ds(pl.multiple_of(base, 1024), 1024)] = proj[0:36]
    ln_cols = nn(comp[:, 1152:2304], chosen).astype(BF)

    for b, view, pos in ((begun[0], e0y, y), (begun[1], e1x, x)):
        for copy, d in zip(b, (3, 1, 2)):
            copy.wait_recv()
            crossed.append(copies.start(view(wrap(pos, d)), view(wrap(pos, d)), me.other()))
    px_copy.wait_recv()
    proj_ref[:, pl.ds(pl.multiple_of(1024 - base, 1024), 1024)] = px[0:36]
    for copy in crossed:
        copy.wait_recv()

    vis0 = vis[0].reshape(768, 640)
    vis1 = vis[1].reshape(768, 640)[:, 128:]
    loads[4].wait()

    def fourth(i, _):
        chips = pl.ds(i, 1)
        rows = pl.ds(pl.multiple_of(i * 192, 192), 192)
        low = vis[0, chips].reshape(192, 640)
        high = vis[1, chips].reshape(192, 640)[:, 128:]
        back = nt(low, w2[:, 0:640]) + nt(high, w2[:, 640:1152])
        fgrad[rows, :] = (back * fslope[rows, :]).astype(BF)
        return 0

    lax.fori_loop(0, 4, fourth, 0)
    here_grad = nn(here, fgrad[...]).astype(BF)
    ln_part = nn(here_grad, w1[...]) * gain_ref[...]
    sums = jnp.sum(ln_part, axis=1, keepdims=True)
    dots = jnp.sum(ln_part * unit_ref[...], axis=1, keepdims=True)
    lane = lax.broadcasted_iota(jnp.int32, (48, 96), 1)
    extra = jnp.where(lane == 0, sums, jnp.where(lane == 1, dots, 0.0))
    for i in range(4):
        lnp[i, :, 0:288] = ln_part[:, i * 288 : (i + 1) * 288]
        lnp[i, :, 288:384] = extra
    lnmine[...] = lnp[...].astype(BF)
    begun = [
        copies.start(lnmine.at[wrap(t, d)], lngot.at[d - 1], me.at(z=wrap(t, d))) for d in (1, 3, 2)
    ]
    fc1_ref[...] = tn(ln_cols, fgrad[...])[0:36]
    vis_cols = (nn(vis0, chosen[0:640]) + nn(vis1, chosen[640:1152])).astype(BF)
    fc2_ref[...] = tn(vis_cols, act_b[...])[0:36]
    vis_here = jnp.concatenate([nn(here, vis0), nn(here, vis1)], axis=1)
    for i in range(4):
        vis4[i] = vis_here[:, i * 288 : (i + 1) * 288]
        unit4[i] = unit_ref[:, i * 288 : (i + 1) * 288]
    for copy in begun:
        copy.wait_recv()
    value = lnp[t]
    for d in range(3):
        value = value + lngot[d].astype(F32)
    mean, slant = value[:, 288:289] / 1152.0, value[:, 289:290] / 1152.0
    result = vis4[t] + (value[:, 0:288] - mean - unit4[t] * slant) / dev_ref[...]
    cells = lax.broadcasted_iota(jnp.int32, (48, 729), 1)
    spot = one_hot(feature_ref[...], cells)
    fg_ref[...] = tn(result.astype(BF), spot).astype(BF)
    copies.finish()


def column_codes():
    column = np.arange(1536)
    code = np.zeros((8, 1536), np.int32)
    code[0], code[1], code[2] = column // 48, column % 48 // 12, column % 12
    return code


def row_codes():
    row = np.arange(768)
    return (row // 48 * 12 + row % 12) * 4 + row % 48 // 12


def local_codes():
    row = np.arange(48)
    return np.stack([row % 12, row // 12], axis=1).astype(np.int32)


def vision_part(spread, embed_all, seq_order, feature, unit_in, deviation, vis_gain, w_proj, w_fc1, w_fc2):
    codes = row_codes().astype(np.int32)
    position = jnp.broadcast_to(seq_order[:192].reshape(16, 1, 12), (16, 4, 12)).reshape(768, 1)
    w_fc1 = w_fc1.T
    hidden = w_fc2.shape[0]
    sems = 48
    return pl.pallas_call(
        vision_kernel,
        name="vision_part",
        out_shape=(
            jax.ShapeDtypeStruct((36, 2048), F32),
            jax.ShapeDtypeStruct((36, hidden), F32),
            jax.ShapeDtypeStruct((36, hidden), F32),
            jax.ShapeDtypeStruct((288, 729), BF),
        ),
        in_specs=[ANY, ANY] + [VM] * 9 + [ANY] * 3,
        out_specs=(VM, VM, VM, VM),
        scratch_shapes=[
            pltpu.VMEM((32, 48, 2560), BF),
            pltpu.VMEM((4, 4, 16, 2048), BF),
            pltpu.VMEM(w_proj.shape, BF),
            pltpu.VMEM(w_fc1.shape, BF),
            pltpu.VMEM(w_fc2.shape, BF),
            pltpu.VMEM((768, 2560), BF),
            pltpu.VMEM((768, 1536), BF),
            pltpu.VMEM((768, 1024), F32),
            pltpu.VMEM((768, hidden), BF),
            pltpu.VMEM((768, hidden), F32),
            pltpu.VMEM((768, hidden), BF),
            pltpu.VMEM((768, 1024), BF),
            pltpu.VMEM((48, 640), BF),
            pltpu.VMEM((3, 48, 640), BF),
            pltpu.VMEM((2, 4, 4, 48, 640), BF),
            pltpu.VMEM((64, 1024), F32),
            pltpu.VMEM((64, 1024), F32),
            pltpu.VMEM((4, 48, 384), F32),
            pltpu.VMEM((4, 48, 384), BF),
            pltpu.VMEM((3, 48, 384), BF),
            pltpu.VMEM((4, 48, 288), F32),
            pltpu.VMEM((4, 48, 288), F32),
            pltpu.SemaphoreType.DMA((5,)),
            pltpu.SemaphoreType.DMA((sems,)),
            pltpu.SemaphoreType.DMA((sems,)),
        ],
        compiler_params=pltpu.CompilerParams(
            collective_id=1, has_side_effects=True, vmem_limit_bytes=60 * 1024 * 1024
        ),
    )(
        spread, embed_all, position, feature, unit_in, deviation, vis_gain,
        jnp.asarray(column_codes()), jnp.asarray(codes.reshape(-1, 1)),
        jnp.asarray(codes.reshape(1, -1)), jnp.asarray(local_codes()),
        w_proj, w_fc1, w_fc2,
    )


def touched_rows(keep_row, live_count, grid):
    width = (grid + 1) // 2
    slots = jnp.arange(keep_row.shape[0], dtype=jnp.int32)[None, :]
    quarter = jnp.arange(4, dtype=jnp.int32)[:, None]
    pool_row = (keep_row // width)[None, :]
    pool_col = (keep_row % width)[None, :]
    grid_row = 2 * pool_row + quarter // 2
    grid_col = 2 * pool_col + quarter % 2
    inside = (grid_row < grid) & (grid_col < grid) & (slots < live_count)
    row_cells = jnp.where(2 * pool_row + 1 < grid, 2.0, 1.0)
    col_cells = jnp.where(2 * pool_col + 1 < grid, 2.0, 1.0)
    weight = jnp.where(inside, 1.0 / (row_cells * col_cells), 0.0).astype(F32)
    feature = jnp.where(inside, grid_row * grid + grid_col, 0)
    return feature.reshape(-1), weight.reshape(-1)


def shards(
    llm_input,
    out_grad,
    llm_gain,
    w_gate,
    w_up,
    w_down,
    keep_index,
    keep_count,
    seq_order,
    vision_in,
    vision_out,
    vis_gain,
    w_proj,
    w_fc1,
    w_fc2,
):
    cells = vision_in.shape[0]
    feature, weight = touched_rows(keep_index[0], keep_count[0], GRID)
    spot = (feature[:, None] == jnp.arange(cells, dtype=jnp.int32)[None, :]).astype(BF)
    rows_out = nn(spot, vision_out).astype(BF)
    rows_in = nn(spot, vision_in)
    center = jnp.mean(rows_in, axis=1, keepdims=True)
    variance = jnp.mean((rows_in - center) * (rows_in - center), axis=1, keepdims=True)
    deviation = jnp.sqrt(variance + 1e-06)
    unit_in = (rows_in - center) / deviation
    ln_out = (unit_in * vis_gain).astype(BF)
    extra = jnp.concatenate(
        [
            jnp.broadcast_to(weight[:, None], (48, 128)),
            jnp.broadcast_to(keep_count.astype(F32)[None, :], (48, 128)),
        ],
        axis=1,
    ).astype(BF)
    packed = jnp.concatenate([rows_out, ln_out, extra], axis=1)
    spread = lax.all_gather(packed, "frame", axis=0, tiled=False)
    embed, embed_all = llm_part(llm_input, out_grad, llm_gain, w_gate, w_up, w_down)
    proj_grad, fc1_grad, fc2_grad, feature_grad = vision_part(
        spread, embed_all, seq_order, feature.reshape(48, 1), unit_in, deviation,
        vis_gain.reshape(1, -1), w_proj, w_fc1, w_fc2,
    )
    return (embed, proj_grad, fc1_grad, fc2_grad.T, feature_grad.T)


def solution(mesh):
    in_specs = (
        P("frame", None),
        P("frame", None),
        P(),
        P(None, ("frame", "tensor")),
        P(None, ("frame", "tensor")),
        P(("frame", "tensor"), None),
        P("frame", None),
        P("frame"),
        P(),
        P("frame", None),
        P("frame", None),
        P(),
        P(None, "tensor"),
        P(None, "tensor"),
        P("tensor", None),
    )
    out_specs = (
        P("frame", "tensor"),
        P("frame", "tensor"),
        P("frame", "tensor"),
        P("tensor", "frame"),
        P("frame", "tensor"),
    )
    return jax.shard_map(shards, mesh=mesh, in_specs=in_specs, out_specs=out_specs, check_vma=False)
```

```python
import functools

import jax
import jax.numpy as jnp
import numpy as np
from jax import lax
from jax.experimental import pallas as pl
from jax.experimental.pallas import tpu as pltpu
from jax.sharding import PartitionSpec as P

GRID = 27
BF = jnp.bfloat16
F32 = jnp.float32
MESH = pl.DeviceIdType.MESH
ANY = pl.BlockSpec(memory_space=pl.ANY)
VM = pl.BlockSpec(memory_space=pltpu.VMEM)


def nt(left, right):
    return lax.dot_general(left, right, (((1,), (1,)), ((), ())), preferred_element_type=F32)


def tn(left, right):
    return lax.dot_general(left, right, (((0,), (0,)), ((), ())), preferred_element_type=F32)


def nn(left, right):
    return jnp.dot(left, right, preferred_element_type=F32)


class Place:
    def __init__(self):
        frame = lax.axis_index("frame")
        self.frame = frame
        self.t = lax.axis_index("tensor")
        self.c = lax.rem(frame, 2)
        self.k = frame // 2
        self.x = lax.rem(self.k, 4)
        self.y = self.k // 4

    def at(self, y=None, x=None, z=None, core=None):
        y = self.y if y is None else y
        x = self.x if x is None else x
        z = self.t if z is None else z
        core = self.c if core is None else core
        return ((y * 4 + x) * 2 + core, z)

    def other(self):
        return self.at(core=1 - self.c)


def greet(targets):
    barrier = pltpu.get_barrier_semaphore()
    for target in targets:
        pl.semaphore_signal(barrier, inc=1, device_id=target, device_id_type=MESH)
    pl.semaphore_wait(barrier, len(targets))


def wrap(pos, d):
    return lax.rem(pos + d, 4)


class Copies:
    def __init__(self, send, recv):
        self.send, self.recv, self.used, self.open = send, recv, 0, []

    def start(self, src, dst, target):
        i = self.used
        self.used += 1
        copy = pltpu.make_async_remote_copy(
            src_ref=src,
            dst_ref=dst,
            send_sem=self.send.at[i],
            recv_sem=self.recv.at[i],
            device_id=target,
            device_id_type=MESH,
        )
        copy.start()
        self.open.append(copy)
        return copy

    def finish(self):
        for copy in self.open:
            copy.wait_send()
        self.open = []

    def settle(self, some):
        for copy in some:
            copy.wait_send()
        self.open = [copy for copy in self.open if not any(copy is done for done in some)]


def ring_begin(copies, pos, view, dev):
    right = copies.start(view(pos, None), view(pos, None), dev(wrap(pos, 1)))
    left = copies.start(view(pos, None), view(pos, None), dev(wrap(pos, 3)))
    return (right, left)


def ring_middle(copies, pos, view, dev, begun):
    right, left = begun
    right.wait_recv()
    on_right = copies.start(view(wrap(pos, 3), 0), view(wrap(pos, 3), 0), dev(wrap(pos, 1)))
    left.wait_recv()
    on_left = copies.start(view(wrap(pos, 1), 1), view(wrap(pos, 1), 1), dev(wrap(pos, 3)))
    return (on_right, on_left)


def ring_end(middle):
    for copy in middle:
        copy.wait_recv()


def direct_begin(copies, pos, view, dev):
    return [copies.start(view(pos), view(pos), dev(wrap(pos, d))) for d in (1, 3, 2)]


def pick(start, width, half):
    if half is None:
        return pl.ds(start, width)
    return pl.ds(start + half * (width // 2), width // 2)


def erf_gelu_slope(values):
    return (
        0.5 * (1.0 + lax.erf(values * 0.7071067811865476))
        + values * jnp.exp(-0.5 * values * values) * 0.3989422804014327
    )


def tanh_gelu_and_slope(values):
    square = values * values
    inner = 0.7978845608028654 * values * (1.0 + 0.044715 * square)
    tangent = jnp.tanh(inner)
    half = 0.5 * (1.0 + tangent)
    act = values * half
    slope = half + 0.5 * values * (1.0 - tangent * tangent) * 0.7978845608028654 * (
        1.0 + 3.0 * 0.044715 * square
    )
    return act, slope


def one_hot(left, right):
    return jnp.where(left == right, 1.0, 0.0).astype(BF)


def whole_kernel(
    x_ref, g_ref, gain_ref, pack_ref, pos_ref, feature_ref, unit_ref, dev_ref, vgain_ref,
    column_ref, rowline_ref, local_ref,
    wg_hbm, wu_hbm, wd_hbm, wp_hbm, w1_hbm, w2_hbm,
    embed_ref, proj_ref, fc1_ref, fc2_ref, fg_ref,
    xg, buf, wg, wu, wd, acc_g, acc_u, acc_h, gg, ug, rb, q,
    ra1, ra2, ra3, sa1, sa2, eall_ref,
    spread, wp, w1, w2, comp,
    vmine, vgot, vis, away, px, lnp, lnmine, lngot, unit4, vis4,
    wsem, send, recv,
):
    me = Place()
    c, t, x, y, k = me.c, me.t, me.x, me.y, me.k
    loads = [
        pltpu.make_async_copy(source, target, wsem.at[i])
        for i, (source, target) in enumerate(
            ((wg_hbm, wg), (wu_hbm, wu), (wd_hbm, wd), (wp_hbm, wp), (w1_hbm, w1), (w2_hbm, w2))
        )
    ]
    for load in loads:
        load.start()
    xg[c, 0] = x_ref[...].astype(F32)
    xg[c, 1] = g_ref[...].astype(F32)
    spread[y, x, c] = pack_ref[...]
    targets = [me.other()]
    targets += [me.at(z=wrap(t, d)) for d in (1, 2, 3)]
    targets += [me.at(x=wrap(x, d)) for d in (1, 2, 3)]
    targets += [me.at(y=wrap(y, d)) for d in (1, 2, 3)]
    greet(targets)
    copies = Copies(send, recv)
    swap = copies.start(xg.at[c], xg.at[c], me.other())

    def view0x(pos, half):
        return buf.at[c, y, pos, :, pick(0, 4096, half)]

    def view1y(pos, half):
        return buf.at[c, pos, x, :, pick(4096, 4096, half)]

    def view0y(pos, half):
        return buf.at[c, pos, :, :, pick(0, 4096, half)]

    def view1x(pos, half):
        return buf.at[c, :, pos, :, pick(4096, 4096, half)]

    def dev_x(pos):
        return me.at(x=pos)

    def dev_y(pos):
        return me.at(y=pos)

    def spread0x(pos, half):
        return spread.at[y, pos, c, :, pick(0, 1280, half)]

    def spread1y(pos, half):
        return spread.at[pos, x, c, :, pick(1280, 1280, half)]

    def spread0y(pos, half):
        return spread.at[pos, :, c, :, pick(0, 1280, half)]

    def spread1x(pos, half):
        return spread.at[:, pos, c, :, pick(1280, 1280, half)]

    def cross(view):
        return copies.start(view, view, me.other())

    def begin(rings):
        return [ring_begin(copies, *ring) for ring in rings]

    def middle(rings, begun):
        return [ring_middle(copies, *ring, b) for ring, b in zip(rings, begun)]

    swap.wait_recv()
    rows = xg[:, 0]
    total = jnp.sum(rows * rows, axis=2, keepdims=True)
    root = jnp.sqrt(total / 8192.0 + 1e-06)

    def make_block(i, _):
        cols = pl.ds(pl.multiple_of(i * 1024, 1024), 1024)
        normed = xg[:, 0, :, cols] / root * gain_ref[:, cols][None]
        block = jnp.where(c == 0, normed, xg[:, 1, :, cols])
        buf[c, y, x, :, cols] = block.reshape(16, 1024).astype(BF)
        return 0

    lax.fori_loop(0, 8, make_block, 0)


    llm1 = [(x, view0x, dev_x), (y, view1y, dev_y)]
    llm2 = [(y, view0y, dev_y), (x, view1x, dev_x)]
    seen1 = [(x, spread0x, dev_x), (y, spread1y, dev_y)]
    seen2 = [(y, spread0y, dev_y), (x, spread1x, dev_x)]
    begun = begin(llm1)
    mid = middle(llm1, begun)
    for m in mid:
        ring_end(m)
    begun = begin(llm2)
    crossed = [cross(view(pos, None)) for pos, view, _ in llm2]
    seen_begun = begin(seen1)
    mid = middle(llm2, begun)
    for pos, view, _ in llm2:
        crossed.append(cross(view(wrap(pos, 1), None)))
        crossed.append(cross(view(wrap(pos, 3), None)))
    seen_mid = middle(seen1, seen_begun)
    for m in mid:
        ring_end(m)
    for pos, view, _ in llm2:
        crossed.append(cross(view(wrap(pos, 2), None)))
    for m in seen_mid:
        ring_end(m)
    sent, copies.open = copies.open, []
    seen_begun = begin(seen2)
    for load in loads[:3]:
        load.wait()
    for copy in crossed:
        copy.wait_recv()

    acc_g[...] = jnp.zeros_like(acc_g)
    acc_u[...] = jnp.zeros_like(acc_u)
    acc_h[...] = jnp.zeros_like(acc_h)

    def first(i, _):
        cols = pl.ds(pl.multiple_of(i * 1024, 1024), 1024)
        normed = buf[0, :, :, :, cols].reshape(256, 1024)
        acc_g[...] += nt(normed, wg[:, cols])
        acc_u[...] += nt(normed, wu[:, cols])
        grads = buf[1, :, :, :, cols].reshape(256, 1024)
        acc_h[...] += nt(grads, wd[:, cols])
        return 0

    lax.fori_loop(0, 8, first, 0)
    gate, up, hidden = acc_g[...], acc_u[...], acc_h[...]
    sig = jax.nn.sigmoid(gate)
    up_grad = (hidden * gate * sig).astype(BF)
    gate_grad = (hidden * up * sig * (1.0 + gate * (1.0 - sig))).astype(BF)
    gg[...] = gate_grad
    ug[...] = up_grad
    inner = jnp.sum(
        gate_grad.astype(F32) * gate + up_grad.astype(F32) * up, axis=1, keepdims=True
    )
    inner = jnp.broadcast_to(inner, (256, 128)).reshape(4, 4, 16, 128)

    def part(base, i):
        cols = pl.ds(pl.multiple_of(base + i * 256, 256), 256)
        value = nn(gg[...], wg[:, cols]) + nn(ug[...], wu[:, cols])
        return value.reshape(4, 4, 16, 256)

    seen_crossed = [cross(view(pos, None)) for pos, view, _ in seen2]
    seen_mid = middle(seen2, seen_begun)
    for pos, view, _ in seen2:
        seen_crossed.append(cross(view(wrap(pos, 1), None)))
        seen_crossed.append(cross(view(wrap(pos, 3), None)))
    for copy in sent:
        copy.wait_send()
    halves = []
    for step in range(4):
        to = wrap(t, step + 1)

        def give(i, _):
            cols = pl.ds(pl.multiple_of(to * 1152 + i * 256, 128), 256)
            buf[0, :, :, :, cols] = part(to * 2048 + (1 - c) * 1024, i).astype(BF)
            return 0

        lax.fori_loop(0, 4, give, 0)
        buf[0, :, :, :, pl.ds(pl.multiple_of(to * 1152 + 1024, 128), 128)] = inner.astype(BF)
        sent = buf.at[0, :, :, :, pl.ds(pl.multiple_of(to * 1152, 128), 1152)]
        halves.append(copies.start(sent, rb.at[to], me.other()))

    cuts = (pl.ds(0, 384), pl.ds(384, 384), pl.ds(768, 384))
    stage1 = []
    for step in range(4):
        to = wrap(t, step + 1)
        halves[step].wait_recv()

        def keep(i, _):
            cols = pl.ds(pl.multiple_of(i * 256, 256), 256)
            mine = part(to * 2048 + c * 1024, i)
            q[to, :, :, :, cols] = (mine + rb[to, :, :, :, cols].astype(F32)).astype(BF)
            return 0

        lax.fori_loop(0, 4, keep, 0)
        q[to, :, :, :, 1024:1152] = (inner + rb[to, :, :, :, 1024:1152].astype(F32)).astype(BF)
        if step < 3:
            stage1.append(
                copies.start(q.at[to, :, :, :, cuts[0]], ra1.at[0, step], me.at(z=to))
            )
    for d in (1, 2, 3):
        to = wrap(y, d)
        stage1.append(copies.start(q.at[:, to, :, :, cuts[1]], ra1.at[1, d - 1], me.at(y=to)))
        to = wrap(x, d)
        stage1.append(copies.start(q.at[:, :, to, :, cuts[2]], ra1.at[2, d - 1], me.at(x=to)))
    own1 = (
        lambda: q[t, :, :, :, cuts[0]],
        lambda: q[:, y, :, :, cuts[1]],
        lambda: q[:, :, x, :, cuts[2]],
    )
    for m in seen_mid:
        ring_end(m)
    for pos, view, _ in seen2:
        seen_crossed.append(cross(view(wrap(pos, 2), None)))
    for copy in seen_crossed:
        copy.wait_recv()
    copies.settle([copy for pair in seen_begun + seen_mid for copy in pair] + seen_crossed)

    counts = spread[:, :, :, 0:16, 2432:2560].reshape(32, 16, 128).astype(F32)[:, 0, :]
    frame_of, quarter_of, slot_of = column_ref[0:1, :], column_ref[1:2, :], column_ref[2:3, :]
    frames = lax.broadcasted_iota(jnp.int32, (32, 1536), 0)
    wide = jnp.broadcast_to(counts[:, :1], (32, 1536))
    offset = jnp.sum(jnp.where(frames < frame_of, wide, 0.0), axis=0, keepdims=True)
    count = jnp.sum(jnp.where(frames == frame_of, wide, 0.0), axis=0, keepdims=True)
    code = (offset.astype(jnp.int32) + slot_of) * 4 + quarter_of
    code = jnp.where(slot_of < count.astype(jnp.int32), code, -1)
    for i in range(3):
        chosen = one_hot(pos_ref[i * 256 : (i + 1) * 256, 1:2], code)
        buf[1, :, :, :, i * 1536 : (i + 1) * 1536] = chosen.reshape(4, 4, 16, 1536)
    lanes = lax.broadcasted_iota(jnp.int32, (32, 128), 0)
    own_offset = jnp.sum(jnp.where(lanes < me.frame, counts, 0.0), axis=0, keepdims=True)
    own_count = jnp.sum(jnp.where(lanes == me.frame, counts, 0.0), axis=0, keepdims=True)
    own_offset = own_offset.astype(jnp.int32)[:, :1]
    own_count = own_count.astype(jnp.int32)[:, :1]
    local_slot, local_quarter = local_ref[:, 0:1], local_ref[:, 1:2]
    own_code = (own_offset + local_slot) * 4 + local_quarter
    own_code = jnp.where(local_slot < own_count, own_code, -1)
    here = one_hot(own_code, rowline_ref[...])

    def compact(i, _):
        cols = pl.ds(pl.multiple_of(i * 256, 256), 256)
        block = spread[:, :, :, :, cols].reshape(1536, 256)
        for j in range(3):
            hot = buf[1, :, :, :, j * 1536 : (j + 1) * 1536].reshape(256, 1536)
            comp[j * 256 : (j + 1) * 256, cols] = nn(hot, block).astype(BF)
        return 0

    lax.fori_loop(0, 10, compact, 0)
    base = c * 1024
    loads[3].wait()

    def first(i, _):
        rows = pl.ds(pl.multiple_of((i // 4) * 192, 48), 192)
        pair = pl.ds(pl.multiple_of(lax.rem(i // 4, 2) * 2, 2), 2)
        cols = pl.multiple_of(lax.rem(i, 4) * 256, 256)
        pre = nn(comp[rows, 0:1152], wp[:, pl.ds(base + cols, 256)])
        weight = comp[rows, 2304:2305].astype(F32)
        tilt = (erf_gelu_slope(pre) * weight).astype(BF)
        spread[i // 8, pair, :, :, pl.ds(1152 + cols, 256)] = tilt.reshape(2, 2, 48, 256)
        return 0

    stage2 = []
    for p in range(3):
        arrived = stage1[:3] if p == 0 else stage1[2 + p :: 2]
        for copy in arrived:
            copy.wait_recv()
        value = own1[p]().astype(F32)
        for d in range(3):
            value = value + ra1[p, d].astype(F32)
        sa1[p] = value.astype(BF)
        for d in (1, 2, 3):
            if p == 0:
                to = wrap(y, d)
                stage2.append(copies.start(sa1.at[0, to], ra2.at[0, d - 1], me.at(y=to)))
            elif p == 1:
                to = wrap(x, d)
                stage2.append(copies.start(sa1.at[1, :, to], ra2.at[1, d - 1], me.at(x=to)))
            else:
                to = wrap(t, d)
                stage2.append(copies.start(sa1.at[2, to], ra2.at[2, d - 1], me.at(z=to)))
    lax.fori_loop(0, 5, first, 0)
    own2 = (lambda: sa1[0, y], lambda: sa1[1, :, x], lambda: sa1[2, t])
    stage3 = []
    for p in range(3):
        for copy in stage2[3 * p : 3 * p + 3]:
            copy.wait_recv()
        value = own2[p]().astype(F32)
        for d in range(3):
            value = value + ra2[p, d].astype(F32)
        sa2[p] = value.astype(BF)
        for d in (1, 2, 3):
            if p == 0:
                to = wrap(x, d)
                stage3.append(copies.start(sa2.at[0, to], ra3.at[0, d - 1], me.at(x=to)))
            elif p == 1:
                to = wrap(t, d)
                stage3.append(copies.start(sa2.at[1, to], ra3.at[1, d - 1], me.at(z=to)))
            else:
                to = wrap(y, d)
                stage3.append(copies.start(sa2.at[2, to], ra3.at[2, d - 1], me.at(y=to)))
    lax.fori_loop(5, 10, first, 0)
    own3 = (lambda: sa2[0, x], lambda: sa2[1, t], lambda: sa2[2, y])
    pieces = []
    for p in range(3):
        for copy in stage3[3 * p : 3 * p + 3]:
            copy.wait_recv()
        value = own3[p]().astype(F32)
        for d in range(3):
            value = value + ra3[p, d].astype(F32)
        pieces.append(value)
    root16 = root.reshape(16, 1)
    mean = pieces[2][:, 256:257] / 8192.0
    for p in range(3):
        width = 384 if p < 2 else 256
        cols = pl.ds(pl.multiple_of(t * 2048 + c * 1024 + p * 384, 128), width)
        unit = xg[:, 0, :, cols].reshape(16, width) / root16
        scaled = pieces[p][:, :width] * gain_ref[:, cols]
        out = xg[:, 1, :, cols].reshape(16, width) + (scaled - unit * mean) / root16
        eall_ref[y, x, :, pl.ds(pl.multiple_of(c * 1024 + p * 384, 128), width)] = out.astype(BF)


    def embed0x(pos):
        return eall_ref.at[y, pos, :, pl.ds(base, 512)]

    def embed1y(pos):
        return eall_ref.at[pos, x, :, pl.ds(base + 512, 512)]

    def embed0y(pos):
        return eall_ref.at[pos, :, :, pl.ds(base, 512)]

    def embed1x(pos):
        return eall_ref.at[:, pos, :, pl.ds(base + 512, 512)]

    begun = [direct_begin(copies, x, embed0x, dev_x), direct_begin(copies, y, embed1y, dev_y)]
    lax.fori_loop(10, 16, first, 0)
    for b in begun:
        for copy in b:
            copy.wait_recv()
    copies.finish()
    begun = [direct_begin(copies, y, embed0y, dev_y), direct_begin(copies, x, embed1x, dev_x)]
    crossed = [cross(embed0y(y)), cross(embed1x(x))]
    loads[4].wait()

    def second(i, _):
        rows = pl.ds(pl.multiple_of(i * 96, 96), 96)
        act, tilt = tanh_gelu_and_slope(nt(comp[rows, 1152:2304], w1[...]))
        at = (2 + i // 4, lax.rem(i, 4))
        spread[at[0], at[1], :, :, 0:1076] = act.astype(BF).reshape(2, 48, 1076)
        spread[at[0], at[1], :, :, 1152:2228] = tilt.astype(BF).reshape(2, 48, 1076)
        return 0

    lax.fori_loop(0, 8, second, 0)
    for b, view, pos in ((begun[0], embed0y, y), (begun[1], embed1x, x)):
        for copy, d in zip(b, (3, 1, 2)):
            copy.wait_recv()
            crossed.append(cross(view(wrap(pos, d))))

    mine = pl.ds(pl.multiple_of(k * 48, 48), 48)
    pre = nn(comp[mine, 0:1152], wp[...])
    tilt = erf_gelu_slope(pre) * comp[mine, 2304:2305].astype(F32)
    for copy in crossed:
        copy.wait_recv()
    places = lax.broadcasted_iota(jnp.int32, (48, 256), 1)
    kept = nn(one_hot(pos_ref[mine, 0:1], places), eall_ref[...].reshape(256, 2048))
    act48 = (kept * tilt).astype(BF)
    part48 = nt(act48, wp[pl.ds(pl.multiple_of(c * 512, 512), 640), :])
    vmine[...] = part48.astype(BF)
    begun = [copies.start(vmine, vgot.at[d - 1], me.at(z=wrap(t, d))) for d in (1, 3, 2)]
    both = eall_ref[y, x].astype(F32)
    embed_ref[...] = jnp.where(c == 0, both[:8], both[8:]).astype(BF)
    places = lax.broadcasted_iota(jnp.int32, (192, 256), 1)

    def third(i, _):
        rows = pl.ds(pl.multiple_of(i * 192, 192), 192)
        kept = nn(
            one_hot(pos_ref[rows, 0:1], places),
            eall_ref[:, :, :, pl.ds(pl.multiple_of(base, 1024), 1024)].reshape(256, 1024),
        )
        pair = pl.ds(pl.multiple_of(lax.rem(i, 2) * 2, 2), 2)
        tilt = spread[i // 2, pair, :, :, 1152:2176].reshape(192, 1024).astype(F32)
        spread[i // 2, pair, :, :, 1152:2176] = (kept * tilt).astype(BF).reshape(2, 2, 48, 1024)
        return 0

    value = part48
    for copy in begun:
        copy.wait_recv()
    for d in range(3):
        value = value + vgot[d].astype(F32)
    vis[c, y, x] = value.astype(BF)

    def e0x(pos):
        return vis.at[c, y, pos, :, pl.ds(0, 384)]

    def e1y(pos):
        return vis.at[c, pos, x, :, pl.ds(384, 256)]

    def e0y(pos):
        return vis.at[c, pos, :, :, pl.ds(0, 384)]

    def e1x(pos):
        return vis.at[c, :, pos, :, pl.ds(384, 256)]

    begun = [direct_begin(copies, x, e0x, dev_x), direct_begin(copies, y, e1y, dev_y)]
    lax.fori_loop(0, 4, third, 0)
    for b in begun:
        for copy in b:
            copy.wait_recv()
    begun = [direct_begin(copies, y, e0y, dev_y), direct_begin(copies, x, e1x, dev_x)]
    crossed = [cross(e0y(y)), cross(e1x(x))]

    source = lax.broadcasted_iota(jnp.int32, (1152, 128), 0)
    lane = lax.broadcasted_iota(jnp.int32, (1152, 128), 1)
    block = me.frame * 36
    other = (me.frame + 1 - 2 * c) * 36
    want = jnp.where(lane < 64, jnp.where(lane < 36, block + lane, -1),
                     jnp.where(lane < 100, other + lane - 64, -1))
    chosen = one_hot(source, want)
    out_cols = nn(comp[:, 0:1152], chosen).astype(BF)
    proj = tn(out_cols, spread[0:2, :, :, :, 1152:2176].reshape(768, 1024))
    away[...] = proj[64:104]
    px_copy = copies.start(away, px, me.other())
    proj_ref[:, pl.ds(pl.multiple_of(base, 1024), 1024)] = proj[0:36]
    ln_cols = nn(comp[:, 1152:2304], chosen).astype(BF)

    for b, view, pos in ((begun[0], e0y, y), (begun[1], e1x, x)):
        for copy, d in zip(b, (3, 1, 2)):
            copy.wait_recv()
            crossed.append(copies.start(view(wrap(pos, d)), view(wrap(pos, d)), me.other()))
    px_copy.wait_recv()
    proj_ref[:, pl.ds(pl.multiple_of(1024 - base, 1024), 1024)] = px[0:36]
    for copy in crossed:
        copy.wait_recv()

    loads[5].wait()

    def fourth(i, _):
        low = vis[0, i].reshape(192, 640)
        high = vis[1, i].reshape(192, 640)[:, 128:]
        back = nt(low, w2[:, 0:640]) + nt(high, w2[:, 640:1152])
        pair = pl.ds(pl.multiple_of(lax.rem(i, 2) * 2, 2), 2)
        tilt = spread[2 + i // 2, pair, :, :, 1152:2228].reshape(192, 1076).astype(F32)
        spread[i // 2, pair, :, :, 0:1076] = (back * tilt).astype(BF).reshape(2, 2, 48, 1076)
        return 0

    lax.fori_loop(0, 4, fourth, 0)
    fgrad = spread[0:2, :, :, :, 0:1076].reshape(768, 1076)
    here_grad = nn(here, fgrad).astype(BF)
    ln_part = nn(here_grad, w1[...]) * vgain_ref[...]
    sums = jnp.sum(ln_part, axis=1, keepdims=True)
    dots = jnp.sum(ln_part * unit_ref[...], axis=1, keepdims=True)
    lane = lax.broadcasted_iota(jnp.int32, (48, 96), 1)
    extra = jnp.where(lane == 0, sums, jnp.where(lane == 1, dots, 0.0))
    for i in range(4):
        lnp[i, :, 0:288] = ln_part[:, i * 288 : (i + 1) * 288]
        lnp[i, :, 288:384] = extra
    lnmine[...] = lnp[...].astype(BF)
    vis0 = vis[0].reshape(768, 640)
    vis1 = vis[1].reshape(768, 640)[:, 128:]
    begun = [
        copies.start(lnmine.at[wrap(t, d)], lngot.at[d - 1], me.at(z=wrap(t, d))) for d in (1, 3, 2)
    ]
    fc1_ref[...] = tn(ln_cols, fgrad)[0:36]
    vis_cols = (nn(vis0, chosen[0:640]) + nn(vis1, chosen[640:1152])).astype(BF)
    fc2_ref[...] = tn(vis_cols, spread[2:4, :, :, :, 0:1076].reshape(768, 1076))[0:36]
    vis_here = jnp.concatenate([nn(here, vis0), nn(here, vis1)], axis=1)
    for i in range(4):
        vis4[i] = vis_here[:, i * 288 : (i + 1) * 288]
        unit4[i] = unit_ref[:, i * 288 : (i + 1) * 288]
    for copy in begun:
        copy.wait_recv()
    value = lnp[t]
    for d in range(3):
        value = value + lngot[d].astype(F32)
    mean, slant = value[:, 288:289] / 1152.0, value[:, 289:290] / 1152.0
    result = vis4[t] + (value[:, 0:288] - mean - unit4[t] * slant) / dev_ref[...]
    cells = lax.broadcasted_iota(jnp.int32, (48, 729), 1)
    spot = one_hot(feature_ref[...], cells)
    fg_ref[...] = tn(result.astype(BF), spot).astype(BF)
    copies.finish()


def column_codes():
    column = np.arange(1536)
    code = np.zeros((8, 1536), np.int32)
    code[0], code[1], code[2] = column // 48, column % 48 // 12, column % 12
    return code


def row_codes():
    row = np.arange(768)
    return (row // 48 * 12 + row % 12) * 4 + row % 48 // 12


def local_codes():
    row = np.arange(48)
    return np.stack([row % 12, row // 12], axis=1).astype(np.int32)


def whole(llm_input, out_grad, llm_gain, packed, seq_order, feature, unit_in, deviation, vis_gain,
          w_gate, w_up, w_down, w_proj, w_fc1, w_fc2):
    codes = row_codes().astype(np.int32)
    position = jnp.broadcast_to(seq_order[:192].reshape(16, 1, 12), (16, 4, 12)).reshape(768, 1)
    position = jnp.concatenate([position, jnp.asarray(codes.reshape(-1, 1))], axis=1)
    w_gate, w_up, w_fc1 = w_gate.T, w_up.T, w_fc1.T
    units = w_gate.shape[0]
    hidden = w_fc2.shape[0]
    sems = 160
    part = (3, 3)
    return pl.pallas_call(
        whole_kernel,
        name="whole",
        out_shape=(
            jax.ShapeDtypeStruct((8, 2048), BF),
            jax.ShapeDtypeStruct((36, 2048), F32),
            jax.ShapeDtypeStruct((36, hidden), F32),
            jax.ShapeDtypeStruct((36, hidden), F32),
            jax.ShapeDtypeStruct((288, 729), BF),
        ),
        in_specs=[VM] * 12 + [ANY] * 6,
        out_specs=(VM,) * 5,
        scratch_shapes=[
            pltpu.VMEM((2, 2, 8, 8192), F32),
            pltpu.VMEM((2, 4, 4, 16, 8192), BF),
            pltpu.VMEM(w_gate.shape, BF),
            pltpu.VMEM(w_up.shape, BF),
            pltpu.VMEM(w_down.shape, BF),
            pltpu.VMEM((256, units), F32),
            pltpu.VMEM((256, units), F32),
            pltpu.VMEM((256, units), F32),
            pltpu.VMEM((256, units), BF),
            pltpu.VMEM((256, units), BF),
            pltpu.VMEM((4, 4, 4, 16, 1152), BF),
            pltpu.VMEM((4, 4, 4, 16, 1152), BF),
            pltpu.VMEM(part + (4, 4, 16, 384), BF),
            pltpu.VMEM(part + (4, 16, 384), BF),
            pltpu.VMEM(part + (16, 384), BF),
            pltpu.VMEM((3, 4, 4, 16, 384), BF),
            pltpu.VMEM((3, 4, 16, 384), BF),
            pltpu.VMEM((4, 4, 16, 2048), BF),
            pltpu.VMEM((4, 4, 2, 48, 2560), BF),
            pltpu.VMEM(w_proj.shape, BF),
            pltpu.VMEM(w_fc1.shape, BF),
            pltpu.VMEM(w_fc2.shape, BF),
            pltpu.VMEM((768, 2560), BF),
            pltpu.VMEM((48, 640), BF),
            pltpu.VMEM((3, 48, 640), BF),
            pltpu.VMEM((2, 4, 4, 48, 640), BF),
            pltpu.VMEM((40, 1024), F32),
            pltpu.VMEM((40, 1024), F32),
            pltpu.VMEM((4, 48, 384), F32),
            pltpu.VMEM((4, 48, 384), BF),
            pltpu.VMEM((3, 48, 384), BF),
            pltpu.VMEM((4, 48, 288), F32),
            pltpu.VMEM((4, 48, 288), F32),
            pltpu.SemaphoreType.DMA((6,)),
            pltpu.SemaphoreType.DMA((sems,)),
            pltpu.SemaphoreType.DMA((sems,)),
        ],
        compiler_params=pltpu.CompilerParams(
            collective_id=0, has_side_effects=True, vmem_limit_bytes=63 * 1024 * 1024
        ),
    )(
        llm_input, out_grad, llm_gain.reshape(1, -1), packed, position, feature, unit_in, deviation,
        vis_gain, jnp.asarray(column_codes()),
        jnp.asarray(codes.reshape(1, -1)), jnp.asarray(local_codes()),
        w_gate, w_up, w_down, w_proj, w_fc1, w_fc2,
    )


def touched_rows(keep_row, live_count, grid):
    width = (grid + 1) // 2
    slots = jnp.arange(keep_row.shape[0], dtype=jnp.int32)[None, :]
    quarter = jnp.arange(4, dtype=jnp.int32)[:, None]
    pool_row = (keep_row // width)[None, :]
    pool_col = (keep_row % width)[None, :]
    grid_row = 2 * pool_row + quarter // 2
    grid_col = 2 * pool_col + quarter % 2
    inside = (grid_row < grid) & (grid_col < grid) & (slots < live_count)
    row_cells = jnp.where(2 * pool_row + 1 < grid, 2.0, 1.0)
    col_cells = jnp.where(2 * pool_col + 1 < grid, 2.0, 1.0)
    weight = jnp.where(inside, 1.0 / (row_cells * col_cells), 0.0).astype(F32)
    feature = jnp.where(inside, grid_row * grid + grid_col, 0)
    return feature.reshape(-1), weight.reshape(-1)


def shards(
    llm_input,
    out_grad,
    llm_gain,
    w_gate,
    w_up,
    w_down,
    keep_index,
    keep_count,
    seq_order,
    vision_in,
    vision_out,
    vis_gain,
    w_proj,
    w_fc1,
    w_fc2,
):
    cells = vision_in.shape[0]
    feature, weight = touched_rows(keep_index[0], keep_count[0], GRID)
    spot = (feature[:, None] == jnp.arange(cells, dtype=jnp.int32)[None, :]).astype(BF)
    rows_out = nn(spot, vision_out).astype(BF)
    rows_in = nn(spot, vision_in)
    center = jnp.mean(rows_in, axis=1, keepdims=True)
    variance = jnp.mean((rows_in - center) * (rows_in - center), axis=1, keepdims=True)
    deviation = jnp.sqrt(variance + 1e-06)
    unit_in = (rows_in - center) / deviation
    ln_out = (unit_in * vis_gain).astype(BF)
    extra = jnp.concatenate(
        [
            jnp.broadcast_to(weight[:, None], (48, 128)),
            jnp.broadcast_to(keep_count.astype(F32)[None, :], (48, 128)),
        ],
        axis=1,
    ).astype(BF)
    packed = jnp.concatenate([rows_out, ln_out, extra], axis=1)
    embed, proj_grad, fc1_grad, fc2_grad, feature_grad = whole(
        llm_input, out_grad, llm_gain, packed, seq_order, feature.reshape(48, 1), unit_in, deviation,
        vis_gain.reshape(1, -1), w_gate, w_up, w_down, w_proj, w_fc1, w_fc2,
    )
    return (embed, proj_grad, fc1_grad, fc2_grad.T, feature_grad.T)


def solution(mesh):
    in_specs = (
        P("frame", None),
        P("frame", None),
        P(),
        P(None, ("frame", "tensor")),
        P(None, ("frame", "tensor")),
        P(("frame", "tensor"), None),
        P("frame", None),
        P("frame"),
        P(),
        P("frame", None),
        P("frame", None),
        P(),
        P(None, "tensor"),
        P(None, "tensor"),
        P("tensor", None),
    )
    out_specs = (
        P("frame", "tensor"),
        P("frame", "tensor"),
        P("frame", "tensor"),
        P("tensor", "frame"),
        P("frame", "tensor"),
    )
    return jax.shard_map(shards, mesh=mesh, in_specs=in_specs, out_specs=out_specs, check_vma=False)
```

```python
import functools

import jax
import jax.numpy as jnp
import numpy as np
from jax import lax
from jax.experimental import pallas as pl
from jax.experimental.pallas import tpu as pltpu
from jax.sharding import PartitionSpec as P

GRID = 27
BF = jnp.bfloat16
F32 = jnp.float32
MESH = pl.DeviceIdType.MESH
ANY = pl.BlockSpec(memory_space=pl.ANY)
VM = pl.BlockSpec(memory_space=pltpu.VMEM)


def nt(left, right):
    return lax.dot_general(left, right, (((1,), (1,)), ((), ())), preferred_element_type=F32)


def tn(left, right):
    return lax.dot_general(left, right, (((0,), (0,)), ((), ())), preferred_element_type=F32)


def nn(left, right):
    return jnp.dot(left, right, preferred_element_type=F32)


class Place:
    def __init__(self):
        frame = lax.axis_index("frame")
        self.frame = frame
        self.t = lax.axis_index("tensor")
        self.c = lax.rem(frame, 2)
        self.k = frame // 2
        self.x = lax.rem(self.k, 4)
        self.y = self.k // 4

    def at(self, y=None, x=None, z=None, core=None):
        y = self.y if y is None else y
        x = self.x if x is None else x
        z = self.t if z is None else z
        core = self.c if core is None else core
        return ((y * 4 + x) * 2 + core, z)

    def other(self):
        return self.at(core=1 - self.c)


def greet(targets):
    barrier = pltpu.get_barrier_semaphore()
    for target in targets:
        pl.semaphore_signal(barrier, inc=1, device_id=target, device_id_type=MESH)
    pl.semaphore_wait(barrier, len(targets))


def wrap(pos, d):
    return lax.rem(pos + d, 4)


class Copies:
    def __init__(self, send, recv):
        self.send, self.recv, self.used, self.open = send, recv, 0, []

    def start(self, src, dst, target):
        i = self.used
        self.used += 1
        copy = pltpu.make_async_remote_copy(
            src_ref=src,
            dst_ref=dst,
            send_sem=self.send.at[i],
            recv_sem=self.recv.at[i],
            device_id=target,
            device_id_type=MESH,
        )
        copy.start()
        self.open.append(copy)
        return copy

    def finish(self):
        for copy in self.open:
            copy.wait_send()
        self.open = []

    def settle(self, some):
        for copy in some:
            copy.wait_send()
        self.open = [copy for copy in self.open if not any(copy is done for done in some)]


def ring_begin(copies, pos, view, dev):
    right = copies.start(view(pos, None), view(pos, None), dev(wrap(pos, 1)))
    left = copies.start(view(pos, None), view(pos, None), dev(wrap(pos, 3)))
    return (right, left)


def ring_middle(copies, pos, view, dev, begun):
    right, left = begun
    right.wait_recv()
    on_right = copies.start(view(wrap(pos, 3), 0), view(wrap(pos, 3), 0), dev(wrap(pos, 1)))
    left.wait_recv()
    on_left = copies.start(view(wrap(pos, 1), 1), view(wrap(pos, 1), 1), dev(wrap(pos, 3)))
    return (on_right, on_left)


def ring_end(middle):
    for copy in middle:
        copy.wait_recv()


def direct_begin(copies, pos, view, dev):
    return [copies.start(view(pos), view(pos), dev(wrap(pos, d))) for d in (1, 3, 2)]


def pick(start, width, half):
    if half is None:
        return pl.ds(start, width)
    return pl.ds(start + half * (width // 2), width // 2)


def erf_gelu_slope(values):
    return (
        0.5 * (1.0 + lax.erf(values * 0.7071067811865476))
        + values * jnp.exp(-0.5 * values * values) * 0.3989422804014327
    )


def tanh_gelu_and_slope(values):
    square = values * values
    inner = 0.7978845608028654 * values * (1.0 + 0.044715 * square)
    tangent = jnp.tanh(inner)
    half = 0.5 * (1.0 + tangent)
    act = values * half
    slope = half + 0.5 * values * (1.0 - tangent * tangent) * 0.7978845608028654 * (
        1.0 + 3.0 * 0.044715 * square
    )
    return act, slope


def one_hot(left, right):
    return jnp.where(left == right, 1.0, 0.0).astype(BF)


def whole_kernel(
    x_ref, g_ref, gain_ref, pack_ref, pos_ref, feature_ref, unit_ref, dev_ref, vgain_ref,
    column_ref, rowline_ref, local_ref,
    wg_hbm, wu_hbm, wd_hbm, wp_hbm, w1_hbm, w2_hbm,
    embed_ref, proj_ref, fc1_ref, fc2_ref, fg_ref,
    xg, buf, wg, wu, wd, acc_g, acc_u, acc_h, gg, ug, rb, q,
    ra1, ra2, ra3, sa1, sa2, eall_ref,
    spread, wp, w1, w2, comp,
    vmine, vgot, vis, away, px, lnp, lnmine, lngot, unit4, vis4,
    wsem, send, recv,
):
    me = Place()
    c, t, x, y, k = me.c, me.t, me.x, me.y, me.k
    loads = [
        pltpu.make_async_copy(source, target, wsem.at[i])
        for i, (source, target) in enumerate(
            ((wg_hbm, wg), (wu_hbm, wu), (wd_hbm, wd), (wp_hbm, wp), (w1_hbm, w1), (w2_hbm, w2))
        )
    ]
    for load in loads:
        load.start()
    xg[c, 0] = x_ref[...].astype(F32)
    xg[c, 1] = g_ref[...].astype(F32)
    spread[y, x, c] = pack_ref[...]
    targets = [me.other()]
    targets += [me.at(z=wrap(t, d)) for d in (1, 2, 3)]
    targets += [me.at(x=wrap(x, d)) for d in (1, 2, 3)]
    targets += [me.at(y=wrap(y, d)) for d in (1, 2, 3)]
    greet(targets)
    copies = Copies(send, recv)
    swap = copies.start(xg.at[c], xg.at[c], me.other())

    def view0x(pos, half):
        return buf.at[c, y, pos, :, pick(0, 4096, half)]

    def view1y(pos, half):
        return buf.at[c, pos, x, :, pick(4096, 4096, half)]

    def dev_x(pos):
        return me.at(x=pos)

    def dev_y(pos):
        return me.at(y=pos)

    def spread0x(pos, half):
        return spread.at[y, pos, c, :, pick(0, 1280, half)]

    def spread1y(pos, half):
        return spread.at[pos, x, c, :, pick(1280, 1280, half)]

    def spread0y(pos, half):
        return spread.at[pos, :, c, :, pick(0, 1280, half)]

    def spread1x(pos, half):
        return spread.at[:, pos, c, :, pick(1280, 1280, half)]

    def cross(view):
        return copies.start(view, view, me.other())

    def begin(rings):
        return [ring_begin(copies, *ring) for ring in rings]

    def middle(rings, begun):
        return [ring_middle(copies, *ring, b) for ring, b in zip(rings, begun)]

    swap.wait_recv()
    rows = xg[:, 0]
    total = jnp.sum(rows * rows, axis=2, keepdims=True)
    root = jnp.sqrt(total / 8192.0 + 1e-06)

    def make_block(i, _):
        cols = pl.ds(pl.multiple_of(i * 1024, 1024), 1024)
        normed = xg[:, 0, :, cols] / root * gain_ref[:, cols][None]
        block = jnp.where(c == 0, normed, xg[:, 1, :, cols])
        buf[c, y, x, :, cols] = block.reshape(16, 1024).astype(BF)
        return 0

    lax.fori_loop(0, 8, make_block, 0)


    def along_y(block):
        return (y, lambda pos, half: buf.at[c, pos, block, :, pick(0, 4096, half)], dev_y)

    def along_x(block):
        return (x, lambda pos, half: buf.at[c, block, pos, :, pick(4096, 4096, half)], dev_x)

    seen1 = [(x, spread0x, dev_x), (y, spread1y, dev_y)]
    seen2 = [(y, spread0y, dev_y), (x, spread1x, dev_x)]
    crossed = []

    def cross_all(rings, steps):
        for pos, view, _ in rings:
            for d in steps:
                crossed.append(cross(view(wrap(pos, d), None)))

    main = [(x, view0x, dev_x), (y, view1y, dev_y)]
    onward = [[along_y(wrap(x, d)), along_x(wrap(y, d))] for d in range(4)]
    begun = begin(main)
    going = {0: begin(onward[0])}
    cross_all(onward[0], (0,))
    mid = middle(main, begun)
    for d in (3, 1):
        going[d] = begin(onward[d])
        cross_all(onward[d], (0,))
    ends = middle(onward[0], going[0])
    cross_all(onward[0], (1, 3))
    for m in mid:
        ring_end(m)
    going[2] = begin(onward[2])
    cross_all(onward[2], (0,))
    for m in ends:
        ring_end(m)
    cross_all(onward[0], (2,))
    last = []
    for d in (3, 1, 2):
        last.append((d, middle(onward[d], going[d])))
        cross_all(onward[d], (1, 3))
    seen_begun = begin(seen1)
    for d, ends in last:
        for m in ends:
            ring_end(m)
        cross_all(onward[d], (2,))
    sent, copies.open = copies.open, []
    for load in loads[:3]:
        load.wait()
    seen_mid = middle(seen1, seen_begun)
    for copy in crossed:
        copy.wait_recv()

    acc_g[...] = jnp.zeros_like(acc_g)
    acc_u[...] = jnp.zeros_like(acc_u)
    acc_h[...] = jnp.zeros_like(acc_h)

    def first(i, _):
        cols = pl.ds(pl.multiple_of(i * 1024, 1024), 1024)
        normed = buf[0, :, :, :, cols].reshape(256, 1024)
        acc_g[...] += nt(normed, wg[:, cols])
        acc_u[...] += nt(normed, wu[:, cols])
        grads = buf[1, :, :, :, cols].reshape(256, 1024)
        acc_h[...] += nt(grads, wd[:, cols])
        return 0

    lax.fori_loop(0, 8, first, 0)
    for m in seen_mid:
        ring_end(m)
    copies.settle([copy for pair in seen_mid for copy in pair])
    seen_begun = begin(seen2)
    gate, up, hidden = acc_g[...], acc_u[...], acc_h[...]
    sig = jax.nn.sigmoid(gate)
    up_grad = (hidden * gate * sig).astype(BF)
    gate_grad = (hidden * up * sig * (1.0 + gate * (1.0 - sig))).astype(BF)
    gg[...] = gate_grad
    ug[...] = up_grad
    inner = jnp.sum(
        gate_grad.astype(F32) * gate + up_grad.astype(F32) * up, axis=1, keepdims=True
    )
    inner = jnp.broadcast_to(inner, (256, 128)).reshape(4, 4, 16, 128)

    def part(base, i):
        cols = pl.ds(pl.multiple_of(base + i * 256, 256), 256)
        value = nn(gg[...], wg[:, cols]) + nn(ug[...], wu[:, cols])
        return value.reshape(4, 4, 16, 256)

    seen_crossed = [cross(view(pos, None)) for pos, view, _ in seen2]
    for copy in sent:
        copy.wait_send()
    halves = []
    for step in range(4):
        to = wrap(t, step + 1)

        def give(i, _):
            cols = pl.ds(pl.multiple_of(to * 1152 + i * 256, 128), 256)
            buf[0, :, :, :, cols] = part(to * 2048 + (1 - c) * 1024, i).astype(BF)
            return 0

        lax.fori_loop(0, 4, give, 0)
        buf[0, :, :, :, pl.ds(pl.multiple_of(to * 1152 + 1024, 128), 128)] = inner.astype(BF)
        sent = buf.at[0, :, :, :, pl.ds(pl.multiple_of(to * 1152, 128), 1152)]
        halves.append(copies.start(sent, rb.at[to], me.other()))

    seen_mid = middle(seen2, seen_begun)
    for pos, view, _ in seen2:
        seen_crossed.append(cross(view(wrap(pos, 1), None)))
        seen_crossed.append(cross(view(wrap(pos, 3), None)))
    cuts = (pl.ds(0, 384), pl.ds(384, 384), pl.ds(768, 384))
    stage1 = []
    for step in range(4):
        to = wrap(t, step + 1)
        halves[step].wait_recv()

        def keep(i, _):
            cols = pl.ds(pl.multiple_of(i * 256, 256), 256)
            mine = part(to * 2048 + c * 1024, i)
            q[to, :, :, :, cols] = (mine + rb[to, :, :, :, cols].astype(F32)).astype(BF)
            return 0

        lax.fori_loop(0, 4, keep, 0)
        q[to, :, :, :, 1024:1152] = (inner + rb[to, :, :, :, 1024:1152].astype(F32)).astype(BF)
        if step < 3:
            stage1.append(
                copies.start(q.at[to, :, :, :, cuts[0]], ra1.at[0, step], me.at(z=to))
            )
    for d in (1, 2, 3):
        to = wrap(y, d)
        stage1.append(copies.start(q.at[:, to, :, :, cuts[1]], ra1.at[1, d - 1], me.at(y=to)))
        to = wrap(x, d)
        stage1.append(copies.start(q.at[:, :, to, :, cuts[2]], ra1.at[2, d - 1], me.at(x=to)))
    own1 = (
        lambda: q[t, :, :, :, cuts[0]],
        lambda: q[:, y, :, :, cuts[1]],
        lambda: q[:, :, x, :, cuts[2]],
    )
    for m in seen_mid:
        ring_end(m)
    for pos, view, _ in seen2:
        seen_crossed.append(cross(view(wrap(pos, 2), None)))
    for copy in seen_crossed:
        copy.wait_recv()
    copies.settle([copy for pair in seen_begun + seen_mid for copy in pair] + seen_crossed)

    counts = spread[:, :, :, 0:16, 2432:2560].reshape(32, 16, 128).astype(F32)[:, 0, :]
    frame_of, quarter_of, slot_of = column_ref[0:1, :], column_ref[1:2, :], column_ref[2:3, :]
    frames = lax.broadcasted_iota(jnp.int32, (32, 1536), 0)
    wide = jnp.broadcast_to(counts[:, :1], (32, 1536))
    offset = jnp.sum(jnp.where(frames < frame_of, wide, 0.0), axis=0, keepdims=True)
    count = jnp.sum(jnp.where(frames == frame_of, wide, 0.0), axis=0, keepdims=True)
    code = (offset.astype(jnp.int32) + slot_of) * 4 + quarter_of
    code = jnp.where(slot_of < count.astype(jnp.int32), code, -1)
    for i in range(3):
        chosen = one_hot(pos_ref[i * 256 : (i + 1) * 256, 1:2], code)
        buf[1, :, :, :, i * 1536 : (i + 1) * 1536] = chosen.reshape(4, 4, 16, 1536)
    lanes = lax.broadcasted_iota(jnp.int32, (32, 128), 0)
    own_offset = jnp.sum(jnp.where(lanes < me.frame, counts, 0.0), axis=0, keepdims=True)
    own_count = jnp.sum(jnp.where(lanes == me.frame, counts, 0.0), axis=0, keepdims=True)
    own_offset = own_offset.astype(jnp.int32)[:, :1]
    own_count = own_count.astype(jnp.int32)[:, :1]
    local_slot, local_quarter = local_ref[:, 0:1], local_ref[:, 1:2]
    own_code = (own_offset + local_slot) * 4 + local_quarter
    own_code = jnp.where(local_slot < own_count, own_code, -1)
    here = one_hot(own_code, rowline_ref[...])

    def compact(i, _):
        cols = pl.ds(pl.multiple_of(i * 256, 256), 256)
        block = spread[:, :, :, :, cols].reshape(1536, 256)
        for j in range(3):
            hot = buf[1, :, :, :, j * 1536 : (j + 1) * 1536].reshape(256, 1536)
            comp[j * 256 : (j + 1) * 256, cols] = nn(hot, block).astype(BF)
        return 0

    lax.fori_loop(0, 10, compact, 0)
    base = c * 1024
    loads[3].wait()

    def first(i, _):
        rows = pl.ds(pl.multiple_of((i // 4) * 192, 48), 192)
        pair = pl.ds(pl.multiple_of(lax.rem(i // 4, 2) * 2, 2), 2)
        cols = pl.multiple_of(lax.rem(i, 4) * 256, 256)
        pre = nn(comp[rows, 0:1152], wp[:, pl.ds(base + cols, 256)])
        weight = comp[rows, 2304:2305].astype(F32)
        tilt = (erf_gelu_slope(pre) * weight).astype(BF)
        spread[i // 8, pair, :, :, pl.ds(1152 + cols, 256)] = tilt.reshape(2, 2, 48, 256)
        return 0

    stage2 = []
    for p in range(3):
        arrived = stage1[:3] if p == 0 else stage1[2 + p :: 2]
        for copy in arrived:
            copy.wait_recv()
        value = own1[p]().astype(F32)
        for d in range(3):
            value = value + ra1[p, d].astype(F32)
        sa1[p] = value.astype(BF)
        for d in (1, 2, 3):
            if p == 0:
                to = wrap(y, d)
                stage2.append(copies.start(sa1.at[0, to], ra2.at[0, d - 1], me.at(y=to)))
            elif p == 1:
                to = wrap(x, d)
                stage2.append(copies.start(sa1.at[1, :, to], ra2.at[1, d - 1], me.at(x=to)))
            else:
                to = wrap(t, d)
                stage2.append(copies.start(sa1.at[2, to], ra2.at[2, d - 1], me.at(z=to)))
    lax.fori_loop(0, 5, first, 0)
    own2 = (lambda: sa1[0, y], lambda: sa1[1, :, x], lambda: sa1[2, t])
    stage3 = []
    for p in range(3):
        for copy in stage2[3 * p : 3 * p + 3]:
            copy.wait_recv()
        value = own2[p]().astype(F32)
        for d in range(3):
            value = value + ra2[p, d].astype(F32)
        sa2[p] = value.astype(BF)
        for d in (1, 2, 3):
            if p == 0:
                to = wrap(x, d)
                stage3.append(copies.start(sa2.at[0, to], ra3.at[0, d - 1], me.at(x=to)))
            elif p == 1:
                to = wrap(t, d)
                stage3.append(copies.start(sa2.at[1, to], ra3.at[1, d - 1], me.at(z=to)))
            else:
                to = wrap(y, d)
                stage3.append(copies.start(sa2.at[2, to], ra3.at[2, d - 1], me.at(y=to)))
    lax.fori_loop(5, 10, first, 0)
    own3 = (lambda: sa2[0, x], lambda: sa2[1, t], lambda: sa2[2, y])
    pieces = []
    for p in range(3):
        for copy in stage3[3 * p : 3 * p + 3]:
            copy.wait_recv()
        value = own3[p]().astype(F32)
        for d in range(3):
            value = value + ra3[p, d].astype(F32)
        pieces.append(value)
    root16 = root.reshape(16, 1)
    mean = pieces[2][:, 256:257] / 8192.0
    for p in range(3):
        width = 384 if p < 2 else 256
        cols = pl.ds(pl.multiple_of(t * 2048 + c * 1024 + p * 384, 128), width)
        unit = xg[:, 0, :, cols].reshape(16, width) / root16
        scaled = pieces[p][:, :width] * gain_ref[:, cols]
        out = xg[:, 1, :, cols].reshape(16, width) + (scaled - unit * mean) / root16
        eall_ref[y, x, :, pl.ds(pl.multiple_of(c * 1024 + p * 384, 128), width)] = out.astype(BF)


    def embed0x(pos):
        return eall_ref.at[y, pos, :, pl.ds(base, 512)]

    def embed1y(pos):
        return eall_ref.at[pos, x, :, pl.ds(base + 512, 512)]

    def embed0y(pos):
        return eall_ref.at[pos, :, :, pl.ds(base, 512)]

    def embed1x(pos):
        return eall_ref.at[:, pos, :, pl.ds(base + 512, 512)]

    begun = [direct_begin(copies, x, embed0x, dev_x), direct_begin(copies, y, embed1y, dev_y)]
    lax.fori_loop(10, 16, first, 0)
    for b in begun:
        for copy in b:
            copy.wait_recv()
    copies.finish()
    begun = [direct_begin(copies, y, embed0y, dev_y), direct_begin(copies, x, embed1x, dev_x)]
    crossed = [cross(embed0y(y)), cross(embed1x(x))]
    loads[4].wait()

    def second(i, _):
        rows = pl.ds(pl.multiple_of(i * 96, 96), 96)
        act, tilt = tanh_gelu_and_slope(nt(comp[rows, 1152:2304], w1[...]))
        at = (2 + i // 4, lax.rem(i, 4))
        spread[at[0], at[1], :, :, 0:1076] = act.astype(BF).reshape(2, 48, 1076)
        spread[at[0], at[1], :, :, 1152:2228] = tilt.astype(BF).reshape(2, 48, 1076)
        return 0

    lax.fori_loop(0, 8, second, 0)
    for b, view, pos in ((begun[0], embed0y, y), (begun[1], embed1x, x)):
        for copy, d in zip(b, (3, 1, 2)):
            copy.wait_recv()
            crossed.append(cross(view(wrap(pos, d))))

    mine = pl.ds(pl.multiple_of(k * 48, 48), 48)
    pre = nn(comp[mine, 0:1152], wp[...])
    tilt = erf_gelu_slope(pre) * comp[mine, 2304:2305].astype(F32)
    for copy in crossed:
        copy.wait_recv()
    places = lax.broadcasted_iota(jnp.int32, (48, 256), 1)
    kept = nn(one_hot(pos_ref[mine, 0:1], places), eall_ref[...].reshape(256, 2048))
    act48 = (kept * tilt).astype(BF)
    part48 = nt(act48, wp[pl.ds(pl.multiple_of(c * 512, 512), 640), :])
    vmine[...] = part48.astype(BF)
    begun = [copies.start(vmine, vgot.at[d - 1], me.at(z=wrap(t, d))) for d in (1, 3, 2)]
    both = eall_ref[y, x].astype(F32)
    embed_ref[...] = jnp.where(c == 0, both[:8], both[8:]).astype(BF)
    places = lax.broadcasted_iota(jnp.int32, (192, 256), 1)

    def third(i, _):
        rows = pl.ds(pl.multiple_of(i * 192, 192), 192)
        kept = nn(
            one_hot(pos_ref[rows, 0:1], places),
            eall_ref[:, :, :, pl.ds(pl.multiple_of(base, 1024), 1024)].reshape(256, 1024),
        )
        pair = pl.ds(pl.multiple_of(lax.rem(i, 2) * 2, 2), 2)
        tilt = spread[i // 2, pair, :, :, 1152:2176].reshape(192, 1024).astype(F32)
        spread[i // 2, pair, :, :, 1152:2176] = (kept * tilt).astype(BF).reshape(2, 2, 48, 1024)
        return 0

    value = part48
    for copy in begun:
        copy.wait_recv()
    for d in range(3):
        value = value + vgot[d].astype(F32)
    vis[c, y, x] = value.astype(BF)

    def e0x(pos):
        return vis.at[c, y, pos, :, pl.ds(0, 384)]

    def e1y(pos):
        return vis.at[c, pos, x, :, pl.ds(384, 256)]

    def e0y(pos):
        return vis.at[c, pos, :, :, pl.ds(0, 384)]

    def e1x(pos):
        return vis.at[c, :, pos, :, pl.ds(384, 256)]

    begun = [direct_begin(copies, x, e0x, dev_x), direct_begin(copies, y, e1y, dev_y)]
    lax.fori_loop(0, 4, third, 0)
    for b in begun:
        for copy in b:
            copy.wait_recv()
    begun = [direct_begin(copies, y, e0y, dev_y), direct_begin(copies, x, e1x, dev_x)]
    crossed = [cross(e0y(y)), cross(e1x(x))]

    source = lax.broadcasted_iota(jnp.int32, (1152, 128), 0)
    lane = lax.broadcasted_iota(jnp.int32, (1152, 128), 1)
    block = me.frame * 36
    other = (me.frame + 1 - 2 * c) * 36
    want = jnp.where(lane < 64, jnp.where(lane < 36, block + lane, -1),
                     jnp.where(lane < 100, other + lane - 64, -1))
    chosen = one_hot(source, want)
    out_cols = nn(comp[:, 0:1152], chosen).astype(BF)
    proj = tn(out_cols, spread[0:2, :, :, :, 1152:2176].reshape(768, 1024))
    away[...] = proj[64:104]
    px_copy = copies.start(away, px, me.other())
    proj_ref[:, pl.ds(pl.multiple_of(base, 1024), 1024)] = proj[0:36]
    ln_cols = nn(comp[:, 1152:2304], chosen).astype(BF)

    for b, view, pos in ((begun[0], e0y, y), (begun[1], e1x, x)):
        for copy, d in zip(b, (3, 1, 2)):
            copy.wait_recv()
            crossed.append(copies.start(view(wrap(pos, d)), view(wrap(pos, d)), me.other()))
    px_copy.wait_recv()
    proj_ref[:, pl.ds(pl.multiple_of(1024 - base, 1024), 1024)] = px[0:36]
    for copy in crossed:
        copy.wait_recv()

    loads[5].wait()

    def fourth(i, _):
        low = vis[0, i].reshape(192, 640)
        high = vis[1, i].reshape(192, 640)[:, 128:]
        back = nt(low, w2[:, 0:640]) + nt(high, w2[:, 640:1152])
        pair = pl.ds(pl.multiple_of(lax.rem(i, 2) * 2, 2), 2)
        tilt = spread[2 + i // 2, pair, :, :, 1152:2228].reshape(192, 1076).astype(F32)
        spread[i // 2, pair, :, :, 0:1076] = (back * tilt).astype(BF).reshape(2, 2, 48, 1076)
        return 0

    lax.fori_loop(0, 4, fourth, 0)
    fgrad = spread[0:2, :, :, :, 0:1076].reshape(768, 1076)
    here_grad = nn(here, fgrad).astype(BF)
    ln_part = nn(here_grad, w1[...]) * vgain_ref[...]
    sums = jnp.sum(ln_part, axis=1, keepdims=True)
    dots = jnp.sum(ln_part * unit_ref[...], axis=1, keepdims=True)
    lane = lax.broadcasted_iota(jnp.int32, (48, 96), 1)
    extra = jnp.where(lane == 0, sums, jnp.where(lane == 1, dots, 0.0))
    for i in range(4):
        lnp[i, :, 0:288] = ln_part[:, i * 288 : (i + 1) * 288]
        lnp[i, :, 288:384] = extra
    lnmine[...] = lnp[...].astype(BF)
    vis0 = vis[0].reshape(768, 640)
    vis1 = vis[1].reshape(768, 640)[:, 128:]
    begun = [
        copies.start(lnmine.at[wrap(t, d)], lngot.at[d - 1], me.at(z=wrap(t, d))) for d in (1, 3, 2)
    ]
    fc1_ref[...] = tn(ln_cols, fgrad)[0:36]
    vis_cols = (nn(vis0, chosen[0:640]) + nn(vis1, chosen[640:1152])).astype(BF)
    fc2_ref[...] = tn(vis_cols, spread[2:4, :, :, :, 0:1076].reshape(768, 1076))[0:36]
    vis_here = jnp.concatenate([nn(here, vis0), nn(here, vis1)], axis=1)
    for i in range(4):
        vis4[i] = vis_here[:, i * 288 : (i + 1) * 288]
        unit4[i] = unit_ref[:, i * 288 : (i + 1) * 288]
    for copy in begun:
        copy.wait_recv()
    value = lnp[t]
    for d in range(3):
        value = value + lngot[d].astype(F32)
    mean, slant = value[:, 288:289] / 1152.0, value[:, 289:290] / 1152.0
    result = vis4[t] + (value[:, 0:288] - mean - unit4[t] * slant) / dev_ref[...]
    cells = lax.broadcasted_iota(jnp.int32, (48, 729), 1)
    spot = one_hot(feature_ref[...], cells)
    fg_ref[...] = tn(result.astype(BF), spot).astype(BF)
    copies.finish()


def column_codes():
    column = np.arange(1536)
    code = np.zeros((8, 1536), np.int32)
    code[0], code[1], code[2] = column // 48, column % 48 // 12, column % 12
    return code


def row_codes():
    row = np.arange(768)
    return (row // 48 * 12 + row % 12) * 4 + row % 48 // 12


def local_codes():
    row = np.arange(48)
    return np.stack([row % 12, row // 12], axis=1).astype(np.int32)


def copy_kernel(*refs):
    count = len(refs) // 2
    copies = [
        pltpu.make_async_copy(refs[i], refs[count + i], refs[-1].at[i]) for i in range(count)
    ]
    for copy in copies:
        copy.start()
    for copy in copies:
        copy.wait()


def hand_over(arrays):
    return pl.pallas_call(
        copy_kernel,
        name="hand_over",
        out_shape=tuple(jax.ShapeDtypeStruct(a.shape, a.dtype) for a in arrays),
        in_specs=[ANY] * len(arrays),
        out_specs=(ANY,) * len(arrays),
        scratch_shapes=[pltpu.SemaphoreType.DMA((len(arrays),))],
    )(*arrays)


def whole(llm_input, out_grad, llm_gain, packed, seq_order, feature, unit_in, deviation, vis_gain,
          w_gate, w_up, w_down, w_proj, w_fc1, w_fc2):
    codes = row_codes().astype(np.int32)
    position = jnp.broadcast_to(seq_order[:192].reshape(16, 1, 12), (16, 4, 12)).reshape(768, 1)
    position = jnp.concatenate([position, jnp.asarray(codes.reshape(-1, 1))], axis=1)
    w_gate, w_up, w_fc1 = w_gate.T, w_up.T, w_fc1.T
    units = w_gate.shape[0]
    hidden = w_fc2.shape[0]
    sems = 200
    part = (3, 3)
    return pl.pallas_call(
        whole_kernel,
        name="whole",
        out_shape=(
            jax.ShapeDtypeStruct((8, 2048), BF),
            jax.ShapeDtypeStruct((36, 2048), F32),
            jax.ShapeDtypeStruct((36, hidden), F32),
            jax.ShapeDtypeStruct((36, hidden), F32),
            jax.ShapeDtypeStruct((288, 729), BF),
        ),
        in_specs=[VM] * 12 + [ANY] * 6,
        out_specs=(VM,) * 5,
        scratch_shapes=[
            pltpu.VMEM((2, 2, 8, 8192), F32),
            pltpu.VMEM((2, 4, 4, 16, 8192), BF),
            pltpu.VMEM(w_gate.shape, BF),
            pltpu.VMEM(w_up.shape, BF),
            pltpu.VMEM(w_down.shape, BF),
            pltpu.VMEM((256, units), F32),
            pltpu.VMEM((256, units), F32),
            pltpu.VMEM((256, units), F32),
            pltpu.VMEM((256, units), BF),
            pltpu.VMEM((256, units), BF),
            pltpu.VMEM((4, 4, 4, 16, 1152), BF),
            pltpu.VMEM((4, 4, 4, 16, 1152), BF),
            pltpu.VMEM(part + (4, 4, 16, 384), BF),
            pltpu.VMEM(part + (4, 16, 384), BF),
            pltpu.VMEM(part + (16, 384), BF),
            pltpu.VMEM((3, 4, 4, 16, 384), BF),
            pltpu.VMEM((3, 4, 16, 384), BF),
            pltpu.VMEM((4, 4, 16, 2048), BF),
            pltpu.VMEM((4, 4, 2, 48, 2560), BF),
            pltpu.VMEM(w_proj.shape, BF),
            pltpu.VMEM(w_fc1.shape, BF),
            pltpu.VMEM(w_fc2.shape, BF),
            pltpu.VMEM((768, 2560), BF),
            pltpu.VMEM((48, 640), BF),
            pltpu.VMEM((3, 48, 640), BF),
            pltpu.VMEM((2, 4, 4, 48, 640), BF),
            pltpu.VMEM((40, 1024), F32),
            pltpu.VMEM((40, 1024), F32),
            pltpu.VMEM((4, 48, 384), F32),
            pltpu.VMEM((4, 48, 384), BF),
            pltpu.VMEM((3, 48, 384), BF),
            pltpu.VMEM((4, 48, 288), F32),
            pltpu.VMEM((4, 48, 288), F32),
            pltpu.SemaphoreType.DMA((6,)),
            pltpu.SemaphoreType.DMA((sems,)),
            pltpu.SemaphoreType.DMA((sems,)),
        ],
        compiler_params=pltpu.CompilerParams(
            collective_id=0, has_side_effects=True, vmem_limit_bytes=63 * 1024 * 1024
        ),
    )(
        llm_input, out_grad, llm_gain.reshape(1, -1), packed, position, feature, unit_in, deviation,
        vis_gain, jnp.asarray(column_codes()),
        jnp.asarray(codes.reshape(1, -1)), jnp.asarray(local_codes()),
        w_gate, w_up, w_down, w_proj, w_fc1, w_fc2,
    )


def touched_rows(keep_row, live_count, grid):
    width = (grid + 1) // 2
    slots = jnp.arange(keep_row.shape[0], dtype=jnp.int32)[None, :]
    quarter = jnp.arange(4, dtype=jnp.int32)[:, None]
    pool_row = (keep_row // width)[None, :]
    pool_col = (keep_row % width)[None, :]
    grid_row = 2 * pool_row + quarter // 2
    grid_col = 2 * pool_col + quarter % 2
    inside = (grid_row < grid) & (grid_col < grid) & (slots < live_count)
    row_cells = jnp.where(2 * pool_row + 1 < grid, 2.0, 1.0)
    col_cells = jnp.where(2 * pool_col + 1 < grid, 2.0, 1.0)
    weight = jnp.where(inside, 1.0 / (row_cells * col_cells), 0.0).astype(F32)
    feature = jnp.where(inside, grid_row * grid + grid_col, 0)
    return feature.reshape(-1), weight.reshape(-1)


def shards(
    llm_input,
    out_grad,
    llm_gain,
    w_gate,
    w_up,
    w_down,
    keep_index,
    keep_count,
    seq_order,
    vision_in,
    vision_out,
    vis_gain,
    w_proj,
    w_fc1,
    w_fc2,
):
    cells = vision_in.shape[0]
    feature, weight = touched_rows(keep_index[0], keep_count[0], GRID)
    spot = (feature[:, None] == jnp.arange(cells, dtype=jnp.int32)[None, :]).astype(BF)
    rows_out = nn(spot, vision_out).astype(BF)
    rows_in = nn(spot, vision_in)
    center = jnp.mean(rows_in, axis=1, keepdims=True)
    variance = jnp.mean((rows_in - center) * (rows_in - center), axis=1, keepdims=True)
    deviation = jnp.sqrt(variance + 1e-06)
    unit_in = (rows_in - center) / deviation
    ln_out = (unit_in * vis_gain).astype(BF)
    extra = jnp.concatenate(
        [
            jnp.broadcast_to(weight[:, None], (48, 128)),
            jnp.broadcast_to(keep_count.astype(F32)[None, :], (48, 128)),
        ],
        axis=1,
    ).astype(BF)
    packed = jnp.concatenate([rows_out, ln_out, extra], axis=1)
    results = whole(
        llm_input, out_grad, llm_gain, packed, seq_order, feature.reshape(48, 1), unit_in, deviation,
        vis_gain.reshape(1, -1), w_gate, w_up, w_down, w_proj, w_fc1, w_fc2,
    )
    embed, proj_grad, fc1_grad, fc2_grad, feature_grad = hand_over(results)
    return (embed, proj_grad, fc1_grad, fc2_grad.T, feature_grad.T)


def solution(mesh):
    in_specs = (
        P("frame", None),
        P("frame", None),
        P(),
        P(None, ("frame", "tensor")),
        P(None, ("frame", "tensor")),
        P(("frame", "tensor"), None),
        P("frame", None),
        P("frame"),
        P(),
        P("frame", None),
        P("frame", None),
        P(),
        P(None, "tensor"),
        P(None, "tensor"),
        P("tensor", None),
    )
    out_specs = (
        P("frame", "tensor"),
        P("frame", "tensor"),
        P("frame", "tensor"),
        P("tensor", "frame"),
        P("frame", "tensor"),
    )
    return jax.shard_map(shards, mesh=mesh, in_specs=in_specs, out_specs=out_specs, check_vma=False)
```

```python
import functools

import jax
import jax.numpy as jnp
import numpy as np
from jax import lax
from jax.experimental import pallas as pl
from jax.experimental.pallas import tpu as pltpu
from jax.sharding import PartitionSpec as P

GRID = 27
BF = jnp.bfloat16
F32 = jnp.float32
MESH = pl.DeviceIdType.MESH
ANY = pl.BlockSpec(memory_space=pl.ANY)
VM = pl.BlockSpec(memory_space=pltpu.VMEM)


def nt(left, right):
    return lax.dot_general(left, right, (((1,), (1,)), ((), ())), preferred_element_type=F32)


def tn(left, right):
    return lax.dot_general(left, right, (((0,), (0,)), ((), ())), preferred_element_type=F32)


def nn(left, right):
    return jnp.dot(left, right, preferred_element_type=F32)


class Place:
    def __init__(self):
        frame = lax.axis_index("frame")
        self.frame = frame
        self.t = lax.axis_index("tensor")
        self.c = lax.rem(frame, 2)
        self.k = frame // 2
        self.x = lax.rem(self.k, 4)
        self.y = self.k // 4

    def at(self, y=None, x=None, z=None, core=None):
        y = self.y if y is None else y
        x = self.x if x is None else x
        z = self.t if z is None else z
        core = self.c if core is None else core
        return ((y * 4 + x) * 2 + core, z)

    def other(self):
        return self.at(core=1 - self.c)


def greet(targets):
    barrier = pltpu.get_barrier_semaphore()
    for target in targets:
        pl.semaphore_signal(barrier, inc=1, device_id=target, device_id_type=MESH)
    pl.semaphore_wait(barrier, len(targets))


def wrap(pos, d):
    return lax.rem(pos + d, 4)


class Copies:
    def __init__(self, send, recv):
        self.send, self.recv, self.used, self.open = send, recv, 0, []

    def start(self, src, dst, target):
        i = self.used
        self.used += 1
        copy = pltpu.make_async_remote_copy(
            src_ref=src,
            dst_ref=dst,
            send_sem=self.send.at[i],
            recv_sem=self.recv.at[i],
            device_id=target,
            device_id_type=MESH,
        )
        copy.start()
        self.open.append(copy)
        return copy

    def finish(self):
        for copy in self.open:
            copy.wait_send()
        self.open = []

    def settle(self, some):
        for copy in some:
            copy.wait_send()
        self.open = [copy for copy in self.open if not any(copy is done for done in some)]


def ring_begin(copies, pos, view, dev):
    right = copies.start(view(pos, None), view(pos, None), dev(wrap(pos, 1)))
    left = copies.start(view(pos, None), view(pos, None), dev(wrap(pos, 3)))
    return (right, left)


def ring_middle(copies, pos, view, dev, begun):
    right, left = begun
    right.wait_recv()
    on_right = copies.start(view(wrap(pos, 3), 0), view(wrap(pos, 3), 0), dev(wrap(pos, 1)))
    left.wait_recv()
    on_left = copies.start(view(wrap(pos, 1), 1), view(wrap(pos, 1), 1), dev(wrap(pos, 3)))
    return (on_right, on_left)


def ring_end(middle):
    for copy in middle:
        copy.wait_recv()


def direct_begin(copies, pos, view, dev):
    return [copies.start(view(pos), view(pos), dev(wrap(pos, d))) for d in (1, 3, 2)]


def pick(start, width, half):
    if half is None:
        return pl.ds(start, width)
    return pl.ds(start + half * (width // 2), width // 2)


def erf_gelu_slope(values):
    return (
        0.5 * (1.0 + lax.erf(values * 0.7071067811865476))
        + values * jnp.exp(-0.5 * values * values) * 0.3989422804014327
    )


def tanh_gelu_and_slope(values):
    square = values * values
    inner = 0.7978845608028654 * values * (1.0 + 0.044715 * square)
    tangent = jnp.tanh(inner)
    half = 0.5 * (1.0 + tangent)
    act = values * half
    slope = half + 0.5 * values * (1.0 - tangent * tangent) * 0.7978845608028654 * (
        1.0 + 3.0 * 0.044715 * square
    )
    return act, slope


def one_hot(left, right):
    return jnp.where(left == right, 1.0, 0.0).astype(BF)


def whole_kernel(
    x_ref, g_ref, gain_ref, pack_ref, pos_ref, feature_ref, unit_ref, dev_ref, vgain_ref,
    column_ref, rowline_ref, local_ref,
    wg_hbm, wu_hbm, wd_hbm, wp_hbm, w1_hbm, w2_hbm,
    embed_ref, proj_ref, fc1_ref, fc2_ref, fg_ref,
    xg, buf, wg, wu, wd, acc_g, acc_u, acc_h, gg, ug, rb, q,
    ra1, ra2, ra3, sa1, sa2, eall_ref,
    spread, wp, w1, w2, comp,
    vmine, vgot, vis, away, px, lnp, lnmine, lngot, unit4, vis4,
    wsem, send, recv,
):
    me = Place()
    c, t, x, y, k = me.c, me.t, me.x, me.y, me.k
    loads = [
        pltpu.make_async_copy(source, target, wsem.at[i])
        for i, (source, target) in enumerate(
            ((wg_hbm, wg), (wu_hbm, wu), (wd_hbm, wd), (wp_hbm, wp), (w1_hbm, w1), (w2_hbm, w2))
        )
    ]
    for load in loads:
        load.start()
    xg[c, 0] = x_ref[...].astype(F32)
    xg[c, 1] = g_ref[...].astype(F32)
    spread[y, x, c] = pack_ref[...]
    targets = [me.other()]
    targets += [me.at(z=wrap(t, d)) for d in (1, 2, 3)]
    targets += [me.at(x=wrap(x, d)) for d in (1, 2, 3)]
    targets += [me.at(y=wrap(y, d)) for d in (1, 2, 3)]
    greet(targets)
    copies = Copies(send, recv)
    swap = copies.start(xg.at[c], xg.at[c], me.other())

    def view0x(pos, half):
        return buf.at[c, y, pos, :, pick(0, 4096, half)]

    def view1y(pos, half):
        return buf.at[c, pos, x, :, pick(4096, 4096, half)]

    def dev_x(pos):
        return me.at(x=pos)

    def dev_y(pos):
        return me.at(y=pos)

    def spread0x(pos, half):
        return spread.at[y, pos, c, :, pick(0, 1280, half)]

    def spread1y(pos, half):
        return spread.at[pos, x, c, :, pick(1280, 1280, half)]

    def spread0y(pos, half):
        return spread.at[pos, :, c, :, pick(0, 1280, half)]

    def spread1x(pos, half):
        return spread.at[:, pos, c, :, pick(1280, 1280, half)]

    def cross(view):
        return copies.start(view, view, me.other())

    def begin(rings):
        return [ring_begin(copies, *ring) for ring in rings]

    def middle(rings, begun):
        return [ring_middle(copies, *ring, b) for ring, b in zip(rings, begun)]

    swap.wait_recv()
    rows = xg[:, 0]
    total = jnp.sum(rows * rows, axis=2, keepdims=True)
    root = jnp.sqrt(total / 8192.0 + 1e-06)

    def make_block(i, _):
        cols = pl.ds(pl.multiple_of(i * 1024, 1024), 1024)
        normed = xg[:, 0, :, cols] / root * gain_ref[:, cols][None]
        block = jnp.where(c == 0, normed, xg[:, 1, :, cols])
        buf[c, y, x, :, cols] = block.reshape(16, 1024).astype(BF)
        return 0

    lax.fori_loop(0, 8, make_block, 0)


    def along_y(block):
        return (y, lambda pos, half: buf.at[c, pos, block, :, pick(0, 4096, half)], dev_y)

    def along_x(block):
        return (x, lambda pos, half: buf.at[c, block, pos, :, pick(4096, 4096, half)], dev_x)

    seen1 = [(x, spread0x, dev_x), (y, spread1y, dev_y)]
    seen2 = [(y, spread0y, dev_y), (x, spread1x, dev_x)]
    crossed = []

    def cross_all(rings, steps):
        for pos, view, _ in rings:
            for d in steps:
                crossed.append(cross(view(wrap(pos, d), None)))

    main = [(x, view0x, dev_x), (y, view1y, dev_y)]
    onward = [[along_y(wrap(x, d)), along_x(wrap(y, d))] for d in range(4)]
    begun = begin(main)
    going = {0: begin(onward[0])}
    seen_begun = begin(seen1)
    cross_all(onward[0], (0,))
    mid = middle(main, begun)
    for d in (3, 1):
        going[d] = begin(onward[d])
        cross_all(onward[d], (0,))
    ends = middle(onward[0], going[0])
    cross_all(onward[0], (1, 3))
    for m in mid:
        ring_end(m)
    going[2] = begin(onward[2])
    cross_all(onward[2], (0,))
    for m in ends:
        ring_end(m)
    cross_all(onward[0], (2,))
    seen_mid = middle(seen1, seen_begun)
    last = []
    for d in (3, 1, 2):
        last.append((d, middle(onward[d], going[d])))
        cross_all(onward[d], (1, 3))
    for m in seen_mid:
        ring_end(m)
    sent, copies.open = copies.open, []
    seen_begun = begin(seen2)
    before = len(copies.open)
    for d, ends in last:
        for m in ends:
            ring_end(m)
        cross_all(onward[d], (2,))
    sent += copies.open[before:]
    copies.open = copies.open[:before]
    for load in loads[:3]:
        load.wait()
    for copy in crossed:
        copy.wait_recv()

    acc_g[...] = jnp.zeros_like(acc_g)
    acc_u[...] = jnp.zeros_like(acc_u)
    acc_h[...] = jnp.zeros_like(acc_h)

    def first(i, _):
        cols = pl.ds(pl.multiple_of(i * 1024, 1024), 1024)
        normed = buf[0, :, :, :, cols].reshape(256, 1024)
        acc_g[...] += nt(normed, wg[:, cols])
        acc_u[...] += nt(normed, wu[:, cols])
        grads = buf[1, :, :, :, cols].reshape(256, 1024)
        acc_h[...] += nt(grads, wd[:, cols])
        return 0

    lax.fori_loop(0, 8, first, 0)
    gate, up, hidden = acc_g[...], acc_u[...], acc_h[...]
    sig = jax.nn.sigmoid(gate)
    up_grad = (hidden * gate * sig).astype(BF)
    gate_grad = (hidden * up * sig * (1.0 + gate * (1.0 - sig))).astype(BF)
    gg[...] = gate_grad
    ug[...] = up_grad
    inner = jnp.sum(
        gate_grad.astype(F32) * gate + up_grad.astype(F32) * up, axis=1, keepdims=True
    )
    inner = jnp.broadcast_to(inner, (256, 128)).reshape(4, 4, 16, 128)

    def part(base, i):
        cols = pl.ds(pl.multiple_of(base + i * 256, 256), 256)
        value = nn(gg[...], wg[:, cols]) + nn(ug[...], wu[:, cols])
        return value.reshape(4, 4, 16, 256)

    seen_crossed = [cross(view(pos, None)) for pos, view, _ in seen2]
    seen_mid = middle(seen2, seen_begun)
    for pos, view, _ in seen2:
        seen_crossed.append(cross(view(wrap(pos, 1), None)))
        seen_crossed.append(cross(view(wrap(pos, 3), None)))
    for copy in sent:
        copy.wait_send()
    halves = []
    for step in range(4):
        to = wrap(t, step + 1)

        def give(i, _):
            cols = pl.ds(pl.multiple_of(to * 1152 + i * 256, 128), 256)
            buf[0, :, :, :, cols] = part(to * 2048 + (1 - c) * 1024, i).astype(BF)
            return 0

        lax.fori_loop(0, 4, give, 0)
        buf[0, :, :, :, pl.ds(pl.multiple_of(to * 1152 + 1024, 128), 128)] = inner.astype(BF)
        sent = buf.at[0, :, :, :, pl.ds(pl.multiple_of(to * 1152, 128), 1152)]
        halves.append(copies.start(sent, rb.at[to], me.other()))

    cuts = (pl.ds(0, 384), pl.ds(384, 384), pl.ds(768, 384))
    stage1 = []
    for step in range(4):
        to = wrap(t, step + 1)
        halves[step].wait_recv()

        def keep(i, _):
            cols = pl.ds(pl.multiple_of(i * 256, 256), 256)
            mine = part(to * 2048 + c * 1024, i)
            q[to, :, :, :, cols] = (mine + rb[to, :, :, :, cols].astype(F32)).astype(BF)
            return 0

        lax.fori_loop(0, 4, keep, 0)
        q[to, :, :, :, 1024:1152] = (inner + rb[to, :, :, :, 1024:1152].astype(F32)).astype(BF)
        if step < 3:
            stage1.append(
                copies.start(q.at[to, :, :, :, cuts[0]], ra1.at[0, step], me.at(z=to))
            )
    for d in (1, 2, 3):
        to = wrap(y, d)
        stage1.append(copies.start(q.at[:, to, :, :, cuts[1]], ra1.at[1, d - 1], me.at(y=to)))
        to = wrap(x, d)
        stage1.append(copies.start(q.at[:, :, to, :, cuts[2]], ra1.at[2, d - 1], me.at(x=to)))
    own1 = (
        lambda: q[t, :, :, :, cuts[0]],
        lambda: q[:, y, :, :, cuts[1]],
        lambda: q[:, :, x, :, cuts[2]],
    )
    for m in seen_mid:
        ring_end(m)
    for pos, view, _ in seen2:
        seen_crossed.append(cross(view(wrap(pos, 2), None)))
    for copy in seen_crossed:
        copy.wait_recv()
    copies.settle([copy for pair in seen_begun + seen_mid for copy in pair] + seen_crossed)

    counts = spread[:, :, :, 0:16, 2432:2560].reshape(32, 16, 128).astype(F32)[:, 0, :]
    frame_of, quarter_of, slot_of = column_ref[0:1, :], column_ref[1:2, :], column_ref[2:3, :]
    frames = lax.broadcasted_iota(jnp.int32, (32, 1536), 0)
    wide = jnp.broadcast_to(counts[:, :1], (32, 1536))
    offset = jnp.sum(jnp.where(frames < frame_of, wide, 0.0), axis=0, keepdims=True)
    count = jnp.sum(jnp.where(frames == frame_of, wide, 0.0), axis=0, keepdims=True)
    code = (offset.astype(jnp.int32) + slot_of) * 4 + quarter_of
    code = jnp.where(slot_of < count.astype(jnp.int32), code, -1)
    for i in range(3):
        chosen = one_hot(pos_ref[i * 256 : (i + 1) * 256, 1:2], code)
        buf[1, :, :, :, i * 1536 : (i + 1) * 1536] = chosen.reshape(4, 4, 16, 1536)
    lanes = lax.broadcasted_iota(jnp.int32, (32, 128), 0)
    own_offset = jnp.sum(jnp.where(lanes < me.frame, counts, 0.0), axis=0, keepdims=True)
    own_count = jnp.sum(jnp.where(lanes == me.frame, counts, 0.0), axis=0, keepdims=True)
    own_offset = own_offset.astype(jnp.int32)[:, :1]
    own_count = own_count.astype(jnp.int32)[:, :1]
    local_slot, local_quarter = local_ref[:, 0:1], local_ref[:, 1:2]
    own_code = (own_offset + local_slot) * 4 + local_quarter
    own_code = jnp.where(local_slot < own_count, own_code, -1)
    here = one_hot(own_code, rowline_ref[...])

    def compact(i, _):
        cols = pl.ds(pl.multiple_of(i * 256, 256), 256)
        block = spread[:, :, :, :, cols].reshape(1536, 256)
        for j in range(3):
            hot = buf[1, :, :, :, j * 1536 : (j + 1) * 1536].reshape(256, 1536)
            comp[j * 256 : (j + 1) * 256, cols] = nn(hot, block).astype(BF)
        return 0

    lax.fori_loop(0, 10, compact, 0)
    base = c * 1024
    loads[3].wait()

    def first(i, _):
        rows = pl.ds(pl.multiple_of((i // 4) * 192, 48), 192)
        pair = pl.ds(pl.multiple_of(lax.rem(i // 4, 2) * 2, 2), 2)
        cols = pl.multiple_of(lax.rem(i, 4) * 256, 256)
        pre = nn(comp[rows, 0:1152], wp[:, pl.ds(base + cols, 256)])
        weight = comp[rows, 2304:2305].astype(F32)
        tilt = (erf_gelu_slope(pre) * weight).astype(BF)
        spread[i // 8, pair, :, :, pl.ds(1152 + cols, 256)] = tilt.reshape(2, 2, 48, 256)
        return 0

    stage2 = []
    for p in range(3):
        arrived = stage1[:3] if p == 0 else stage1[2 + p :: 2]
        for copy in arrived:
            copy.wait_recv()
        value = own1[p]().astype(F32)
        for d in range(3):
            value = value + ra1[p, d].astype(F32)
        sa1[p] = value.astype(BF)
        for d in (1, 2, 3):
            if p == 0:
                to = wrap(y, d)
                stage2.append(copies.start(sa1.at[0, to], ra2.at[0, d - 1], me.at(y=to)))
            elif p == 1:
                to = wrap(x, d)
                stage2.append(copies.start(sa1.at[1, :, to], ra2.at[1, d - 1], me.at(x=to)))
            else:
                to = wrap(t, d)
                stage2.append(copies.start(sa1.at[2, to], ra2.at[2, d - 1], me.at(z=to)))
    lax.fori_loop(0, 5, first, 0)
    own2 = (lambda: sa1[0, y], lambda: sa1[1, :, x], lambda: sa1[2, t])
    stage3 = []
    for p in range(3):
        for copy in stage2[3 * p : 3 * p + 3]:
            copy.wait_recv()
        value = own2[p]().astype(F32)
        for d in range(3):
            value = value + ra2[p, d].astype(F32)
        sa2[p] = value.astype(BF)
        for d in (1, 2, 3):
            if p == 0:
                to = wrap(x, d)
                stage3.append(copies.start(sa2.at[0, to], ra3.at[0, d - 1], me.at(x=to)))
            elif p == 1:
                to = wrap(t, d)
                stage3.append(copies.start(sa2.at[1, to], ra3.at[1, d - 1], me.at(z=to)))
            else:
                to = wrap(y, d)
                stage3.append(copies.start(sa2.at[2, to], ra3.at[2, d - 1], me.at(y=to)))
    lax.fori_loop(5, 10, first, 0)
    own3 = (lambda: sa2[0, x], lambda: sa2[1, t], lambda: sa2[2, y])
    pieces = []
    for p in range(3):
        for copy in stage3[3 * p : 3 * p + 3]:
            copy.wait_recv()
        value = own3[p]().astype(F32)
        for d in range(3):
            value = value + ra3[p, d].astype(F32)
        pieces.append(value)
    root16 = root.reshape(16, 1)
    mean = pieces[2][:, 256:257] / 8192.0
    for p in range(3):
        width = 384 if p < 2 else 256
        cols = pl.ds(pl.multiple_of(t * 2048 + c * 1024 + p * 384, 128), width)
        unit = xg[:, 0, :, cols].reshape(16, width) / root16
        scaled = pieces[p][:, :width] * gain_ref[:, cols]
        out = xg[:, 1, :, cols].reshape(16, width) + (scaled - unit * mean) / root16
        eall_ref[y, x, :, pl.ds(pl.multiple_of(c * 1024 + p * 384, 128), width)] = out.astype(BF)


    def embed0x(pos):
        return eall_ref.at[y, pos, :, pl.ds(base, 512)]

    def embed1y(pos):
        return eall_ref.at[pos, x, :, pl.ds(base + 512, 512)]

    def embed0y(pos):
        return eall_ref.at[pos, :, :, pl.ds(base, 512)]

    def embed1x(pos):
        return eall_ref.at[:, pos, :, pl.ds(base + 512, 512)]

    begun = [direct_begin(copies, x, embed0x, dev_x), direct_begin(copies, y, embed1y, dev_y)]
    lax.fori_loop(10, 16, first, 0)
    for b in begun:
        for copy in b:
            copy.wait_recv()
    copies.finish()
    begun = [direct_begin(copies, y, embed0y, dev_y), direct_begin(copies, x, embed1x, dev_x)]
    crossed = [cross(embed0y(y)), cross(embed1x(x))]
    loads[4].wait()

    def second(i, _):
        rows = pl.ds(pl.multiple_of(i * 96, 96), 96)
        act, tilt = tanh_gelu_and_slope(nt(comp[rows, 1152:2304], w1[...]))
        at = (2 + i // 4, lax.rem(i, 4))
        spread[at[0], at[1], :, :, 0:1076] = act.astype(BF).reshape(2, 48, 1076)
        spread[at[0], at[1], :, :, 1152:2228] = tilt.astype(BF).reshape(2, 48, 1076)
        return 0

    lax.fori_loop(0, 8, second, 0)
    for b, view, pos in ((begun[0], embed0y, y), (begun[1], embed1x, x)):
        for copy, d in zip(b, (3, 1, 2)):
            copy.wait_recv()
            crossed.append(cross(view(wrap(pos, d))))

    mine = pl.ds(pl.multiple_of(k * 48, 48), 48)
    pre = nn(comp[mine, 0:1152], wp[...])
    tilt = erf_gelu_slope(pre) * comp[mine, 2304:2305].astype(F32)
    for copy in crossed:
        copy.wait_recv()
    places = lax.broadcasted_iota(jnp.int32, (48, 256), 1)
    kept = nn(one_hot(pos_ref[mine, 0:1], places), eall_ref[...].reshape(256, 2048))
    act48 = (kept * tilt).astype(BF)
    part48 = nt(act48, wp[pl.ds(pl.multiple_of(c * 512, 512), 640), :])
    vmine[...] = part48.astype(BF)
    begun = [copies.start(vmine, vgot.at[d - 1], me.at(z=wrap(t, d))) for d in (1, 3, 2)]
    both = eall_ref[y, x].astype(F32)
    embed_ref[...] = jnp.where(c == 0, both[:8], both[8:]).astype(BF)
    places = lax.broadcasted_iota(jnp.int32, (192, 256), 1)

    def third(i, _):
        rows = pl.ds(pl.multiple_of(i * 192, 192), 192)
        kept = nn(
            one_hot(pos_ref[rows, 0:1], places),
            eall_ref[:, :, :, pl.ds(pl.multiple_of(base, 1024), 1024)].reshape(256, 1024),
        )
        pair = pl.ds(pl.multiple_of(lax.rem(i, 2) * 2, 2), 2)
        tilt = spread[i // 2, pair, :, :, 1152:2176].reshape(192, 1024).astype(F32)
        spread[i // 2, pair, :, :, 1152:2176] = (kept * tilt).astype(BF).reshape(2, 2, 48, 1024)
        return 0

    value = part48
    for copy in begun:
        copy.wait_recv()
    for d in range(3):
        value = value + vgot[d].astype(F32)
    vis[c, y, x] = value.astype(BF)

    def e0x(pos):
        return vis.at[c, y, pos, :, pl.ds(0, 384)]

    def e1y(pos):
        return vis.at[c, pos, x, :, pl.ds(384, 256)]

    def e0y(pos):
        return vis.at[c, pos, :, :, pl.ds(0, 384)]

    def e1x(pos):
        return vis.at[c, :, pos, :, pl.ds(384, 256)]

    begun = [direct_begin(copies, x, e0x, dev_x), direct_begin(copies, y, e1y, dev_y)]
    lax.fori_loop(0, 4, third, 0)
    for b in begun:
        for copy in b:
            copy.wait_recv()
    begun = [direct_begin(copies, y, e0y, dev_y), direct_begin(copies, x, e1x, dev_x)]
    crossed = [cross(e0y(y)), cross(e1x(x))]

    source = lax.broadcasted_iota(jnp.int32, (1152, 128), 0)
    lane = lax.broadcasted_iota(jnp.int32, (1152, 128), 1)
    block = me.frame * 36
    other = (me.frame + 1 - 2 * c) * 36
    want = jnp.where(lane < 64, jnp.where(lane < 36, block + lane, -1),
                     jnp.where(lane < 100, other + lane - 64, -1))
    chosen = one_hot(source, want)
    out_cols = nn(comp[:, 0:1152], chosen).astype(BF)
    proj = tn(out_cols, spread[0:2, :, :, :, 1152:2176].reshape(768, 1024))
    away[...] = proj[64:104]
    px_copy = copies.start(away, px, me.other())
    proj_ref[:, pl.ds(pl.multiple_of(base, 1024), 1024)] = proj[0:36]
    ln_cols = nn(comp[:, 1152:2304], chosen).astype(BF)

    for b, view, pos in ((begun[0], e0y, y), (begun[1], e1x, x)):
        for copy, d in zip(b, (3, 1, 2)):
            copy.wait_recv()
            crossed.append(copies.start(view(wrap(pos, d)), view(wrap(pos, d)), me.other()))
    px_copy.wait_recv()
    proj_ref[:, pl.ds(pl.multiple_of(1024 - base, 1024), 1024)] = px[0:36]
    for copy in crossed:
        copy.wait_recv()

    loads[5].wait()

    def fourth(i, _):
        low = vis[0, i].reshape(192, 640)
        high = vis[1, i].reshape(192, 640)[:, 128:]
        back = nt(low, w2[:, 0:640]) + nt(high, w2[:, 640:1152])
        pair = pl.ds(pl.multiple_of(lax.rem(i, 2) * 2, 2), 2)
        tilt = spread[2 + i // 2, pair, :, :, 1152:2228].reshape(192, 1076).astype(F32)
        spread[i // 2, pair, :, :, 0:1076] = (back * tilt).astype(BF).reshape(2, 2, 48, 1076)
        return 0

    lax.fori_loop(0, 4, fourth, 0)
    fgrad = spread[0:2, :, :, :, 0:1076].reshape(768, 1076)
    here_grad = nn(here, fgrad).astype(BF)
    ln_part = nn(here_grad, w1[...]) * vgain_ref[...]
    sums = jnp.sum(ln_part, axis=1, keepdims=True)
    dots = jnp.sum(ln_part * unit_ref[...], axis=1, keepdims=True)
    lane = lax.broadcasted_iota(jnp.int32, (48, 96), 1)
    extra = jnp.where(lane == 0, sums, jnp.where(lane == 1, dots, 0.0))
    for i in range(4):
        lnp[i, :, 0:288] = ln_part[:, i * 288 : (i + 1) * 288]
        lnp[i, :, 288:384] = extra
    lnmine[...] = lnp[...].astype(BF)
    vis0 = vis[0].reshape(768, 640)
    vis1 = vis[1].reshape(768, 640)[:, 128:]
    begun = [
        copies.start(lnmine.at[wrap(t, d)], lngot.at[d - 1], me.at(z=wrap(t, d))) for d in (1, 3, 2)
    ]
    fc1_ref[...] = tn(ln_cols, fgrad)[0:36]
    vis_cols = (nn(vis0, chosen[0:640]) + nn(vis1, chosen[640:1152])).astype(BF)
    fc2_ref[...] = tn(vis_cols, spread[2:4, :, :, :, 0:1076].reshape(768, 1076))[0:36]
    vis_here = jnp.concatenate([nn(here, vis0), nn(here, vis1)], axis=1)
    for i in range(4):
        vis4[i] = vis_here[:, i * 288 : (i + 1) * 288]
        unit4[i] = unit_ref[:, i * 288 : (i + 1) * 288]
    for copy in begun:
        copy.wait_recv()
    value = lnp[t]
    for d in range(3):
        value = value + lngot[d].astype(F32)
    mean, slant = value[:, 288:289] / 1152.0, value[:, 289:290] / 1152.0
    result = vis4[t] + (value[:, 0:288] - mean - unit4[t] * slant) / dev_ref[...]
    cells = lax.broadcasted_iota(jnp.int32, (48, 729), 1)
    spot = one_hot(feature_ref[...], cells)
    fg_ref[...] = tn(result.astype(BF), spot).astype(BF)
    copies.finish()


def column_codes():
    column = np.arange(1536)
    code = np.zeros((8, 1536), np.int32)
    code[0], code[1], code[2] = column // 48, column % 48 // 12, column % 12
    return code


def row_codes():
    row = np.arange(768)
    return (row // 48 * 12 + row % 12) * 4 + row % 48 // 12


def local_codes():
    row = np.arange(48)
    return np.stack([row % 12, row // 12], axis=1).astype(np.int32)


def copy_kernel(*refs):
    count = (len(refs) - 2) // 3
    into = [
        pltpu.make_async_copy(refs[i], refs[2 * count + i], refs[-2].at[i]) for i in range(count)
    ]
    away = [
        pltpu.make_async_copy(refs[2 * count + i], refs[count + i], refs[-1].at[i])
        for i in range(count)
    ]
    for copy in into:
        copy.start()
    for first, second in zip(into, away):
        first.wait()
        second.start()
    for copy in away:
        copy.wait()


def hand_over(arrays):
    return pl.pallas_call(
        copy_kernel,
        name="hand_over",
        out_shape=tuple(jax.ShapeDtypeStruct(a.shape, a.dtype) for a in arrays),
        in_specs=[ANY] * len(arrays),
        out_specs=(ANY,) * len(arrays),
        scratch_shapes=[pltpu.VMEM(a.shape, a.dtype) for a in arrays]
        + [pltpu.SemaphoreType.DMA((len(arrays),))] * 2,
    )(*arrays)


def whole(llm_input, out_grad, llm_gain, packed, seq_order, feature, unit_in, deviation, vis_gain,
          w_gate, w_up, w_down, w_proj, w_fc1, w_fc2):
    codes = row_codes().astype(np.int32)
    position = jnp.broadcast_to(seq_order[:192].reshape(16, 1, 12), (16, 4, 12)).reshape(768, 1)
    position = jnp.concatenate([position, jnp.asarray(codes.reshape(-1, 1))], axis=1)
    w_gate, w_up, w_fc1 = w_gate.T, w_up.T, w_fc1.T
    units = w_gate.shape[0]
    hidden = w_fc2.shape[0]
    sems = 200
    part = (3, 3)
    return pl.pallas_call(
        whole_kernel,
        name="whole",
        out_shape=(
            jax.ShapeDtypeStruct((8, 2048), BF),
            jax.ShapeDtypeStruct((36, 2048), F32),
            jax.ShapeDtypeStruct((36, hidden), F32),
            jax.ShapeDtypeStruct((36, hidden), F32),
            jax.ShapeDtypeStruct((288, 729), BF),
        ),
        in_specs=[VM] * 12 + [ANY] * 6,
        out_specs=(VM,) * 5,
        scratch_shapes=[
            pltpu.VMEM((2, 2, 8, 8192), F32),
            pltpu.VMEM((2, 4, 4, 16, 8192), BF),
            pltpu.VMEM(w_gate.shape, BF),
            pltpu.VMEM(w_up.shape, BF),
            pltpu.VMEM(w_down.shape, BF),
            pltpu.VMEM((256, units), F32),
            pltpu.VMEM((256, units), F32),
            pltpu.VMEM((256, units), F32),
            pltpu.VMEM((256, units), BF),
            pltpu.VMEM((256, units), BF),
            pltpu.VMEM((4, 4, 4, 16, 1152), BF),
            pltpu.VMEM((4, 4, 4, 16, 1152), BF),
            pltpu.VMEM(part + (4, 4, 16, 384), BF),
            pltpu.VMEM(part + (4, 16, 384), BF),
            pltpu.VMEM(part + (16, 384), BF),
            pltpu.VMEM((3, 4, 4, 16, 384), BF),
            pltpu.VMEM((3, 4, 16, 384), BF),
            pltpu.VMEM((4, 4, 16, 2048), BF),
            pltpu.VMEM((4, 4, 2, 48, 2560), BF),
            pltpu.VMEM(w_proj.shape, BF),
            pltpu.VMEM(w_fc1.shape, BF),
            pltpu.VMEM(w_fc2.shape, BF),
            pltpu.VMEM((768, 2560), BF),
            pltpu.VMEM((48, 640), BF),
            pltpu.VMEM((3, 48, 640), BF),
            pltpu.VMEM((2, 4, 4, 48, 640), BF),
            pltpu.VMEM((40, 1024), F32),
            pltpu.VMEM((40, 1024), F32),
            pltpu.VMEM((4, 48, 384), F32),
            pltpu.VMEM((4, 48, 384), BF),
            pltpu.VMEM((3, 48, 384), BF),
            pltpu.VMEM((4, 48, 288), F32),
            pltpu.VMEM((4, 48, 288), F32),
            pltpu.SemaphoreType.DMA((6,)),
            pltpu.SemaphoreType.DMA((sems,)),
            pltpu.SemaphoreType.DMA((sems,)),
        ],
        compiler_params=pltpu.CompilerParams(
            collective_id=0, has_side_effects=True, vmem_limit_bytes=63 * 1024 * 1024
        ),
    )(
        llm_input, out_grad, llm_gain.reshape(1, -1), packed, position, feature, unit_in, deviation,
        vis_gain, jnp.asarray(column_codes()),
        jnp.asarray(codes.reshape(1, -1)), jnp.asarray(local_codes()),
        w_gate, w_up, w_down, w_proj, w_fc1, w_fc2,
    )


def touched_rows(keep_row, live_count, grid):
    width = (grid + 1) // 2
    slots = jnp.arange(keep_row.shape[0], dtype=jnp.int32)[None, :]
    quarter = jnp.arange(4, dtype=jnp.int32)[:, None]
    pool_row = (keep_row // width)[None, :]
    pool_col = (keep_row % width)[None, :]
    grid_row = 2 * pool_row + quarter // 2
    grid_col = 2 * pool_col + quarter % 2
    inside = (grid_row < grid) & (grid_col < grid) & (slots < live_count)
    row_cells = jnp.where(2 * pool_row + 1 < grid, 2.0, 1.0)
    col_cells = jnp.where(2 * pool_col + 1 < grid, 2.0, 1.0)
    weight = jnp.where(inside, 1.0 / (row_cells * col_cells), 0.0).astype(F32)
    feature = jnp.where(inside, grid_row * grid + grid_col, 0)
    return feature.reshape(-1), weight.reshape(-1)


def shards(
    llm_input,
    out_grad,
    llm_gain,
    w_gate,
    w_up,
    w_down,
    keep_index,
    keep_count,
    seq_order,
    vision_in,
    vision_out,
    vis_gain,
    w_proj,
    w_fc1,
    w_fc2,
):
    cells = vision_in.shape[0]
    feature, weight = touched_rows(keep_index[0], keep_count[0], GRID)
    spot = (feature[:, None] == jnp.arange(cells, dtype=jnp.int32)[None, :]).astype(BF)
    rows_out = nn(spot, vision_out).astype(BF)
    rows_in = nn(spot, vision_in)
    center = jnp.mean(rows_in, axis=1, keepdims=True)
    variance = jnp.mean((rows_in - center) * (rows_in - center), axis=1, keepdims=True)
    deviation = jnp.sqrt(variance + 1e-06)
    unit_in = (rows_in - center) / deviation
    ln_out = (unit_in * vis_gain).astype(BF)
    extra = jnp.concatenate(
        [
            jnp.broadcast_to(weight[:, None], (48, 128)),
            jnp.broadcast_to(keep_count.astype(F32)[None, :], (48, 128)),
        ],
        axis=1,
    ).astype(BF)
    packed = jnp.concatenate([rows_out, ln_out, extra], axis=1)
    results = whole(
        llm_input, out_grad, llm_gain, packed, seq_order, feature.reshape(48, 1), unit_in, deviation,
        vis_gain.reshape(1, -1), w_gate, w_up, w_down, w_proj, w_fc1, w_fc2,
    )
    embed, proj_grad, fc1_grad, fc2_grad, feature_grad = hand_over(results)
    return (embed, proj_grad, fc1_grad, fc2_grad.T, feature_grad.T)


def solution(mesh):
    in_specs = (
        P("frame", None),
        P("frame", None),
        P(),
        P(None, ("frame", "tensor")),
        P(None, ("frame", "tensor")),
        P(("frame", "tensor"), None),
        P("frame", None),
        P("frame"),
        P(),
        P("frame", None),
        P("frame", None),
        P(),
        P(None, "tensor"),
        P(None, "tensor"),
        P("tensor", None),
    )
    out_specs = (
        P("frame", "tensor"),
        P("frame", "tensor"),
        P("frame", "tensor"),
        P("tensor", "frame"),
        P("frame", "tensor"),
    )
    return jax.shard_map(shards, mesh=mesh, in_specs=in_specs, out_specs=out_specs, check_vma=False)
```

```python
import functools

import jax
import jax.numpy as jnp
import numpy as np
from jax import lax
from jax.experimental import pallas as pl
from jax.experimental.pallas import tpu as pltpu
from jax.sharding import PartitionSpec as P

GRID = 27
BF = jnp.bfloat16
F32 = jnp.float32
MESH = pl.DeviceIdType.MESH
ANY = pl.BlockSpec(memory_space=pl.ANY)
VM = pl.BlockSpec(memory_space=pltpu.VMEM)


def nt(left, right):
    return lax.dot_general(left, right, (((1,), (1,)), ((), ())), preferred_element_type=F32)


def tn(left, right):
    return lax.dot_general(left, right, (((0,), (0,)), ((), ())), preferred_element_type=F32)


def nn(left, right):
    return jnp.dot(left, right, preferred_element_type=F32)


class Place:
    def __init__(self):
        frame = lax.axis_index("frame")
        self.frame = frame
        self.t = lax.axis_index("tensor")
        self.c = lax.rem(frame, 2)
        self.k = frame // 2
        self.x = lax.rem(self.k, 4)
        self.y = self.k // 4

    def at(self, y=None, x=None, z=None, core=None):
        y = self.y if y is None else y
        x = self.x if x is None else x
        z = self.t if z is None else z
        core = self.c if core is None else core
        return ((y * 4 + x) * 2 + core, z)

    def other(self):
        return self.at(core=1 - self.c)


def greet(targets):
    barrier = pltpu.get_barrier_semaphore()
    for target in targets:
        pl.semaphore_signal(barrier, inc=1, device_id=target, device_id_type=MESH)
    pl.semaphore_wait(barrier, len(targets))


def wrap(pos, d):
    return lax.rem(pos + d, 4)


class Copies:
    def __init__(self, send, recv):
        self.send, self.recv, self.used, self.open = send, recv, 0, []

    def start(self, src, dst, target):
        i = self.used
        self.used += 1
        copy = pltpu.make_async_remote_copy(
            src_ref=src,
            dst_ref=dst,
            send_sem=self.send.at[i],
            recv_sem=self.recv.at[i],
            device_id=target,
            device_id_type=MESH,
        )
        copy.start()
        self.open.append(copy)
        return copy

    def finish(self):
        for copy in self.open:
            copy.wait_send()
        self.open = []

    def settle(self, some):
        for copy in some:
            copy.wait_send()
        self.open = [copy for copy in self.open if not any(copy is done for done in some)]


def ring_begin(copies, pos, view, dev):
    right = copies.start(view(pos, None), view(pos, None), dev(wrap(pos, 1)))
    left = copies.start(view(pos, None), view(pos, None), dev(wrap(pos, 3)))
    return (right, left)


def ring_middle(copies, pos, view, dev, begun):
    right, left = begun
    right.wait_recv()
    on_right = copies.start(view(wrap(pos, 3), 0), view(wrap(pos, 3), 0), dev(wrap(pos, 1)))
    left.wait_recv()
    on_left = copies.start(view(wrap(pos, 1), 1), view(wrap(pos, 1), 1), dev(wrap(pos, 3)))
    return (on_right, on_left)


def ring_end(middle):
    for copy in middle:
        copy.wait_recv()


def direct_begin(copies, pos, view, dev):
    return [copies.start(view(pos), view(pos), dev(wrap(pos, d))) for d in (1, 3, 2)]


def pick(start, width, half):
    if half is None:
        return pl.ds(start, width)
    return pl.ds(start + half * (width // 2), width // 2)


def erf_gelu_slope(values):
    return (
        0.5 * (1.0 + lax.erf(values * 0.7071067811865476))
        + values * jnp.exp(-0.5 * values * values) * 0.3989422804014327
    )


def tanh_gelu_and_slope(values):
    square = values * values
    inner = 0.7978845608028654 * values * (1.0 + 0.044715 * square)
    tangent = jnp.tanh(inner)
    half = 0.5 * (1.0 + tangent)
    act = values * half
    slope = half + 0.5 * values * (1.0 - tangent * tangent) * 0.7978845608028654 * (
        1.0 + 3.0 * 0.044715 * square
    )
    return act, slope


def one_hot(left, right):
    return jnp.where(left == right, 1.0, 0.0).astype(BF)


def whole_kernel(
    x_ref, g_ref, gain_ref, pack_ref, pos_ref, feature_ref, unit_ref, dev_ref, vgain_ref,
    column_ref, rowline_ref, local_ref,
    wg_hbm, wu_hbm, wd_hbm, wp_hbm, w1_hbm, w2_hbm,
    embed_ref, proj_ref, fc1_ref, fc2_ref, fg_ref,
    xg, buf, wg, wu, wd, acc_g, acc_u, acc_h, gg, ug, rb, q,
    ra1, ra2, ra3, sa1, sa2, eall_ref,
    spread, wp, w1, w2, comp,
    vmine, vgot, vis, away, px, lnp, lnmine, lngot, unit4, vis4,
    wsem, send, recv,
):
    me = Place()
    c, t, x, y, k = me.c, me.t, me.x, me.y, me.k
    loads = [
        pltpu.make_async_copy(source, target, wsem.at[i])
        for i, (source, target) in enumerate(
            ((wg_hbm, wg), (wu_hbm, wu), (wd_hbm, wd), (wp_hbm, wp), (w1_hbm, w1), (w2_hbm, w2))
        )
    ]
    for load in loads:
        load.start()
    xg[c, 0] = x_ref[...].astype(F32)
    xg[c, 1] = g_ref[...].astype(F32)
    spread[y, x, c] = pack_ref[...]
    targets = [me.other()]
    targets += [me.at(z=wrap(t, d)) for d in (1, 2, 3)]
    targets += [me.at(x=wrap(x, d)) for d in (1, 2, 3)]
    targets += [me.at(y=wrap(y, d)) for d in (1, 2, 3)]
    greet(targets)
    copies = Copies(send, recv)
    swap = copies.start(xg.at[c], xg.at[c], me.other())

    def view0x(pos, half):
        return buf.at[c, y, pos, :, pick(0, 4096, half)]

    def view1y(pos, half):
        return buf.at[c, pos, x, :, pick(4096, 4096, half)]

    def dev_x(pos):
        return me.at(x=pos)

    def dev_y(pos):
        return me.at(y=pos)

    def spread0x(pos, half):
        return spread.at[y, pos, c, :, pick(0, 1280, half)]

    def spread1y(pos, half):
        return spread.at[pos, x, c, :, pick(1280, 1280, half)]

    def spread0y(pos, half):
        return spread.at[pos, :, c, :, pick(0, 1280, half)]

    def spread1x(pos, half):
        return spread.at[:, pos, c, :, pick(1280, 1280, half)]

    def cross(view):
        return copies.start(view, view, me.other())

    def begin(rings):
        return [ring_begin(copies, *ring) for ring in rings]

    def middle(rings, begun):
        return [ring_middle(copies, *ring, b) for ring, b in zip(rings, begun)]

    swap.wait_recv()
    rows = xg[:, 0]
    total = jnp.sum(rows * rows, axis=2, keepdims=True)
    root = jnp.sqrt(total / 8192.0 + 1e-06)

    def make_block(i, _):
        cols = pl.ds(pl.multiple_of(i * 1024, 1024), 1024)
        normed = xg[:, 0, :, cols] / root * gain_ref[:, cols][None]
        block = jnp.where(c == 0, normed, xg[:, 1, :, cols])
        buf[c, y, x, :, cols] = block.reshape(16, 1024).astype(BF)
        return 0

    lax.fori_loop(0, 8, make_block, 0)


    def along_y(block):
        return (y, lambda pos, half: buf.at[c, pos, block, :, pick(0, 4096, half)], dev_y)

    def along_x(block):
        return (x, lambda pos, half: buf.at[c, block, pos, :, pick(4096, 4096, half)], dev_x)

    seen1 = [(x, spread0x, dev_x), (y, spread1y, dev_y)]
    seen2 = [(y, spread0y, dev_y), (x, spread1x, dev_x)]
    crossed = []

    def cross_all(rings, steps):
        for pos, view, _ in rings:
            for d in steps:
                crossed.append(cross(view(wrap(pos, d), None)))

    main = [(x, view0x, dev_x), (y, view1y, dev_y)]
    onward = [[along_y(wrap(x, d)), along_x(wrap(y, d))] for d in range(4)]
    begun = begin(main)
    going = {0: begin(onward[0])}
    seen_begun = begin(seen1)
    cross_all(onward[0], (0,))
    mid = middle(main, begun)
    for d in (3, 1):
        going[d] = begin(onward[d])
        cross_all(onward[d], (0,))
    ends = middle(onward[0], going[0])
    cross_all(onward[0], (1, 3))
    for m in mid:
        ring_end(m)
    going[2] = begin(onward[2])
    cross_all(onward[2], (0,))
    for m in ends:
        ring_end(m)
    cross_all(onward[0], (2,))
    seen_mid = middle(seen1, seen_begun)
    last = []
    for d in (3, 1, 2):
        last.append((d, middle(onward[d], going[d])))
        cross_all(onward[d], (1, 3))
    for m in seen_mid:
        ring_end(m)
    sent, copies.open = copies.open, []
    seen_begun = begin(seen2)
    before = len(copies.open)
    for d, ends in last:
        for m in ends:
            ring_end(m)
        cross_all(onward[d], (2,))
    sent += copies.open[before:]
    copies.open = copies.open[:before]
    for load in loads[:3]:
        load.wait()
    for copy in crossed:
        copy.wait_recv()

    acc_g[...] = jnp.zeros_like(acc_g)
    acc_u[...] = jnp.zeros_like(acc_u)
    acc_h[...] = jnp.zeros_like(acc_h)

    def first(i, _):
        cols = pl.ds(pl.multiple_of(i * 1024, 1024), 1024)
        normed = buf[0, :, :, :, cols].reshape(256, 1024)
        acc_g[...] += nt(normed, wg[:, cols])
        acc_u[...] += nt(normed, wu[:, cols])
        grads = buf[1, :, :, :, cols].reshape(256, 1024)
        acc_h[...] += nt(grads, wd[:, cols])
        return 0

    lax.fori_loop(0, 8, first, 0)
    gate, up, hidden = acc_g[...], acc_u[...], acc_h[...]
    sig = jax.nn.sigmoid(gate)
    up_grad = (hidden * gate * sig).astype(BF)
    gate_grad = (hidden * up * sig * (1.0 + gate * (1.0 - sig))).astype(BF)
    gg[...] = gate_grad
    ug[...] = up_grad
    inner = jnp.sum(
        gate_grad.astype(F32) * gate + up_grad.astype(F32) * up, axis=1, keepdims=True
    )
    inner = jnp.broadcast_to(inner, (256, 128)).reshape(4, 4, 16, 128)

    def part(base, i):
        cols = pl.ds(pl.multiple_of(base + i * 256, 256), 256)
        value = nn(gg[...], wg[:, cols]) + nn(ug[...], wu[:, cols])
        return value.reshape(4, 4, 16, 256)

    seen_crossed = [cross(view(pos, None)) for pos, view, _ in seen2]
    seen_mid = middle(seen2, seen_begun)
    for pos, view, _ in seen2:
        seen_crossed.append(cross(view(wrap(pos, 1), None)))
        seen_crossed.append(cross(view(wrap(pos, 3), None)))
    for copy in sent:
        copy.wait_send()
    halves = []
    for step in range(4):
        to = wrap(t, step + 1)

        def give(i, _):
            cols = pl.ds(pl.multiple_of(to * 1152 + i * 256, 128), 256)
            buf[0, :, :, :, cols] = part(to * 2048 + (1 - c) * 1024, i).astype(BF)
            return 0

        lax.fori_loop(0, 4, give, 0)
        buf[0, :, :, :, pl.ds(pl.multiple_of(to * 1152 + 1024, 128), 128)] = inner.astype(BF)
        sent = buf.at[0, :, :, :, pl.ds(pl.multiple_of(to * 1152, 128), 1152)]
        halves.append(copies.start(sent, rb.at[to], me.other()))

    cuts = (pl.ds(0, 384), pl.ds(384, 384), pl.ds(768, 384))
    stage1 = []
    for step in range(4):
        to = wrap(t, step + 1)
        halves[step].wait_recv()

        def keep(i, _):
            cols = pl.ds(pl.multiple_of(i * 256, 256), 256)
            mine = part(to * 2048 + c * 1024, i)
            q[to, :, :, :, cols] = (mine + rb[to, :, :, :, cols].astype(F32)).astype(BF)
            return 0

        lax.fori_loop(0, 4, keep, 0)
        q[to, :, :, :, 1024:1152] = (inner + rb[to, :, :, :, 1024:1152].astype(F32)).astype(BF)
        if step < 3:
            stage1.append(
                copies.start(q.at[to, :, :, :, cuts[0]], ra1.at[0, step], me.at(z=to))
            )
    for d in (1, 2, 3):
        to = wrap(y, d)
        stage1.append(copies.start(q.at[:, to, :, :, cuts[1]], ra1.at[1, d - 1], me.at(y=to)))
        to = wrap(x, d)
        stage1.append(copies.start(q.at[:, :, to, :, cuts[2]], ra1.at[2, d - 1], me.at(x=to)))
    own1 = (
        lambda: q[t, :, :, :, cuts[0]],
        lambda: q[:, y, :, :, cuts[1]],
        lambda: q[:, :, x, :, cuts[2]],
    )
    for m in seen_mid:
        ring_end(m)
    for pos, view, _ in seen2:
        seen_crossed.append(cross(view(wrap(pos, 2), None)))
    for copy in seen_crossed:
        copy.wait_recv()
    copies.settle([copy for pair in seen_begun + seen_mid for copy in pair] + seen_crossed)

    counts = spread[:, :, :, 0:16, 2432:2560].reshape(32, 16, 128).astype(F32)[:, 0, :]
    frame_of, quarter_of, slot_of = column_ref[0:1, :], column_ref[1:2, :], column_ref[2:3, :]
    frames = lax.broadcasted_iota(jnp.int32, (32, 1536), 0)
    wide = jnp.broadcast_to(counts[:, :1], (32, 1536))
    offset = jnp.sum(jnp.where(frames < frame_of, wide, 0.0), axis=0, keepdims=True)
    count = jnp.sum(jnp.where(frames == frame_of, wide, 0.0), axis=0, keepdims=True)
    code = (offset.astype(jnp.int32) + slot_of) * 4 + quarter_of
    code = jnp.where(slot_of < count.astype(jnp.int32), code, -1)
    for i in range(3):
        chosen = one_hot(pos_ref[i * 256 : (i + 1) * 256, 1:2], code)
        buf[1, :, :, :, i * 1536 : (i + 1) * 1536] = chosen.reshape(4, 4, 16, 1536)
    lanes = lax.broadcasted_iota(jnp.int32, (32, 128), 0)
    own_offset = jnp.sum(jnp.where(lanes < me.frame, counts, 0.0), axis=0, keepdims=True)
    own_count = jnp.sum(jnp.where(lanes == me.frame, counts, 0.0), axis=0, keepdims=True)
    own_offset = own_offset.astype(jnp.int32)[:, :1]
    own_count = own_count.astype(jnp.int32)[:, :1]
    local_slot, local_quarter = local_ref[:, 0:1], local_ref[:, 1:2]
    own_code = (own_offset + local_slot) * 4 + local_quarter
    own_code = jnp.where(local_slot < own_count, own_code, -1)
    here = one_hot(own_code, rowline_ref[...])

    def compact(i, _):
        cols = pl.ds(pl.multiple_of(i * 256, 256), 256)
        block = spread[:, :, :, :, cols].reshape(1536, 256)
        for j in range(3):
            hot = buf[1, :, :, :, j * 1536 : (j + 1) * 1536].reshape(256, 1536)
            comp[j * 256 : (j + 1) * 256, cols] = nn(hot, block).astype(BF)
        return 0

    lax.fori_loop(0, 10, compact, 0)
    base = c * 1024
    loads[3].wait()

    def first(i, _):
        rows = pl.ds(pl.multiple_of((i // 4) * 192, 48), 192)
        pair = pl.ds(pl.multiple_of(lax.rem(i // 4, 2) * 2, 2), 2)
        cols = pl.multiple_of(lax.rem(i, 4) * 256, 256)
        pre = nn(comp[rows, 0:1152], wp[:, pl.ds(base + cols, 256)])
        weight = comp[rows, 2304:2305].astype(F32)
        tilt = (erf_gelu_slope(pre) * weight).astype(BF)
        spread[i // 8, pair, :, :, pl.ds(1152 + cols, 256)] = tilt.reshape(2, 2, 48, 256)
        return 0

    stage2 = []
    for p in range(3):
        arrived = stage1[:3] if p == 0 else stage1[2 + p :: 2]
        for copy in arrived:
            copy.wait_recv()
        value = own1[p]().astype(F32)
        for d in range(3):
            value = value + ra1[p, d].astype(F32)
        sa1[p] = value.astype(BF)
        for d in (1, 2, 3):
            if p == 0:
                to = wrap(y, d)
                stage2.append(copies.start(sa1.at[0, to], ra2.at[0, d - 1], me.at(y=to)))
            elif p == 1:
                to = wrap(x, d)
                stage2.append(copies.start(sa1.at[1, :, to], ra2.at[1, d - 1], me.at(x=to)))
            else:
                to = wrap(t, d)
                stage2.append(copies.start(sa1.at[2, to], ra2.at[2, d - 1], me.at(z=to)))
    lax.fori_loop(0, 5, first, 0)
    own2 = (lambda: sa1[0, y], lambda: sa1[1, :, x], lambda: sa1[2, t])
    stage3 = []
    for p in range(3):
        for copy in stage2[3 * p : 3 * p + 3]:
            copy.wait_recv()
        value = own2[p]().astype(F32)
        for d in range(3):
            value = value + ra2[p, d].astype(F32)
        sa2[p] = value.astype(BF)
        for d in (1, 2, 3):
            if p == 0:
                to = wrap(x, d)
                stage3.append(copies.start(sa2.at[0, to], ra3.at[0, d - 1], me.at(x=to)))
            elif p == 1:
                to = wrap(t, d)
                stage3.append(copies.start(sa2.at[1, to], ra3.at[1, d - 1], me.at(z=to)))
            else:
                to = wrap(y, d)
                stage3.append(copies.start(sa2.at[2, to], ra3.at[2, d - 1], me.at(y=to)))
    lax.fori_loop(5, 10, first, 0)
    own3 = (lambda: sa2[0, x], lambda: sa2[1, t], lambda: sa2[2, y])
    pieces = []
    for p in range(3):
        for copy in stage3[3 * p : 3 * p + 3]:
            copy.wait_recv()
        value = own3[p]().astype(F32)
        for d in range(3):
            value = value + ra3[p, d].astype(F32)
        pieces.append(value)
    root16 = root.reshape(16, 1)
    mean = pieces[2][:, 256:257] / 8192.0
    for p in range(3):
        width = 384 if p < 2 else 256
        cols = pl.ds(pl.multiple_of(t * 2048 + c * 1024 + p * 384, 128), width)
        unit = xg[:, 0, :, cols].reshape(16, width) / root16
        scaled = pieces[p][:, :width] * gain_ref[:, cols]
        out = xg[:, 1, :, cols].reshape(16, width) + (scaled - unit * mean) / root16
        eall_ref[y, x, :, pl.ds(pl.multiple_of(c * 1024 + p * 384, 128), width)] = out.astype(BF)


    def embed0x(pos):
        return eall_ref.at[y, pos, :, pl.ds(base, 512)]

    def embed1y(pos):
        return eall_ref.at[pos, x, :, pl.ds(base + 512, 512)]

    def embed0y(pos):
        return eall_ref.at[pos, :, :, pl.ds(base, 512)]

    def embed1x(pos):
        return eall_ref.at[:, pos, :, pl.ds(base + 512, 512)]

    begun = [direct_begin(copies, x, embed0x, dev_x), direct_begin(copies, y, embed1y, dev_y)]
    lax.fori_loop(10, 16, first, 0)
    for b in begun:
        for copy in b:
            copy.wait_recv()
    copies.finish()
    begun = [direct_begin(copies, y, embed0y, dev_y), direct_begin(copies, x, embed1x, dev_x)]
    crossed = [cross(embed0y(y)), cross(embed1x(x))]
    loads[4].wait()

    def second(i, _):
        rows = pl.ds(pl.multiple_of(i * 96, 96), 96)
        act, tilt = tanh_gelu_and_slope(nt(comp[rows, 1152:2304], w1[...]))
        at = (2 + i // 4, lax.rem(i, 4))
        spread[at[0], at[1], :, :, 0:1076] = act.astype(BF).reshape(2, 48, 1076)
        spread[at[0], at[1], :, :, 1152:2228] = tilt.astype(BF).reshape(2, 48, 1076)
        return 0

    lax.fori_loop(0, 8, second, 0)
    for b, view, pos in ((begun[0], embed0y, y), (begun[1], embed1x, x)):
        for copy, d in zip(b, (3, 1, 2)):
            copy.wait_recv()
            crossed.append(cross(view(wrap(pos, d))))

    mine = pl.ds(pl.multiple_of(k * 48, 48), 48)
    pre = nn(comp[mine, 0:1152], wp[...])
    tilt = erf_gelu_slope(pre) * comp[mine, 2304:2305].astype(F32)
    for copy in crossed:
        copy.wait_recv()
    places = lax.broadcasted_iota(jnp.int32, (48, 256), 1)
    kept = nn(one_hot(pos_ref[mine, 0:1], places), eall_ref[...].reshape(256, 2048))
    act48 = (kept * tilt).astype(BF)
    part48 = nt(act48, wp[pl.ds(pl.multiple_of(c * 512, 512), 640), :])
    vmine[...] = part48.astype(BF)
    begun = [copies.start(vmine, vgot.at[d - 1], me.at(z=wrap(t, d))) for d in (1, 3, 2)]
    both = eall_ref[y, x].astype(F32)
    embed_ref[...] = jnp.where(c == 0, both[:8], both[8:]).astype(BF)
    places = lax.broadcasted_iota(jnp.int32, (192, 256), 1)

    def third(i, _):
        rows = pl.ds(pl.multiple_of(i * 192, 192), 192)
        kept = nn(
            one_hot(pos_ref[rows, 0:1], places),
            eall_ref[:, :, :, pl.ds(pl.multiple_of(base, 1024), 1024)].reshape(256, 1024),
        )
        pair = pl.ds(pl.multiple_of(lax.rem(i, 2) * 2, 2), 2)
        tilt = spread[i // 2, pair, :, :, 1152:2176].reshape(192, 1024).astype(F32)
        spread[i // 2, pair, :, :, 1152:2176] = (kept * tilt).astype(BF).reshape(2, 2, 48, 1024)
        return 0

    value = part48
    for copy in begun:
        copy.wait_recv()
    for d in range(3):
        value = value + vgot[d].astype(F32)
    vis[c, y, x] = value.astype(BF)

    def e0x(pos):
        return vis.at[c, y, pos, :, pl.ds(0, 384)]

    def e1y(pos):
        return vis.at[c, pos, x, :, pl.ds(384, 256)]

    def e0y(pos):
        return vis.at[c, pos, :, :, pl.ds(0, 384)]

    def e1x(pos):
        return vis.at[c, :, pos, :, pl.ds(384, 256)]

    begun = [direct_begin(copies, x, e0x, dev_x), direct_begin(copies, y, e1y, dev_y)]
    lax.fori_loop(0, 4, third, 0)
    for b in begun:
        for copy in b:
            copy.wait_recv()
    begun = [direct_begin(copies, y, e0y, dev_y), direct_begin(copies, x, e1x, dev_x)]
    crossed = [cross(e0y(y)), cross(e1x(x))]

    source = lax.broadcasted_iota(jnp.int32, (1152, 128), 0)
    lane = lax.broadcasted_iota(jnp.int32, (1152, 128), 1)
    block = me.frame * 36
    other = (me.frame + 1 - 2 * c) * 36
    want = jnp.where(lane < 64, jnp.where(lane < 36, block + lane, -1),
                     jnp.where(lane < 100, other + lane - 64, -1))
    chosen = one_hot(source, want)
    out_cols = nn(comp[:, 0:1152], chosen).astype(BF)
    proj = tn(out_cols, spread[0:2, :, :, :, 1152:2176].reshape(768, 1024))
    away[...] = proj[64:104]
    px_copy = copies.start(away, px, me.other())
    proj_ref[:, pl.ds(pl.multiple_of(base, 1024), 1024)] = proj[0:36]
    ln_cols = nn(comp[:, 1152:2304], chosen).astype(BF)

    for b, view, pos in ((begun[0], e0y, y), (begun[1], e1x, x)):
        for copy, d in zip(b, (3, 1, 2)):
            copy.wait_recv()
            crossed.append(copies.start(view(wrap(pos, d)), view(wrap(pos, d)), me.other()))
    px_copy.wait_recv()
    proj_ref[:, pl.ds(pl.multiple_of(1024 - base, 1024), 1024)] = px[0:36]
    for copy in crossed:
        copy.wait_recv()

    loads[5].wait()

    def fourth(i, _):
        low = vis[0, i].reshape(192, 640)
        high = vis[1, i].reshape(192, 640)[:, 128:]
        back = nt(low, w2[:, 0:640]) + nt(high, w2[:, 640:1152])
        pair = pl.ds(pl.multiple_of(lax.rem(i, 2) * 2, 2), 2)
        tilt = spread[2 + i // 2, pair, :, :, 1152:2228].reshape(192, 1076).astype(F32)
        spread[i // 2, pair, :, :, 0:1076] = (back * tilt).astype(BF).reshape(2, 2, 48, 1076)
        return 0

    lax.fori_loop(0, 4, fourth, 0)
    fgrad = spread[0:2, :, :, :, 0:1076].reshape(768, 1076)
    here_grad = nn(here, fgrad).astype(BF)
    ln_part = nn(here_grad, w1[...]) * vgain_ref[...]
    sums = jnp.sum(ln_part, axis=1, keepdims=True)
    dots = jnp.sum(ln_part * unit_ref[...], axis=1, keepdims=True)
    lane = lax.broadcasted_iota(jnp.int32, (48, 96), 1)
    extra = jnp.where(lane == 0, sums, jnp.where(lane == 1, dots, 0.0))
    for i in range(4):
        lnp[i, :, 0:288] = ln_part[:, i * 288 : (i + 1) * 288]
        lnp[i, :, 288:384] = extra
    lnmine[...] = lnp[...].astype(BF)
    vis0 = vis[0].reshape(768, 640)
    vis1 = vis[1].reshape(768, 640)[:, 128:]
    begun = [
        copies.start(lnmine.at[wrap(t, d)], lngot.at[d - 1], me.at(z=wrap(t, d))) for d in (1, 3, 2)
    ]
    fc1_ref[...] = tn(ln_cols, fgrad)[0:36]
    vis_cols = (nn(vis0, chosen[0:640]) + nn(vis1, chosen[640:1152])).astype(BF)
    fc2_ref[...] = tn(vis_cols, spread[2:4, :, :, :, 0:1076].reshape(768, 1076))[0:36]
    vis_here = jnp.concatenate([nn(here, vis0), nn(here, vis1)], axis=1)
    for i in range(4):
        vis4[i] = vis_here[:, i * 288 : (i + 1) * 288]
        unit4[i] = unit_ref[:, i * 288 : (i + 1) * 288]
    for copy in begun:
        copy.wait_recv()
    value = lnp[t]
    for d in range(3):
        value = value + lngot[d].astype(F32)
    mean, slant = value[:, 288:289] / 1152.0, value[:, 289:290] / 1152.0
    result = vis4[t] + (value[:, 0:288] - mean - unit4[t] * slant) / dev_ref[...]
    cells = lax.broadcasted_iota(jnp.int32, (48, 729), 1)
    spot = one_hot(feature_ref[...], cells)
    fg_ref[...] = tn(result.astype(BF), spot).astype(BF)
    copies.finish()


def column_codes():
    column = np.arange(1536)
    code = np.zeros((8, 1536), np.int32)
    code[0], code[1], code[2] = column // 48, column % 48 // 12, column % 12
    return code


def row_codes():
    row = np.arange(768)
    return (row // 48 * 12 + row % 12) * 4 + row % 48 // 12


def local_codes():
    row = np.arange(48)
    return np.stack([row % 12, row // 12], axis=1).astype(np.int32)


def copy_kernel(*refs):
    count = (len(refs) - 2) // 3
    into = [
        pltpu.make_async_copy(refs[i], refs[2 * count + i], refs[-2].at[i]) for i in range(count)
    ]
    away = [
        pltpu.make_async_copy(refs[2 * count + i], refs[count + i], refs[-1].at[i])
        for i in range(count)
    ]
    for copy in into:
        copy.start()
    for first, second in zip(into, away):
        first.wait()
        second.start()
    for copy in away:
        copy.wait()


def hand_over(arrays):
    return pl.pallas_call(
        copy_kernel,
        name="hand_over",
        out_shape=tuple(jax.ShapeDtypeStruct(a.shape, a.dtype) for a in arrays),
        in_specs=[ANY] * len(arrays),
        out_specs=(ANY,) * len(arrays),
        scratch_shapes=[pltpu.VMEM(a.shape, a.dtype) for a in arrays]
        + [pltpu.SemaphoreType.DMA((len(arrays),))] * 2,
    )(*arrays)


def whole(llm_input, out_grad, llm_gain, packed, position, feature, unit_in, deviation, vis_gain,
          w_gate, w_up, w_down, w_proj, w_fc1, w_fc2):
    codes = row_codes().astype(np.int32)
    w_gate, w_up, w_fc1 = w_gate.T, w_up.T, w_fc1.T
    units = w_gate.shape[0]
    hidden = w_fc2.shape[0]
    sems = 200
    part = (3, 3)
    return pl.pallas_call(
        whole_kernel,
        name="whole",
        out_shape=(
            jax.ShapeDtypeStruct((8, 2048), BF),
            jax.ShapeDtypeStruct((36, 2048), F32),
            jax.ShapeDtypeStruct((36, hidden), F32),
            jax.ShapeDtypeStruct((36, hidden), F32),
            jax.ShapeDtypeStruct((288, 729), BF),
        ),
        in_specs=[VM] * 12 + [ANY] * 6,
        out_specs=(VM,) * 5,
        scratch_shapes=[
            pltpu.VMEM((2, 2, 8, 8192), F32),
            pltpu.VMEM((2, 4, 4, 16, 8192), BF),
            pltpu.VMEM(w_gate.shape, BF),
            pltpu.VMEM(w_up.shape, BF),
            pltpu.VMEM(w_down.shape, BF),
            pltpu.VMEM((256, units), F32),
            pltpu.VMEM((256, units), F32),
            pltpu.VMEM((256, units), F32),
            pltpu.VMEM((256, units), BF),
            pltpu.VMEM((256, units), BF),
            pltpu.VMEM((4, 4, 4, 16, 1152), BF),
            pltpu.VMEM((4, 4, 4, 16, 1152), BF),
            pltpu.VMEM(part + (4, 4, 16, 384), BF),
            pltpu.VMEM(part + (4, 16, 384), BF),
            pltpu.VMEM(part + (16, 384), BF),
            pltpu.VMEM((3, 4, 4, 16, 384), BF),
            pltpu.VMEM((3, 4, 16, 384), BF),
            pltpu.VMEM((4, 4, 16, 2048), BF),
            pltpu.VMEM((4, 4, 2, 48, 2560), BF),
            pltpu.VMEM(w_proj.shape, BF),
            pltpu.VMEM(w_fc1.shape, BF),
            pltpu.VMEM(w_fc2.shape, BF),
            pltpu.VMEM((768, 2560), BF),
            pltpu.VMEM((48, 640), BF),
            pltpu.VMEM((3, 48, 640), BF),
            pltpu.VMEM((2, 4, 4, 48, 640), BF),
            pltpu.VMEM((40, 1024), F32),
            pltpu.VMEM((40, 1024), F32),
            pltpu.VMEM((4, 48, 384), F32),
            pltpu.VMEM((4, 48, 384), BF),
            pltpu.VMEM((3, 48, 384), BF),
            pltpu.VMEM((4, 48, 288), F32),
            pltpu.VMEM((4, 48, 288), F32),
            pltpu.SemaphoreType.DMA((6,)),
            pltpu.SemaphoreType.DMA((sems,)),
            pltpu.SemaphoreType.DMA((sems,)),
        ],
        compiler_params=pltpu.CompilerParams(
            collective_id=0, has_side_effects=True, vmem_limit_bytes=63 * 1024 * 1024
        ),
    )(
        llm_input, out_grad, llm_gain.reshape(1, -1), packed, position, feature, unit_in, deviation,
        vis_gain, jnp.asarray(column_codes()),
        jnp.asarray(codes.reshape(1, -1)), jnp.asarray(local_codes()),
        w_gate, w_up, w_down, w_proj, w_fc1, w_fc2,
    )


def prepare_kernel(
    index_ref, count_ref, seq_ref, in_ref, out_ref, gain_ref, codes_ref,
    packed_ref, pos_ref, feature_ref, unit_ref, dev_ref, vgain_ref,
):
    width = (GRID + 1) // 2
    row = lax.broadcasted_iota(jnp.int32, (48, 1), 0)
    quarter = (
        jnp.where(row >= 12, 1, 0) + jnp.where(row >= 24, 1, 0) + jnp.where(row >= 36, 1, 0)
    )
    slot = row - 12 * quarter
    pool_row = jnp.zeros_like(row)
    pool_col = jnp.zeros_like(row)
    for i in range(12):
        token = index_ref[0, i]
        down = token // width
        pool_row = jnp.where(slot == i, down, pool_row)
        pool_col = jnp.where(slot == i, token - down * width, pool_col)
    low = jnp.where(quarter >= 2, 1, 0)
    grid_row = 2 * pool_row + low
    grid_col = 2 * pool_col + quarter - 2 * low
    count = count_ref[0]
    inside = (grid_row < GRID) & (grid_col < GRID) & (slot < count)
    row_cells = jnp.where(2 * pool_row + 1 < GRID, 0.5, 1.0)
    col_cells = jnp.where(2 * pool_col + 1 < GRID, 0.5, 1.0)
    weight = jnp.where(inside, row_cells * col_cells, 0.0)
    feature = jnp.where(inside, grid_row * GRID + grid_col, 0)
    feature_ref[...] = feature
    cells = lax.broadcasted_iota(jnp.int32, (48, in_ref.shape[0]), 1)
    spot = one_hot(feature, cells)
    packed_ref[:, 0:1152] = nn(spot, out_ref[...]).astype(BF)
    rows_in = nn(spot, in_ref[...])
    center = jnp.mean(rows_in, axis=1, keepdims=True)
    variance = jnp.mean((rows_in - center) * (rows_in - center), axis=1, keepdims=True)
    deviation = jnp.sqrt(variance + 1e-06)
    unit_in = (rows_in - center) / deviation
    unit_ref[...] = unit_in
    gain = gain_ref[...].reshape(1, 1152)
    vgain_ref[...] = gain
    dev_ref[...] = deviation
    packed_ref[:, 1152:2304] = (unit_in * gain).astype(BF)
    packed_ref[:, 2304:2432] = jnp.broadcast_to(weight, (48, 128)).astype(BF)
    packed_ref[:, 2432:2560] = jnp.full((48, 128), count, jnp.int32).astype(F32).astype(BF)
    tokens = lax.broadcasted_iota(jnp.int32, (768, 256), 1)
    place = jnp.where(codes_ref[:, 0:1] == tokens, seq_ref[...].astype(F32), 0.0)
    pos_ref[:, 0:1] = jnp.sum(place, axis=1, keepdims=True).astype(jnp.int32)
    pos_ref[:, 1:2] = codes_ref[:, 1:2]


def prepare(keep_index, keep_count, seq_order, vision_in, vision_out, vis_gain):
    codes = row_codes()
    codes = np.stack([codes // 4, codes], axis=1).astype(np.int32)
    scalar = pl.BlockSpec(memory_space=pltpu.SMEM)
    return pl.pallas_call(
        prepare_kernel,
        name="prepare",
        out_shape=(
            jax.ShapeDtypeStruct((48, 2560), BF),
            jax.ShapeDtypeStruct((768, 2), jnp.int32),
            jax.ShapeDtypeStruct((48, 1), jnp.int32),
            jax.ShapeDtypeStruct((48, 1152), F32),
            jax.ShapeDtypeStruct((48, 1), F32),
            jax.ShapeDtypeStruct((1, 1152), F32),
        ),
        in_specs=[scalar, scalar, VM, VM, VM, VM, VM],
        out_specs=(VM,) * 6,
        compiler_params=pltpu.CompilerParams(vmem_limit_bytes=63 * 1024 * 1024),
    )(
        keep_index, keep_count, seq_order.reshape(1, -1), vision_in, vision_out, vis_gain,
        jnp.asarray(codes),
    )


def shards(
    llm_input,
    out_grad,
    llm_gain,
    w_gate,
    w_up,
    w_down,
    keep_index,
    keep_count,
    seq_order,
    vision_in,
    vision_out,
    vis_gain,
    w_proj,
    w_fc1,
    w_fc2,
):
    packed, position, feature, unit_in, deviation, vis_gain = prepare(
        keep_index, keep_count, seq_order, vision_in, vision_out, vis_gain
    )
    results = whole(
        llm_input, out_grad, llm_gain, packed, position, feature, unit_in, deviation,
        vis_gain, w_gate, w_up, w_down, w_proj, w_fc1, w_fc2,
    )
    embed, proj_grad, fc1_grad, fc2_grad, feature_grad = hand_over(results)
    return (embed, proj_grad, fc1_grad, fc2_grad.T, feature_grad.T)


def solution(mesh):
    in_specs = (
        P("frame", None),
        P("frame", None),
        P(),
        P(None, ("frame", "tensor")),
        P(None, ("frame", "tensor")),
        P(("frame", "tensor"), None),
        P("frame", None),
        P("frame"),
        P(),
        P("frame", None),
        P("frame", None),
        P(),
        P(None, "tensor"),
        P(None, "tensor"),
        P("tensor", None),
    )
    out_specs = (
        P("frame", "tensor"),
        P("frame", "tensor"),
        P("frame", "tensor"),
        P("tensor", "frame"),
        P("frame", "tensor"),
    )
    return jax.shard_map(shards, mesh=mesh, in_specs=in_specs, out_specs=out_specs, check_vma=False)
```

```python
import functools

import jax
import jax.numpy as jnp
import numpy as np
from jax import lax
from jax.experimental import pallas as pl
from jax.experimental.pallas import tpu as pltpu
from jax.sharding import PartitionSpec as P

GRID = 27
BF = jnp.bfloat16
F32 = jnp.float32
MESH = pl.DeviceIdType.MESH
ANY = pl.BlockSpec(memory_space=pl.ANY)
VM = pl.BlockSpec(memory_space=pltpu.VMEM)


def nt(left, right):
    return lax.dot_general(left, right, (((1,), (1,)), ((), ())), preferred_element_type=F32)


def tn(left, right):
    return lax.dot_general(left, right, (((0,), (0,)), ((), ())), preferred_element_type=F32)


def nn(left, right):
    return jnp.dot(left, right, preferred_element_type=F32)


class Place:
    def __init__(self):
        frame = lax.axis_index("frame")
        self.frame = frame
        self.t = lax.axis_index("tensor")
        self.c = lax.rem(frame, 2)
        self.k = frame // 2
        self.x = lax.rem(self.k, 4)
        self.y = self.k // 4

    def at(self, y=None, x=None, z=None, core=None):
        y = self.y if y is None else y
        x = self.x if x is None else x
        z = self.t if z is None else z
        core = self.c if core is None else core
        return ((y * 4 + x) * 2 + core, z)

    def other(self):
        return self.at(core=1 - self.c)


def greet(targets):
    barrier = pltpu.get_barrier_semaphore()
    for target in targets:
        pl.semaphore_signal(barrier, inc=1, device_id=target, device_id_type=MESH)
    pl.semaphore_wait(barrier, len(targets))


def wrap(pos, d):
    return lax.rem(pos + d, 4)


class Copies:
    def __init__(self, send, recv):
        self.send, self.recv, self.used, self.open = send, recv, 0, []

    def start(self, src, dst, target):
        i = self.used
        self.used += 1
        copy = pltpu.make_async_remote_copy(
            src_ref=src,
            dst_ref=dst,
            send_sem=self.send.at[i],
            recv_sem=self.recv.at[i],
            device_id=target,
            device_id_type=MESH,
        )
        copy.start()
        self.open.append(copy)
        return copy

    def finish(self):
        for copy in self.open:
            copy.wait_send()
        self.open = []

    def settle(self, some):
        for copy in some:
            copy.wait_send()
        self.open = [copy for copy in self.open if not any(copy is done for done in some)]


def ring_begin(copies, pos, view, dev):
    right = copies.start(view(pos, None), view(pos, None), dev(wrap(pos, 1)))
    left = copies.start(view(pos, None), view(pos, None), dev(wrap(pos, 3)))
    return (right, left)


def ring_middle(copies, pos, view, dev, begun):
    right, left = begun
    right.wait_recv()
    on_right = copies.start(view(wrap(pos, 3), 0), view(wrap(pos, 3), 0), dev(wrap(pos, 1)))
    left.wait_recv()
    on_left = copies.start(view(wrap(pos, 1), 1), view(wrap(pos, 1), 1), dev(wrap(pos, 3)))
    return (on_right, on_left)


def ring_end(middle):
    for copy in middle:
        copy.wait_recv()


def direct_begin(copies, pos, view, dev):
    return [copies.start(view(pos), view(pos), dev(wrap(pos, d))) for d in (1, 3, 2)]


def pick(start, width, half):
    if half is None:
        return pl.ds(start, width)
    return pl.ds(start + half * (width // 2), width // 2)


def erf_gelu_slope(values):
    return (
        0.5 * (1.0 + lax.erf(values * 0.7071067811865476))
        + values * jnp.exp(-0.5 * values * values) * 0.3989422804014327
    )


def tanh_gelu_and_slope(values):
    square = values * values
    inner = 0.7978845608028654 * values * (1.0 + 0.044715 * square)
    tangent = jnp.tanh(inner)
    half = 0.5 * (1.0 + tangent)
    act = values * half
    slope = half + 0.5 * values * (1.0 - tangent * tangent) * 0.7978845608028654 * (
        1.0 + 3.0 * 0.044715 * square
    )
    return act, slope


def one_hot(left, right):
    return jnp.where(left == right, 1.0, 0.0).astype(BF)


def whole_kernel(
    x_ref, g_ref, gain_ref, pack_ref, pos_ref, feature_ref, unit_ref, dev_ref, vgain_ref,
    column_ref, rowline_ref, local_ref,
    wg_hbm, wu_hbm, wd_hbm, wp_hbm, w1_hbm, w2_hbm,
    embed_ref, proj_ref, fc1_ref, fc2_ref, fg_ref,
    xg, buf, wg, wu, wd, acc_g, acc_u, acc_h, gg, ug, rb, q,
    ra1, ra2, ra3, sa1, sa2, eall_ref,
    spread, wp, w1, w2, comp,
    vmine, vgot, vis, away, px, lnp, lnmine, lngot, unit4, vis4,
    wsem, send, recv,
):
    me = Place()
    c, t, x, y, k = me.c, me.t, me.x, me.y, me.k
    loads = [
        pltpu.make_async_copy(source, target, wsem.at[i])
        for i, (source, target) in enumerate(
            ((wg_hbm, wg), (wu_hbm, wu), (wd_hbm, wd), (wp_hbm, wp), (w1_hbm, w1), (w2_hbm, w2))
        )
    ]
    for load in loads:
        load.start()
    xg[c, 0] = x_ref[...].astype(F32)
    xg[c, 1] = g_ref[...].astype(F32)
    spread[y, x, c] = pack_ref[...]
    targets = [me.other()]
    targets += [me.at(z=wrap(t, d)) for d in (1, 2, 3)]
    targets += [me.at(x=wrap(x, d)) for d in (1, 2, 3)]
    targets += [me.at(y=wrap(y, d)) for d in (1, 2, 3)]
    greet(targets)
    copies = Copies(send, recv)
    swap = copies.start(xg.at[c], xg.at[c], me.other())

    def view0x(pos, half):
        return buf.at[c, y, pos, :, pick(0, 4096, half)]

    def view1y(pos, half):
        return buf.at[c, pos, x, :, pick(4096, 4096, half)]

    def dev_x(pos):
        return me.at(x=pos)

    def dev_y(pos):
        return me.at(y=pos)

    def spread0x(pos, half):
        return spread.at[y, pos, c, :, pick(0, 1280, half)]

    def spread1y(pos, half):
        return spread.at[pos, x, c, :, pick(1280, 1280, half)]

    def spread0y(pos, half):
        return spread.at[pos, :, c, :, pick(0, 1280, half)]

    def spread1x(pos, half):
        return spread.at[:, pos, c, :, pick(1280, 1280, half)]

    def cross(view):
        return copies.start(view, view, me.other())

    def begin(rings):
        return [ring_begin(copies, *ring) for ring in rings]

    def middle(rings, begun):
        return [ring_middle(copies, *ring, b) for ring, b in zip(rings, begun)]

    swap.wait_recv()
    rows = xg[:, 0]
    total = jnp.sum(rows * rows, axis=2, keepdims=True)
    root = jnp.sqrt(total / 8192.0 + 1e-06)

    def make_block(i, _):
        cols = pl.ds(pl.multiple_of(i * 1024, 1024), 1024)
        normed = xg[:, 0, :, cols] / root * gain_ref[:, cols][None]
        block = jnp.where(c == 0, normed, xg[:, 1, :, cols])
        buf[c, y, x, :, cols] = block.reshape(16, 1024).astype(BF)
        return 0

    lax.fori_loop(0, 8, make_block, 0)


    def along_y(block):
        return (y, lambda pos, half: buf.at[c, pos, block, :, pick(0, 4096, half)], dev_y)

    def along_x(block):
        return (x, lambda pos, half: buf.at[c, block, pos, :, pick(4096, 4096, half)], dev_x)

    seen1 = [(x, spread0x, dev_x), (y, spread1y, dev_y)]
    seen2 = [(y, spread0y, dev_y), (x, spread1x, dev_x)]
    crossed = []

    def cross_all(rings, steps):
        for pos, view, _ in rings:
            for d in steps:
                crossed.append(cross(view(wrap(pos, d), None)))

    main = [(x, view0x, dev_x), (y, view1y, dev_y)]
    onward = [[along_y(wrap(x, d)), along_x(wrap(y, d))] for d in range(4)]
    begun = begin(main)
    going = {0: begin(onward[0])}
    seen_begun = begin(seen1)
    cross_all(onward[0], (0,))
    mid = middle(main, begun)
    for d in (3, 1):
        going[d] = begin(onward[d])
        cross_all(onward[d], (0,))
    ends = middle(onward[0], going[0])
    cross_all(onward[0], (1, 3))
    for m in mid:
        ring_end(m)
    going[2] = begin(onward[2])
    cross_all(onward[2], (0,))
    for m in ends:
        ring_end(m)
    cross_all(onward[0], (2,))
    seen_mid = middle(seen1, seen_begun)
    last = []
    for d in (3, 1, 2):
        last.append((d, middle(onward[d], going[d])))
        cross_all(onward[d], (1, 3))
    for m in seen_mid:
        ring_end(m)
    sent, copies.open = copies.open, []
    seen_begun = begin(seen2)
    before = len(copies.open)
    for d, ends in last:
        for m in ends:
            ring_end(m)
        cross_all(onward[d], (2,))
    sent += copies.open[before:]
    copies.open = copies.open[:before]
    for load in loads[:3]:
        load.wait()
    for copy in crossed:
        copy.wait_recv()

    acc_g[...] = jnp.zeros_like(acc_g)
    acc_u[...] = jnp.zeros_like(acc_u)
    acc_h[...] = jnp.zeros_like(acc_h)

    def first(i, _):
        cols = pl.ds(pl.multiple_of(i * 1024, 1024), 1024)
        normed = buf[0, :, :, :, cols].reshape(256, 1024)
        acc_g[...] += nt(normed, wg[:, cols])
        acc_u[...] += nt(normed, wu[:, cols])
        grads = buf[1, :, :, :, cols].reshape(256, 1024)
        acc_h[...] += nt(grads, wd[:, cols])
        return 0

    lax.fori_loop(0, 8, first, 0)
    gate, up, hidden = acc_g[...], acc_u[...], acc_h[...]
    sig = jax.nn.sigmoid(gate)
    up_grad = (hidden * gate * sig).astype(BF)
    gate_grad = (hidden * up * sig * (1.0 + gate * (1.0 - sig))).astype(BF)
    gg[...] = gate_grad
    ug[...] = up_grad
    inner = jnp.sum(
        gate_grad.astype(F32) * gate + up_grad.astype(F32) * up, axis=1, keepdims=True
    )
    inner = jnp.broadcast_to(inner, (256, 128)).reshape(4, 4, 16, 128)

    def part(base, i):
        cols = pl.ds(pl.multiple_of(base + i * 256, 256), 256)
        value = nn(gg[...], wg[:, cols]) + nn(ug[...], wu[:, cols])
        return value.reshape(4, 4, 16, 256)

    seen_crossed = [cross(view(pos, None)) for pos, view, _ in seen2]
    seen_mid = middle(seen2, seen_begun)
    for pos, view, _ in seen2:
        seen_crossed.append(cross(view(wrap(pos, 1), None)))
        seen_crossed.append(cross(view(wrap(pos, 3), None)))
    for copy in sent:
        copy.wait_send()
    halves = []
    for step in range(4):
        to = wrap(t, step + 1)

        def give(i, _):
            cols = pl.ds(pl.multiple_of(to * 1152 + i * 256, 128), 256)
            buf[0, :, :, :, cols] = part(to * 2048 + (1 - c) * 1024, i).astype(BF)
            return 0

        lax.fori_loop(0, 4, give, 0)
        buf[0, :, :, :, pl.ds(pl.multiple_of(to * 1152 + 1024, 128), 128)] = inner.astype(BF)
        sent = buf.at[0, :, :, :, pl.ds(pl.multiple_of(to * 1152, 128), 1152)]
        halves.append(copies.start(sent, rb.at[to], me.other()))

    cuts = (pl.ds(0, 384), pl.ds(384, 384), pl.ds(768, 384))
    stage1 = []
    for step in range(4):
        to = wrap(t, step + 1)
        halves[step].wait_recv()

        def keep(i, _):
            cols = pl.ds(pl.multiple_of(i * 256, 256), 256)
            mine = part(to * 2048 + c * 1024, i)
            q[to, :, :, :, cols] = (mine + rb[to, :, :, :, cols].astype(F32)).astype(BF)
            return 0

        lax.fori_loop(0, 4, keep, 0)
        q[to, :, :, :, 1024:1152] = (inner + rb[to, :, :, :, 1024:1152].astype(F32)).astype(BF)
        if step < 3:
            stage1.append(
                copies.start(q.at[to, :, :, :, cuts[0]], ra1.at[0, step], me.at(z=to))
            )
    for d in (1, 2, 3):
        to = wrap(y, d)
        stage1.append(copies.start(q.at[:, to, :, :, cuts[1]], ra1.at[1, d - 1], me.at(y=to)))
        to = wrap(x, d)
        stage1.append(copies.start(q.at[:, :, to, :, cuts[2]], ra1.at[2, d - 1], me.at(x=to)))
    own1 = (
        lambda: q[t, :, :, :, cuts[0]],
        lambda: q[:, y, :, :, cuts[1]],
        lambda: q[:, :, x, :, cuts[2]],
    )
    for m in seen_mid:
        ring_end(m)
    for pos, view, _ in seen2:
        seen_crossed.append(cross(view(wrap(pos, 2), None)))
    for copy in seen_crossed:
        copy.wait_recv()
    copies.settle([copy for pair in seen_begun + seen_mid for copy in pair] + seen_crossed)

    counts = spread[:, :, :, 0:16, 2432:2560].reshape(32, 16, 128).astype(F32)[:, 0, :]
    frame_of, quarter_of, slot_of = column_ref[0:1, :], column_ref[1:2, :], column_ref[2:3, :]
    frames = lax.broadcasted_iota(jnp.int32, (32, 1536), 0)
    wide = jnp.broadcast_to(counts[:, :1], (32, 1536))
    offset = jnp.sum(jnp.where(frames < frame_of, wide, 0.0), axis=0, keepdims=True)
    count = jnp.sum(jnp.where(frames == frame_of, wide, 0.0), axis=0, keepdims=True)
    code = (offset.astype(jnp.int32) + slot_of) * 4 + quarter_of
    code = jnp.where(slot_of < count.astype(jnp.int32), code, -1)
    for i in range(3):
        chosen = one_hot(pos_ref[i * 256 : (i + 1) * 256, 1:2], code)
        buf[1, :, :, :, i * 1536 : (i + 1) * 1536] = chosen.reshape(4, 4, 16, 1536)
    lanes = lax.broadcasted_iota(jnp.int32, (32, 128), 0)
    own_offset = jnp.sum(jnp.where(lanes < me.frame, counts, 0.0), axis=0, keepdims=True)
    own_count = jnp.sum(jnp.where(lanes == me.frame, counts, 0.0), axis=0, keepdims=True)
    own_offset = own_offset.astype(jnp.int32)[:, :1]
    own_count = own_count.astype(jnp.int32)[:, :1]
    local_slot, local_quarter = local_ref[:, 0:1], local_ref[:, 1:2]
    own_code = (own_offset + local_slot) * 4 + local_quarter
    own_code = jnp.where(local_slot < own_count, own_code, -1)
    here = one_hot(own_code, rowline_ref[...])

    def compact(i, _):
        cols = pl.ds(pl.multiple_of(i * 256, 256), 256)
        block = spread[:, :, :, :, cols].reshape(1536, 256)
        for j in range(3):
            hot = buf[1, :, :, :, j * 1536 : (j + 1) * 1536].reshape(256, 1536)
            comp[j * 256 : (j + 1) * 256, cols] = nn(hot, block).astype(BF)
        return 0

    lax.fori_loop(0, 10, compact, 0)
    base = c * 1024
    loads[3].wait()

    def first(i, _):
        rows = pl.ds(pl.multiple_of((i // 4) * 192, 48), 192)
        pair = pl.ds(pl.multiple_of(lax.rem(i // 4, 2) * 2, 2), 2)
        cols = pl.multiple_of(lax.rem(i, 4) * 256, 256)
        pre = nn(comp[rows, 0:1152], wp[:, pl.ds(base + cols, 256)])
        weight = comp[rows, 2304:2305].astype(F32)
        tilt = (erf_gelu_slope(pre) * weight).astype(BF)
        spread[i // 8, pair, :, :, pl.ds(1152 + cols, 256)] = tilt.reshape(2, 2, 48, 256)
        return 0

    stage2 = []
    for p in range(3):
        arrived = stage1[:3] if p == 0 else stage1[2 + p :: 2]
        for copy in arrived:
            copy.wait_recv()
        value = own1[p]().astype(F32)
        for d in range(3):
            value = value + ra1[p, d].astype(F32)
        sa1[p] = value.astype(BF)
        for d in (1, 2, 3):
            if p == 0:
                to = wrap(y, d)
                stage2.append(copies.start(sa1.at[0, to], ra2.at[0, d - 1], me.at(y=to)))
            elif p == 1:
                to = wrap(x, d)
                stage2.append(copies.start(sa1.at[1, :, to], ra2.at[1, d - 1], me.at(x=to)))
            else:
                to = wrap(t, d)
                stage2.append(copies.start(sa1.at[2, to], ra2.at[2, d - 1], me.at(z=to)))
    lax.fori_loop(0, 5, first, 0)
    own2 = (lambda: sa1[0, y], lambda: sa1[1, :, x], lambda: sa1[2, t])
    stage3 = []
    for p in range(3):
        for copy in stage2[3 * p : 3 * p + 3]:
            copy.wait_recv()
        value = own2[p]().astype(F32)
        for d in range(3):
            value = value + ra2[p, d].astype(F32)
        sa2[p] = value.astype(BF)
        for d in (1, 2, 3):
            if p == 0:
                to = wrap(x, d)
                stage3.append(copies.start(sa2.at[0, to], ra3.at[0, d - 1], me.at(x=to)))
            elif p == 1:
                to = wrap(t, d)
                stage3.append(copies.start(sa2.at[1, to], ra3.at[1, d - 1], me.at(z=to)))
            else:
                to = wrap(y, d)
                stage3.append(copies.start(sa2.at[2, to], ra3.at[2, d - 1], me.at(y=to)))
    lax.fori_loop(5, 10, first, 0)
    own3 = (lambda: sa2[0, x], lambda: sa2[1, t], lambda: sa2[2, y])
    pieces = []
    for p in range(3):
        for copy in stage3[3 * p : 3 * p + 3]:
            copy.wait_recv()
        value = own3[p]().astype(F32)
        for d in range(3):
            value = value + ra3[p, d].astype(F32)
        pieces.append(value)
    root16 = root.reshape(16, 1)
    mean = pieces[2][:, 256:257] / 8192.0
    for p in range(3):
        width = 384 if p < 2 else 256
        cols = pl.ds(pl.multiple_of(t * 2048 + c * 1024 + p * 384, 128), width)
        unit = xg[:, 0, :, cols].reshape(16, width) / root16
        scaled = pieces[p][:, :width] * gain_ref[:, cols]
        out = xg[:, 1, :, cols].reshape(16, width) + (scaled - unit * mean) / root16
        eall_ref[y, x, :, pl.ds(pl.multiple_of(c * 1024 + p * 384, 128), width)] = out.astype(BF)


    def embed0x(pos):
        return eall_ref.at[y, pos, :, pl.ds(base, 512)]

    def embed1y(pos):
        return eall_ref.at[pos, x, :, pl.ds(base + 512, 512)]

    def embed0y(pos):
        return eall_ref.at[pos, :, :, pl.ds(base, 512)]

    def embed1x(pos):
        return eall_ref.at[:, pos, :, pl.ds(base + 512, 512)]

    begun = [direct_begin(copies, x, embed0x, dev_x), direct_begin(copies, y, embed1y, dev_y)]
    lax.fori_loop(10, 16, first, 0)
    for b in begun:
        for copy in b:
            copy.wait_recv()
    copies.finish()
    begun = [direct_begin(copies, y, embed0y, dev_y), direct_begin(copies, x, embed1x, dev_x)]
    crossed = [cross(embed0y(y)), cross(embed1x(x))]
    loads[4].wait()

    def second(i, _):
        rows = pl.ds(pl.multiple_of(i * 192, 192), 192)
        act, tilt = tanh_gelu_and_slope(nt(comp[rows, 1152:2304], w1[...]))
        pair = pl.ds(pl.multiple_of(lax.rem(i, 2) * 2, 2), 2)
        spread[2 + i // 2, pair, :, :, 0:1076] = act.astype(BF).reshape(2, 2, 48, 1076)
        spread[2 + i // 2, pair, :, :, 1152:2228] = tilt.astype(BF).reshape(2, 2, 48, 1076)
        return 0

    lax.fori_loop(0, 4, second, 0)
    for b, view, pos in ((begun[0], embed0y, y), (begun[1], embed1x, x)):
        for copy, d in zip(b, (3, 1, 2)):
            copy.wait_recv()
            crossed.append(cross(view(wrap(pos, d))))

    mine = pl.ds(pl.multiple_of(k * 48, 48), 48)
    pre = nn(comp[mine, 0:1152], wp[...])
    tilt = erf_gelu_slope(pre) * comp[mine, 2304:2305].astype(F32)
    for copy in crossed:
        copy.wait_recv()
    places = lax.broadcasted_iota(jnp.int32, (48, 256), 1)
    kept = nn(one_hot(pos_ref[mine, 0:1], places), eall_ref[...].reshape(256, 2048))
    act48 = (kept * tilt).astype(BF)
    part48 = nt(act48, wp[pl.ds(pl.multiple_of(c * 512, 512), 640), :])
    vmine[...] = part48.astype(BF)
    begun = [copies.start(vmine, vgot.at[d - 1], me.at(z=wrap(t, d))) for d in (1, 3, 2)]
    both = eall_ref[y, x].astype(F32)
    embed_ref[...] = jnp.where(c == 0, both[:8], both[8:]).astype(BF)
    places = lax.broadcasted_iota(jnp.int32, (192, 256), 1)

    def third(i, _):
        rows = pl.ds(pl.multiple_of(i * 192, 192), 192)
        kept = nn(
            one_hot(pos_ref[rows, 0:1], places),
            eall_ref[:, :, :, pl.ds(pl.multiple_of(base, 1024), 1024)].reshape(256, 1024),
        )
        pair = pl.ds(pl.multiple_of(lax.rem(i, 2) * 2, 2), 2)
        tilt = spread[i // 2, pair, :, :, 1152:2176].reshape(192, 1024).astype(F32)
        spread[i // 2, pair, :, :, 1152:2176] = (kept * tilt).astype(BF).reshape(2, 2, 48, 1024)
        return 0

    value = part48
    for copy in begun:
        copy.wait_recv()
    for d in range(3):
        value = value + vgot[d].astype(F32)
    vis[c, y, x] = value.astype(BF)

    def e0x(pos):
        return vis.at[c, y, pos, :, pl.ds(0, 384)]

    def e1y(pos):
        return vis.at[c, pos, x, :, pl.ds(384, 256)]

    def e0y(pos):
        return vis.at[c, pos, :, :, pl.ds(0, 384)]

    def e1x(pos):
        return vis.at[c, :, pos, :, pl.ds(384, 256)]

    begun = [direct_begin(copies, x, e0x, dev_x), direct_begin(copies, y, e1y, dev_y)]
    lax.fori_loop(0, 4, third, 0)
    for b in begun:
        for copy in b:
            copy.wait_recv()
    begun = [direct_begin(copies, y, e0y, dev_y), direct_begin(copies, x, e1x, dev_x)]
    crossed = [cross(e0y(y)), cross(e1x(x))]

    source = lax.broadcasted_iota(jnp.int32, (1152, 128), 0)
    lane = lax.broadcasted_iota(jnp.int32, (1152, 128), 1)
    block = me.frame * 36
    other = (me.frame + 1 - 2 * c) * 36
    want = jnp.where(lane < 64, jnp.where(lane < 36, block + lane, -1),
                     jnp.where(lane < 100, other + lane - 64, -1))
    chosen = one_hot(source, want)
    out_cols = nn(comp[:, 0:1152], chosen).astype(BF)
    proj = tn(out_cols, spread[0:2, :, :, :, 1152:2176].reshape(768, 1024))
    away[...] = proj[64:104]
    px_copy = copies.start(away, px, me.other())
    proj_ref[:, pl.ds(pl.multiple_of(base, 1024), 1024)] = proj[0:36]
    ln_cols = nn(comp[:, 1152:2304], chosen).astype(BF)

    for b, view, pos in ((begun[0], e0y, y), (begun[1], e1x, x)):
        for copy, d in zip(b, (3, 1, 2)):
            copy.wait_recv()
            crossed.append(copies.start(view(wrap(pos, d)), view(wrap(pos, d)), me.other()))
    px_copy.wait_recv()
    proj_ref[:, pl.ds(pl.multiple_of(1024 - base, 1024), 1024)] = px[0:36]
    for copy in crossed:
        copy.wait_recv()

    loads[5].wait()

    def fourth(i, _):
        low = vis[0, i].reshape(192, 640)
        high = vis[1, i].reshape(192, 640)[:, 128:]
        back = nt(low, w2[:, 0:640]) + nt(high, w2[:, 640:1152])
        pair = pl.ds(pl.multiple_of(lax.rem(i, 2) * 2, 2), 2)
        tilt = spread[2 + i // 2, pair, :, :, 1152:2228].reshape(192, 1076).astype(F32)
        spread[i // 2, pair, :, :, 0:1076] = (back * tilt).astype(BF).reshape(2, 2, 48, 1076)
        return 0

    lax.fori_loop(0, 4, fourth, 0)
    fgrad = spread[0:2, :, :, :, 0:1076].reshape(768, 1076)
    here_grad = nn(here, fgrad).astype(BF)
    ln_part = nn(here_grad, w1[...]) * vgain_ref[...]
    sums = jnp.sum(ln_part, axis=1, keepdims=True)
    dots = jnp.sum(ln_part * unit_ref[...], axis=1, keepdims=True)
    lane = lax.broadcasted_iota(jnp.int32, (48, 96), 1)
    extra = jnp.where(lane == 0, sums, jnp.where(lane == 1, dots, 0.0))
    for i in range(4):
        lnp[i, :, 0:288] = ln_part[:, i * 288 : (i + 1) * 288]
        lnp[i, :, 288:384] = extra
    lnmine[...] = lnp[...].astype(BF)
    vis0 = vis[0].reshape(768, 640)
    vis1 = vis[1].reshape(768, 640)[:, 128:]
    begun = [
        copies.start(lnmine.at[wrap(t, d)], lngot.at[d - 1], me.at(z=wrap(t, d))) for d in (1, 3, 2)
    ]
    fc1_ref[...] = tn(ln_cols, fgrad)[0:36]
    vis_cols = (nn(vis0, chosen[0:640]) + nn(vis1, chosen[640:1152])).astype(BF)
    fc2_ref[...] = tn(vis_cols, spread[2:4, :, :, :, 0:1076].reshape(768, 1076))[0:36]
    vis_here = jnp.concatenate([nn(here, vis0), nn(here, vis1)], axis=1)
    for i in range(4):
        vis4[i] = vis_here[:, i * 288 : (i + 1) * 288]
        unit4[i] = unit_ref[:, i * 288 : (i + 1) * 288]
    for copy in begun:
        copy.wait_recv()
    value = lnp[t]
    for d in range(3):
        value = value + lngot[d].astype(F32)
    mean, slant = value[:, 288:289] / 1152.0, value[:, 289:290] / 1152.0
    result = vis4[t] + (value[:, 0:288] - mean - unit4[t] * slant) / dev_ref[...]
    cells = lax.broadcasted_iota(jnp.int32, (48, 729), 1)
    spot = one_hot(feature_ref[...], cells)
    fg_ref[...] = tn(result.astype(BF), spot).astype(BF)
    copies.finish()


def column_codes():
    column = np.arange(1536)
    code = np.zeros((8, 1536), np.int32)
    code[0], code[1], code[2] = column // 48, column % 48 // 12, column % 12
    return code


def row_codes():
    row = np.arange(768)
    return (row // 48 * 12 + row % 12) * 4 + row % 48 // 12


def local_codes():
    row = np.arange(48)
    return np.stack([row % 12, row // 12], axis=1).astype(np.int32)


def copy_kernel(*refs):
    count = (len(refs) - 2) // 3
    into = [
        pltpu.make_async_copy(refs[i], refs[2 * count + i], refs[-2].at[i]) for i in range(count)
    ]
    away = [
        pltpu.make_async_copy(refs[2 * count + i], refs[count + i], refs[-1].at[i])
        for i in range(count)
    ]
    for copy in into:
        copy.start()
    for first, second in zip(into, away):
        first.wait()
        second.start()
    for copy in away:
        copy.wait()


def hand_over(arrays):
    return pl.pallas_call(
        copy_kernel,
        name="hand_over",
        out_shape=tuple(jax.ShapeDtypeStruct(a.shape, a.dtype) for a in arrays),
        in_specs=[ANY] * len(arrays),
        out_specs=(ANY,) * len(arrays),
        scratch_shapes=[pltpu.VMEM(a.shape, a.dtype) for a in arrays]
        + [pltpu.SemaphoreType.DMA((len(arrays),))] * 2,
    )(*arrays)


def whole(llm_input, out_grad, llm_gain, packed, position, feature, unit_in, deviation, vis_gain,
          w_gate, w_up, w_down, w_proj, w_fc1, w_fc2):
    codes = row_codes().astype(np.int32)
    w_gate, w_up, w_fc1 = w_gate.T, w_up.T, w_fc1.T
    units = w_gate.shape[0]
    hidden = w_fc2.shape[0]
    sems = 200
    part = (3, 3)
    return pl.pallas_call(
        whole_kernel,
        name="whole",
        out_shape=(
            jax.ShapeDtypeStruct((8, 2048), BF),
            jax.ShapeDtypeStruct((36, 2048), F32),
            jax.ShapeDtypeStruct((36, hidden), F32),
            jax.ShapeDtypeStruct((36, hidden), F32),
            jax.ShapeDtypeStruct((288, 729), BF),
        ),
        in_specs=[VM] * 12 + [ANY] * 6,
        out_specs=(VM,) * 5,
        scratch_shapes=[
            pltpu.VMEM((2, 2, 8, 8192), F32),
            pltpu.VMEM((2, 4, 4, 16, 8192), BF),
            pltpu.VMEM(w_gate.shape, BF),
            pltpu.VMEM(w_up.shape, BF),
            pltpu.VMEM(w_down.shape, BF),
            pltpu.VMEM((256, units), F32),
            pltpu.VMEM((256, units), F32),
            pltpu.VMEM((256, units), F32),
            pltpu.VMEM((256, units), BF),
            pltpu.VMEM((256, units), BF),
            pltpu.VMEM((4, 4, 4, 16, 1152), BF),
            pltpu.VMEM((4, 4, 4, 16, 1152), BF),
            pltpu.VMEM(part + (4, 4, 16, 384), BF),
            pltpu.VMEM(part + (4, 16, 384), BF),
            pltpu.VMEM(part + (16, 384), BF),
            pltpu.VMEM((3, 4, 4, 16, 384), BF),
            pltpu.VMEM((3, 4, 16, 384), BF),
            pltpu.VMEM((4, 4, 16, 2048), BF),
            pltpu.VMEM((4, 4, 2, 48, 2560), BF),
            pltpu.VMEM(w_proj.shape, BF),
            pltpu.VMEM(w_fc1.shape, BF),
            pltpu.VMEM(w_fc2.shape, BF),
            pltpu.VMEM((768, 2560), BF),
            pltpu.VMEM((48, 640), BF),
            pltpu.VMEM((3, 48, 640), BF),
            pltpu.VMEM((2, 4, 4, 48, 640), BF),
            pltpu.VMEM((40, 1024), F32),
            pltpu.VMEM((40, 1024), F32),
            pltpu.VMEM((4, 48, 384), F32),
            pltpu.VMEM((4, 48, 384), BF),
            pltpu.VMEM((3, 48, 384), BF),
            pltpu.VMEM((4, 48, 288), F32),
            pltpu.VMEM((4, 48, 288), F32),
            pltpu.SemaphoreType.DMA((6,)),
            pltpu.SemaphoreType.DMA((sems,)),
            pltpu.SemaphoreType.DMA((sems,)),
        ],
        compiler_params=pltpu.CompilerParams(
            collective_id=0, has_side_effects=True, vmem_limit_bytes=63 * 1024 * 1024
        ),
    )(
        llm_input, out_grad, llm_gain.reshape(1, -1), packed, position, feature, unit_in, deviation,
        vis_gain, jnp.asarray(column_codes()),
        jnp.asarray(codes.reshape(1, -1)), jnp.asarray(local_codes()),
        w_gate, w_up, w_down, w_proj, w_fc1, w_fc2,
    )


def prepare_kernel(
    index_ref, count_ref, seq_ref, in_ref, out_ref, gain_ref, codes_ref,
    packed_ref, pos_ref, feature_ref, unit_ref, dev_ref, vgain_ref,
):
    width = (GRID + 1) // 2
    row = lax.broadcasted_iota(jnp.int32, (48, 1), 0)
    quarter = (
        jnp.where(row >= 12, 1, 0) + jnp.where(row >= 24, 1, 0) + jnp.where(row >= 36, 1, 0)
    )
    slot = row - 12 * quarter
    pool_row = jnp.zeros_like(row)
    pool_col = jnp.zeros_like(row)
    for i in range(12):
        token = index_ref[0, i]
        down = token // width
        pool_row = jnp.where(slot == i, down, pool_row)
        pool_col = jnp.where(slot == i, token - down * width, pool_col)
    low = jnp.where(quarter >= 2, 1, 0)
    grid_row = 2 * pool_row + low
    grid_col = 2 * pool_col + quarter - 2 * low
    count = count_ref[0]
    inside = (grid_row < GRID) & (grid_col < GRID) & (slot < count)
    row_cells = jnp.where(2 * pool_row + 1 < GRID, 0.5, 1.0)
    col_cells = jnp.where(2 * pool_col + 1 < GRID, 0.5, 1.0)
    weight = jnp.where(inside, row_cells * col_cells, 0.0)
    feature = jnp.where(inside, grid_row * GRID + grid_col, 0)
    feature_ref[...] = feature
    cells = lax.broadcasted_iota(jnp.int32, (48, in_ref.shape[0]), 1)
    spot = one_hot(feature, cells)
    packed_ref[:, 0:1152] = nn(spot, out_ref[...]).astype(BF)
    rows_in = nn(spot, in_ref[...])
    center = jnp.mean(rows_in, axis=1, keepdims=True)
    variance = jnp.mean((rows_in - center) * (rows_in - center), axis=1, keepdims=True)
    deviation = jnp.sqrt(variance + 1e-06)
    unit_in = (rows_in - center) / deviation
    unit_ref[...] = unit_in
    gain = gain_ref[...].reshape(1, 1152)
    vgain_ref[...] = gain
    dev_ref[...] = deviation
    packed_ref[:, 1152:2304] = (unit_in * gain).astype(BF)
    packed_ref[:, 2304:2432] = jnp.broadcast_to(weight, (48, 128)).astype(BF)
    packed_ref[:, 2432:2560] = jnp.full((48, 128), count, jnp.int32).astype(F32).astype(BF)
    tokens = lax.broadcasted_iota(jnp.int32, (768, 256), 1)
    place = jnp.where(codes_ref[:, 0:1] == tokens, seq_ref[...].astype(F32), 0.0)
    pos_ref[:, 0:1] = jnp.sum(place, axis=1, keepdims=True).astype(jnp.int32)
    pos_ref[:, 1:2] = codes_ref[:, 1:2]


def prepare(keep_index, keep_count, seq_order, vision_in, vision_out, vis_gain):
    codes = row_codes()
    codes = np.stack([codes // 4, codes], axis=1).astype(np.int32)
    scalar = pl.BlockSpec(memory_space=pltpu.SMEM)
    return pl.pallas_call(
        prepare_kernel,
        name="prepare",
        out_shape=(
            jax.ShapeDtypeStruct((48, 2560), BF),
            jax.ShapeDtypeStruct((768, 2), jnp.int32),
            jax.ShapeDtypeStruct((48, 1), jnp.int32),
            jax.ShapeDtypeStruct((48, 1152), F32),
            jax.ShapeDtypeStruct((48, 1), F32),
            jax.ShapeDtypeStruct((1, 1152), F32),
        ),
        in_specs=[scalar, scalar, VM, VM, VM, VM, VM],
        out_specs=(VM,) * 6,
        compiler_params=pltpu.CompilerParams(vmem_limit_bytes=63 * 1024 * 1024),
    )(
        keep_index, keep_count, seq_order.reshape(1, -1), vision_in, vision_out, vis_gain,
        jnp.asarray(codes),
    )


def shards(
    llm_input,
    out_grad,
    llm_gain,
    w_gate,
    w_up,
    w_down,
    keep_index,
    keep_count,
    seq_order,
    vision_in,
    vision_out,
    vis_gain,
    w_proj,
    w_fc1,
    w_fc2,
):
    packed, position, feature, unit_in, deviation, vis_gain = prepare(
        keep_index, keep_count, seq_order, vision_in, vision_out, vis_gain
    )
    results = whole(
        llm_input, out_grad, llm_gain, packed, position, feature, unit_in, deviation,
        vis_gain, w_gate, w_up, w_down, w_proj, w_fc1, w_fc2,
    )
    embed, proj_grad, fc1_grad, fc2_grad, feature_grad = hand_over(results)
    return (embed, proj_grad, fc1_grad, fc2_grad.T, feature_grad.T)


def solution(mesh):
    in_specs = (
        P("frame", None),
        P("frame", None),
        P(),
        P(None, ("frame", "tensor")),
        P(None, ("frame", "tensor")),
        P(("frame", "tensor"), None),
        P("frame", None),
        P("frame"),
        P(),
        P("frame", None),
        P("frame", None),
        P(),
        P(None, "tensor"),
        P(None, "tensor"),
        P("tensor", None),
    )
    out_specs = (
        P("frame", "tensor"),
        P("frame", "tensor"),
        P("frame", "tensor"),
        P("tensor", "frame"),
        P("frame", "tensor"),
    )
    return jax.shard_map(shards, mesh=mesh, in_specs=in_specs, out_specs=out_specs, check_vma=False)
```
